32 devices in a mesh: groups: 2 (over y), seq: 4 (over z), head: 2 (over x), dp: 2 (over core).
Axes of the slice: x: 2, y: 2, z: 4, core: 2. Of those that a mesh axis runs over, the one named last changes fastest.
Arguments:
- x_input: bfloat16 [4, 1024, 5120], P(('groups', 'dp'), 'seq', 'head'), parts along dimension 0, may hold values from -6 to 6
- bc_input: bfloat16 [4, 1024, 256], P(('groups', 'dp'), 'seq'), parts along dimension 0, may hold values from -6 to 6
- decays: float32 [4, 80, 1024], P(('groups', 'dp'), 'head', 'seq'), parts along dimension 0, may hold values from 0.5 to 1, as said below
- conv_x: float32 [4, 5120], P(None, 'head'), may hold values from -3 to 3
- conv_bc: float32 [4, 256], replicated, may hold values from -3 to 3
- skip_gain: float32 [80], P('head'), may hold values from 0.5 to 2
- grad_out: bfloat16 [4, 1024, 5120], P(('groups', 'dp'), 'seq', 'head'), parts along dimension 0, may hold values from -6 to 6
Outputs:
- y_output: bfloat16 [4, 1024, 5120], P(('groups', 'dp'), 'seq', 'head'), parts along dimension 0
- grad_x: bfloat16 [4, 1024, 5120], P(('groups', 'dp'), 'seq', 'head'), parts along dimension 0
- grad_bc: bfloat16 [4, 1024, 256], P(('groups', 'dp'), 'seq'), parts along dimension 0
- grad_conv_x: float32 [8, 5120], P('groups', 'head'), parts along dimension 0
- grad_conv_bc: float32 [8, 256], P('groups'), parts along dimension 0
- grad_skip: float32 [160], P(('groups', 'head')), parts along dimension 0
The draws below stay inside these ranges and needn't reach their ends.
There are 2 independent parts, one for each index of `groups`. The reference program is written for one: setup_inputs(seed, part) draws one part's arguments, and reference() takes and returns one part's arrays. A program takes and returns all parts, laid end to end along the dimension named above; an argument that names none is the same for every part. Nothing has to cross between parts.
Inputs may be any that keep to these rules, and one draw needn't show every extreme that they name: `decays`: every decay is strictly below 1.
All inputs are finite; a program needn't handle non-finite values.
Results may differ from the reference program's by a relative error of at most 0.009.
Values may be sent and summed in bfloat16 or wider, within the bound.
No kernel may reach another device: no remote copies, remote signals or barrier semaphores. Data moves between devices by JAX's collectives and lax.ppermute only.
A program may use at most 64 MiB of HBM per device.

```python
import math
import jax
import jax.numpy as jnp
from jax import lax

NUMBER_OF_HEADS = 80
HEAD_DIM = 64
STATE_DIM = 128
BLOCK_LEN = 256
CONV_WIDTH = 4
INNER_DIM = 5120
SEQUENCE_LENGTH = 1024
GROUP_SEQUENCES = 2


def draw_decays(key, part):
    random_subkeys = jax.random.split(key, 7)
    position = jnp.arange(SEQUENCE_LENGTH, dtype=jnp.float32)[None, None, :]
    fast_share = 0.5
    head_shape = (GROUP_SEQUENCES, NUMBER_OF_HEADS, 1)
    full_shape = (GROUP_SEQUENCES, NUMBER_OF_HEADS, SEQUENCE_LENGTH)
    is_fast = jax.random.uniform(random_subkeys[0], head_shape) < fast_share
    memory = jnp.exp(jax.random.uniform(random_subkeys[1], head_shape, minval=math.log(30.0), maxval=math.log(50.0)))
    slow_rate = jnp.exp(jax.random.uniform(random_subkeys[2], head_shape, minval=math.log(0.05), maxval=math.log(0.6))) / SEQUENCE_LENGTH
    base_rate = jnp.where(is_fast, 1.0 / memory, slow_rate)
    jitter = jnp.exp(jax.random.uniform(random_subkeys[3], full_shape, minval=-0.7, maxval=0.7))
    phase_shift = jax.random.uniform(random_subkeys[4], head_shape, minval=0.0, maxval=2.0 * math.pi)
    wave_factor = jnp.exp(0.7 * jnp.sin(2.0 * math.pi * 3.0 * position / SEQUENCE_LENGTH + phase_shift))
    every_rate = base_rate * jitter * wave_factor
    spike_position = jax.random.randint(random_subkeys[5], (GROUP_SEQUENCES, NUMBER_OF_HEADS, 2), 0, SEQUENCE_LENGTH)
    spike_flag = jnp.any(jnp.arange(SEQUENCE_LENGTH)[None, None, :, None] == spike_position[:, :, None, :], axis=-1)
    retained_values = jax.random.uniform(random_subkeys[6], full_shape, minval=0.5, maxval=0.8)
    logarithm_decay = jnp.where(spike_flag, jnp.log(retained_values), -every_rate)
    return jnp.exp(logarithm_decay).astype(jnp.float32)


def block_scale(own_key, shape, shards, least, top_value):
    gain, own = 1.0, jax.random.fold_in(own_key, 6)
    for axis_at, parts in shards:
        heights = jnp.exp(jax.random.uniform(jax.random.fold_in(own, axis_at), (parts,), jnp.float32, least / len(shards), top_value / len(shards)))
        gain = gain * jnp.repeat(heights, shape[axis_at] // parts).reshape([-1 if axis == axis_at else 1 for axis in range(len(shape))])
    return gain


def normal_values(key, shape, width, most, cuts=(), held_as=jnp.bfloat16):
    level = block_scale(key, shape, cuts, -0.22, 0.18) if cuts else 1.0
    array = jax.random.normal(key, shape, jnp.float32) * width * level
    return jnp.minimum(jnp.maximum(array, -most), most).astype(held_as)


def setup_inputs(seed: int = 0, part: int = 0) -> dict:
    splits = jax.random.split(jax.random.key(seed), 8)
    part_keys = jax.random.split(jax.random.fold_in(splits[7], part), 8)
    return {
        "x_input": normal_values(part_keys[0], (GROUP_SEQUENCES, SEQUENCE_LENGTH, INNER_DIM), 1.0, 6.0, ((0, 2), (1, 4), (2, 2))),
        "bc_input": normal_values(part_keys[1], (GROUP_SEQUENCES, SEQUENCE_LENGTH, 2 * STATE_DIM), 1.0, 6.0, ((0, 2), (1, 4))),
        "decays": draw_decays(jax.random.fold_in(jax.random.fold_in(splits[7], part), 71), part),
        "conv_x": normal_values(splits[3], (CONV_WIDTH, INNER_DIM), CONV_WIDTH ** -0.5, 3.0, ((1, 2),), jnp.float32),
        "conv_bc": normal_values(splits[4], (CONV_WIDTH, 2 * STATE_DIM), CONV_WIDTH ** -0.5, 3.0, (), jnp.float32),
        "skip_gain": jnp.clip(jnp.exp(math.log(2.0) - 1.3862944 * jax.random.uniform(splits[5], (NUMBER_OF_HEADS,), jnp.float32) ** block_scale(splits[5], (NUMBER_OF_HEADS,), ((0, 2),), -0.2, 0.2)), 0.5, 2.0),
        "grad_out": normal_values(part_keys[6], (GROUP_SEQUENCES, SEQUENCE_LENGTH, INNER_DIM), 1.0, 6.0, ((0, 2), (1, 4), (2, 2))),
    }


highest = lax.Precision.HIGHEST

def silu_grad(pre):
    sigma = jax.nn.sigmoid(pre)
    return sigma * (1.0 + pre * (1.0 - sigma))

def conv_forward(padded, weight, length):
    total = jnp.zeros((length, weight.shape[1]), jnp.float32)
    for shift in range(weight.shape[0]):
        total = total + weight[shift][None, :] * padded[shift:shift + length].astype(jnp.float32)
    return total

def conv_backward(pregrad, weight):
    taps = weight.shape[0]
    length = pregrad.shape[0]
    padded = jnp.concatenate([pregrad, jnp.zeros((taps - 1, pregrad.shape[1]), jnp.float32)], axis=0)
    total = jnp.zeros(pregrad.shape, jnp.float32)
    for shift in range(taps):
        total = total + weight[shift][None, :] * padded[taps - 1 - shift:taps - 1 - shift + length]
    return total

def conv_weight_grad(pregrad, padded, taps):
    length = pregrad.shape[0]
    return jnp.stack([lax.optimization_barrier(jnp.sum(pregrad * padded[shift:shift + length].astype(jnp.float32), axis=0)) for shift in range(taps)])

def decay_matrix(cum_block):
    size = cum_block.shape[-1]
    rows = jnp.arange(size)
    lower = (rows[:, None] >= rows[None, :])[None]
    diff = cum_block[:, :, None] - cum_block[:, None, :]
    return jnp.where(lower, jnp.exp(jnp.where(lower, diff, 0.0)), 0.0)

def one_row(x_row, bc_row, decay_row, conv_x, conv_bc, skip_gain, grad_row):
    length = x_row.shape[0]
    scale = STATE_DIM ** (-0.5)
    taps = CONV_WIDTH
    x_pad = jnp.concatenate([jnp.zeros((taps - 1, INNER_DIM), jnp.bfloat16), x_row], axis=0)
    bc_pad = jnp.concatenate([jnp.zeros((taps - 1, 2 * STATE_DIM), jnp.bfloat16), bc_row], axis=0)
    pre_x = conv_forward(x_pad, conv_x, length)
    pre_bc = conv_forward(bc_pad, conv_bc, length)
    inner = jax.nn.silu(pre_x).astype(jnp.bfloat16)
    mapped = jax.nn.silu(pre_bc).astype(jnp.bfloat16)
    b_mat = mapped[:, :STATE_DIM]
    c_mat = mapped[:, STATE_DIM:]
    logarithm_decay = jnp.log(decay_row)
    input_gain = jnp.sqrt(-jnp.expm1(2.0 * logarithm_decay))
    inner_heads = inner.astype(jnp.float32).reshape(length, NUMBER_OF_HEADS, HEAD_DIM)
    weighted = (inner_heads * input_gain.T[:, :, None]).astype(jnp.bfloat16)
    blocks = length // BLOCK_LEN
    cum = jnp.cumsum(logarithm_decay.reshape(NUMBER_OF_HEADS, blocks, BLOCK_LEN), axis=-1).transpose(1, 0, 2)
    w_blocks = weighted.reshape(blocks, BLOCK_LEN, NUMBER_OF_HEADS, HEAD_DIM)
    b_blocks = b_mat.reshape(blocks, BLOCK_LEN, STATE_DIM)
    c_blocks = c_mat.reshape(blocks, BLOCK_LEN, STATE_DIM)
    g_blocks = grad_row.reshape(blocks, BLOCK_LEN, NUMBER_OF_HEADS, HEAD_DIM)

    def forward_step(state, item):
        cum_b, w_b, b_b, c_b = item
        sim = jnp.dot(c_b, b_b.T, preferred_element_type=jnp.float32)
        mixing = (decay_matrix(cum_b) * sim[None]).astype(jnp.bfloat16)
        intra = jnp.einsum('hij,jhp->ihp', mixing.astype(jnp.float32), w_b.astype(jnp.float32))
        inter = jnp.exp(cum_b).T[:, :, None] * jnp.einsum('in,hpn->ihp', c_b.astype(jnp.float32), state, precision=highest)
        tail = jnp.exp(cum_b[:, -1:] - cum_b)
        update = jnp.einsum('jhp,jn->hpn', w_b.astype(jnp.float32) * tail.T[:, :, None], b_b.astype(jnp.float32), precision=highest)
        return (jnp.exp(cum_b[:, -1])[:, None, None] * state + update, (intra + inter, state))
    zero_state = jnp.zeros((NUMBER_OF_HEADS, HEAD_DIM, STATE_DIM), jnp.float32)
    final_state, (mixed, prior) = lax.scan(forward_step, zero_state, (cum, w_blocks, b_blocks, c_blocks))
    skip_rep = jnp.repeat(skip_gain, HEAD_DIM)[None, :]
    y_row = (scale * mixed.reshape(length, INNER_DIM) + skip_rep * inner.astype(jnp.float32)).astype(jnp.bfloat16)

    def backward_step(grad, item):
        cum_b, w_b, b_b, c_b, g_b, prior_b = item
        sim = jnp.dot(c_b, b_b.T, preferred_element_type=jnp.float32)
        decay_b = decay_matrix(cum_b)
        mixing = (decay_b * sim[None]).astype(jnp.bfloat16)
        g_f = g_b.astype(jnp.float32)
        w_f = w_b.astype(jnp.float32)
        tail = jnp.exp(cum_b[:, -1:] - cum_b)
        d_w = scale * jnp.einsum('hij,ihp->jhp', mixing.astype(jnp.float32), g_f)
        d_w = d_w + tail.T[:, :, None] * jnp.einsum('jn,hpn->jhp', b_b.astype(jnp.float32), grad, precision=highest)
        d_mix = scale * jnp.einsum('ihp,jhp->hij', g_f, w_f)
        d_sim = lax.optimization_barrier(jnp.sum(d_mix * decay_b, axis=0))
        lead = scale * g_f * jnp.exp(cum_b).T[:, :, None]
        d_c = jnp.dot(d_sim, b_b.astype(jnp.float32), precision=highest)
        d_c = d_c + jnp.einsum('ihp,hpn->in', lead, prior_b, precision=highest)
        d_b = jnp.dot(d_sim.T, c_b.astype(jnp.float32), precision=highest)
        d_b = d_b + jnp.einsum('jhp,hpn->jn', w_f * tail.T[:, :, None], grad, precision=highest)
        new_grad = jnp.exp(cum_b[:, -1])[:, None, None] * grad + jnp.einsum('ihp,in->hpn', lead, c_b.astype(jnp.float32), precision=highest)
        return (new_grad, (d_w, d_b, d_c))
    start_grad, (d_weighted, d_bmat, d_cmat) = lax.scan(backward_step, zero_state, (cum, w_blocks, b_blocks, c_blocks, g_blocks, prior), reverse=True)
    d_weighted = d_weighted.reshape(length, NUMBER_OF_HEADS, HEAD_DIM)
    d_inner = (input_gain.T[:, :, None] * d_weighted).reshape(length, INNER_DIM) + skip_rep * grad_row.astype(jnp.float32)
    d_pre_x = d_inner * silu_grad(pre_x)
    d_mapped = jnp.concatenate([d_bmat.reshape(length, STATE_DIM), d_cmat.reshape(length, STATE_DIM)], axis=1)
    d_pre_bc = d_mapped * silu_grad(pre_bc)
    grad_x = conv_backward(d_pre_x, conv_x).astype(jnp.bfloat16)
    grad_bc = conv_backward(d_pre_bc, conv_bc).astype(jnp.bfloat16)
    taps_x = conv_weight_grad(d_pre_x, x_pad, taps)
    taps_bc = conv_weight_grad(d_pre_bc, bc_pad, taps)
    skip_term = lax.optimization_barrier(jnp.sum((grad_row.astype(jnp.float32) * inner.astype(jnp.float32)).reshape(length, NUMBER_OF_HEADS, HEAD_DIM), axis=(0, 2)))
    return (y_row, grad_x, grad_bc, taps_x, taps_bc, skip_term)

def reference(x_input, bc_input, decays, conv_x, conv_bc, skip_gain, grad_out):
    outputs = [one_row(x_input[row], bc_input[row], decays[row], conv_x, conv_bc, skip_gain, grad_out[row]) for row in range(GROUP_SEQUENCES)]
    y_output = jnp.stack([item[0] for item in outputs])
    grad_x = jnp.stack([item[1] for item in outputs])
    grad_bc = jnp.stack([item[2] for item in outputs])
    norm_tokens = float(GROUP_SEQUENCES * SEQUENCE_LENGTH) ** (-0.5)
    norm_skip = float(GROUP_SEQUENCES * SEQUENCE_LENGTH * HEAD_DIM) ** (-0.5)
    grad_conv_x = sum((item[3] for item in outputs)) * norm_tokens
    grad_conv_bc = sum((item[4] for item in outputs)) * norm_tokens
    grad_skip = sum((item[5] for item in outputs)) * norm_skip
    return (y_output, grad_x, grad_bc, grad_conv_x, grad_conv_bc, grad_skip)
```

```python
import functools

import jax
import jax.numpy as jnp
from jax import lax
from jax.experimental import pallas as pl
from jax.experimental.pallas import tpu as pltpu
from jax.sharding import PartitionSpec as P

BLOCK_LEN = 256
LANES = 128
HALO = 8
NEG = -1e30
f32 = jnp.float32
bf16 = jnp.bfloat16
HIGHEST = lax.Precision.HIGHEST
VMEM_LIMIT = 48 * 1024 * 1024


def dot(a, b, precision=None):
    return jnp.dot(a, b, preferred_element_type=f32, precision=precision)


def dot_nt(a, b):
    return lax.dot_general(a, b, (((1,), (1,)), ((), ())), preferred_element_type=f32)


def sigmoid(v):
    return 0.5 * jnp.tanh(0.5 * v) + 0.5


def conv_rows(pad_ref, taps, lanes, rows, first):
    total = None
    for k in range(len(taps)):
        term = taps[k] * pad_ref[first + k : first + k + rows, lanes]
        total = term if total is None else total + term
    return total


def tap_rows(ref, lanes, count):
    block = ref[:, lanes]
    return [block[k : k + 1] for k in range(count)]


def spread(row_a, row_b):
    half, rows = LANES // 2, row_a.shape[1]
    both = jnp.concatenate(
        [jnp.broadcast_to(row_a, (half, rows)), jnp.broadcast_to(row_b, (half, rows))], axis=0
    )
    return both.T


def column(row):
    return jnp.broadcast_to(row, (LANES, row.shape[1])).T


def running_sum(dec):
    rows = dec.shape[1]
    before = lax.broadcasted_iota(jnp.int32, (rows, rows), 0)
    after = lax.broadcasted_iota(jnp.int32, (rows, rows), 1)
    upper = (before <= after).astype(f32)
    return dot(jnp.log(dec), upper, HIGHEST)


def gain_of(dec):
    return jnp.sqrt((1.0 - dec) * (1.0 + dec))


def tail_of(cum):
    return jnp.exp(cum[:, -1:] - cum)


def mapped_of(bc_ref, bch_ref, wbc_ref, bcpad, rows):
    bcpad[0:HALO, :] = bch_ref[...].astype(f32)
    bcpad[HALO : HALO + rows, :] = bc_ref[...].astype(f32)
    taps = wbc_ref.shape[0]
    weights = [wbc_ref[k : k + 1, :] for k in range(taps)]
    return conv_rows(bcpad, weights, slice(None), rows, HALO - taps + 1)


def state_kernel(first, heads_before, head_dim, scale, *refs):
    if first:
        dec_ref, x_ref, g_ref, xh_ref, wx_ref, bc_ref, bch_ref, wbc_ref = refs[:8]
        u_ref, v_ref, tot_ref, lw_ref, lg_ref, cum_ref, map_ref = refs[8:15]
        xpad, bt, ct, gt, sl, bcpad = refs[15:]
    else:
        dec_ref, x_ref, g_ref, xh_ref, wx_ref, cum_ref, map_ref = refs[:7]
        u_ref, v_ref, tot_ref, lw_ref, lg_ref = refs[7:12]
        xpad, bt, ct, gt, sl = refs[12:]
    rows, width = x_ref.shape
    taps = wx_ref.shape[0]
    state = bt.shape[0]

    @pl.when(pl.program_id(0) == 0)
    def _():
        dec = dec_ref[...]
        if first:
            cum = running_sum(dec)
            cum_ref[...] = cum
            pre = mapped_of(bc_ref, bch_ref, wbc_ref, bcpad, rows)
            mapped_f = pre * sigmoid(pre)
            map_ref[...] = mapped_f.astype(bf16)
        else:
            cum = cum_ref[...]
            mapped_f = map_ref[...].astype(f32)
        bt[...] = mapped_f[:, :state].T.astype(bf16)
        ct[...] = mapped_f[:, state:].T.astype(bf16)
        gt[...] = gain_of(dec) * tail_of(cum)
        sl[...] = scale * jnp.exp(cum)

    xpad[0:HALO, :] = xh_ref[...].astype(f32)
    xpad[HALO : HALO + rows, :] = x_ref[...].astype(f32)
    head0 = heads_before + pl.program_id(0) * (width // head_dim)
    for q in range(width // LANES):
        lanes = slice(q * LANES, (q + 1) * LANES)
        h = head0 + 2 * q
        pre = conv_rows(xpad, tap_rows(wx_ref, lanes, taps), lanes, rows, HALO - taps + 1)
        inner = (pre * sigmoid(pre)).astype(bf16).astype(f32)
        factor = spread(gt[pl.ds(h, 1), :], gt[pl.ds(h + 1, 1), :])
        lw_ref[:, lanes] = (inner * factor).astype(bf16)
        lead = spread(sl[pl.ds(h, 1), :], sl[pl.ds(h + 1, 1), :])
        lg_ref[:, lanes] = (g_ref[:, lanes].astype(f32) * lead).astype(bf16)
        tot_ref[:, lanes] = jnp.broadcast_to(lead[rows - 1 :, :] * (1.0 / scale), (8, LANES))
    u_ref[...] = dot(bt[...], lw_ref[...])
    v_ref[...] = dot(ct[...], lg_ref[...])


def intra_kernel(first, last, heads_before, head_dim, scale, *refs):
    x_ref, g_ref, xh_ref, wx_ref, dec_ref, cum_ref, map_ref, skip_ref = refs[:8]
    refs = refs[8:]
    if not first:
        dsim_in, gs_in = refs[:2]
        refs = refs[2:]
    y0_ref, dx_ref, q_ref, ls_ref, dsim_ref, gs_ref = refs[:6]
    refs = refs[6:]
    if last:
        dbc_ref = refs[0]
        refs = refs[1:]
    xpad, sim, gain, tail, sl = refs
    rows, width = x_ref.shape
    taps = wx_ref.shape[0]
    state = map_ref.shape[1] // 2
    half = rows // 2
    dec = dec_ref[...]
    gain[...] = gain_of(dec)
    tail[...] = tail_of(cum_ref[...])
    sl[...] = scale * jnp.exp(cum_ref[...])
    xpad[0:HALO, :] = xh_ref[...].astype(f32)
    xpad[HALO : HALO + rows, :] = x_ref[...].astype(f32)
    sim[...] = dot_nt(map_ref[:, state:], map_ref[:, :state])
    if first:
        dsim_ref[...] = jnp.zeros(dsim_ref.shape, f32)
        gs_ref[...] = jnp.zeros(gs_ref.shape, f32)
    else:
        dsim_ref[...] = dsim_in[...]
        gs_ref[...] = gs_in[...]
    lane = lax.broadcasted_iota(jnp.int32, (1, LANES), 1)
    low = lane < head_dim
    r_i = lax.broadcasted_iota(jnp.int32, (half, half), 0)
    c_i = lax.broadcasted_iota(jnp.int32, (half, half), 1)
    lower = r_i >= c_i

    def pair(q, carry):
        lanes = pl.ds(pl.multiple_of(q * LANES, LANES), LANES)
        h = heads_before + 2 * q
        pre = conv_rows(xpad, tap_rows(wx_ref, lanes, taps), lanes, rows, HALO - taps + 1)
        sg = sigmoid(pre)
        inner = (pre * sg).astype(bf16).astype(f32)
        sgrad = sg * (1.0 + pre * (1.0 - sg))
        gn = spread(gain[pl.ds(h, 1), :], gain[pl.ds(h + 1, 1), :])
        tl = spread(tail[pl.ds(h, 1), :], tail[pl.ds(h + 1, 1), :])
        ls = spread(sl[pl.ds(h, 1), :], sl[pl.ds(h + 1, 1), :])
        w = (inner * gn).astype(bf16)
        g = g_ref[:, lanes]
        gf = g.astype(f32)
        g_t = gf.T.astype(bf16)
        y = None
        dw_t = []
        for a in range(2):
            row = cum_ref[pl.ds(h + a, 1), :]
            col = column(row)
            keep = low if a == 0 else jnp.logical_not(low)
            d00 = jnp.exp(jnp.where(lower, col[:half] - row[:, :half], NEG))
            d10 = jnp.exp(col[half:] - row[:, :half])
            d11 = jnp.exp(jnp.where(lower, col[half:] - row[:, half:], NEG))
            m00 = (d00 * sim[0:half, 0:half]).astype(bf16)
            m10 = (d10 * sim[half:rows, 0:half]).astype(bf16)
            m11 = (d11 * sim[half:rows, half:rows]).astype(bf16)
            w_a = jnp.where(keep, w, jnp.zeros_like(w))
            top = dot(m00, w_a[:half])
            bot = dot(jnp.concatenate([m10, m11], axis=1), w_a)
            y_a = jnp.concatenate([top, bot], axis=0)
            y = y_a if y is None else y + y_a
            g_at = g_t[a * head_dim : (a + 1) * head_dim]
            left = dot(g_at, jnp.concatenate([m00, m10], axis=0))
            right = dot(g_at[:, half:], m11)
            dw_t.append(jnp.concatenate([left, right], axis=1))
            mix_top = dot_nt(g[:half], w_a[:half])
            mix_bot = dot_nt(g[half:], w_a)
            dsim_ref[0:half, 0:half] += d00 * mix_top
            dsim_ref[half:rows, 0:half] += d10 * mix_bot[:, :half]
            dsim_ref[half:rows, half:rows] += d11 * mix_bot[:, half:]
        dw = scale * jnp.concatenate(dw_t, axis=0).T
        skip = jnp.where(low, skip_ref[h], skip_ref[h + 1])
        y0_ref[:, lanes] = scale * y + skip * inner
        dx_ref[:, lanes] = (gn * dw + skip * gf) * sgrad
        q_ref[:, lanes] = (gn * tl * sgrad).astype(bf16)
        ls_ref[:, lanes] = ls.astype(bf16)
        gi = jnp.sum(gf * inner, axis=0, keepdims=True)
        sum_a = jnp.sum(jnp.where(low, gi, 0.0), axis=1, keepdims=True)
        sum_b = jnp.sum(jnp.where(low, 0.0, gi), axis=1, keepdims=True)
        gs_ref[...] += jnp.where(lane == h, sum_a, 0.0) + jnp.where(lane == h + 1, sum_b, 0.0)
        return carry

    lax.fori_loop(0, width // LANES, pair, 0)
    if last:
        ds = scale * dsim_ref[...]
        high = ds.astype(bf16)
        rest = (ds - high.astype(f32)).astype(bf16)
        ds_t = ds.T
        high_t = ds_t.astype(bf16)
        rest_t = (ds_t - high_t.astype(f32)).astype(bf16)
        b, c = map_ref[:, :state], map_ref[:, state:]
        dbc_ref[:, :state] = dot(high_t, c) + dot(rest_t, c)
        dbc_ref[:, state:] = dot(high, b) + dot(rest, b)


def pick(place, parts, wanted):
    total = jnp.zeros(parts[0].shape, bf16)
    for hop, ref in enumerate(parts):
        total = jnp.where(place == wanted(hop), ref[...], total)
    return total


def edge_kernel(count, hops, *refs):
    place_ref, dx_ref, q_ref, map_ref = refs[:4]
    parts, out_ref = refs[4 : 4 + hops], refs[4 + hops]
    state = map_ref.shape[1] // 2
    if hops:
        grad = pick(place_ref[0], parts, lambda hop: count - 2 - hop)
        extra = dot(map_ref[:, :state], grad)
        out_ref[...] = (dx_ref[...] + q_ref[...].astype(f32) * extra).astype(bf16)
    else:
        out_ref[...] = dx_ref[...].astype(bf16)


def finish_kernel(count, chunk, chunks, *refs):
    last = chunk == chunks - 1
    hops = count - 1
    place_ref, y0_ref, dx_ref, q_ref, ls_ref, x_ref, wx_ref = refs[:7]
    lw_ref, lg_ref, map_ref, edge_ref, dbc_in = refs[7:12]
    refs = refs[12:]
    parts, refs = refs[:hops], refs[hops:]
    if chunk:
        refs = refs[2:]
    if last:
        bc_ref, bch_ref, wbc_ref, gs_ref = refs[:4]
        before, refs = refs[4 : 4 + chunks - 1], refs[4 + chunks - 1 :]
        y_ref, gx_ref, sums_ref, head_ref, own_ref, dpad, dbc_ref, taps_ref, bcpad = refs
    else:
        y_ref, gx_ref, taps_ref, dbc_ref, dpad = refs
    rows, width = x_ref.shape
    taps = wx_ref.shape[0]
    state = map_ref.shape[1] // 2
    step = pl.program_id(0)

    @pl.when(step == 0)
    def _():
        dbc_ref[...] = dbc_in[...]

    place = place_ref[0]
    enter = pick(place, parts, lambda hop: hop + 1)
    grad = pick(place, parts, lambda hop: count - 2 - hop)
    b, c = map_ref[:, :state], map_ref[:, state:]
    y_ref[...] = (y0_ref[...] + ls_ref[...].astype(f32) * dot(c, enter)).astype(bf16)
    dpad[0:rows, :] = dx_ref[...] + q_ref[...].astype(f32) * dot(b, grad)
    dpad[rows : rows + HALO, :] = edge_ref[...].astype(f32)[0:HALO]
    dbc_ref[:, :state] += dot_nt(lw_ref[...], grad)
    dbc_ref[:, state:] += dot_nt(lg_ref[...], enter)
    for q in range(width // LANES):
        lanes = slice(q * LANES, (q + 1) * LANES)
        weights = tap_rows(wx_ref, lanes, taps)
        x = x_ref[:, lanes].astype(f32)
        total = None
        sums = []
        for k in range(taps):
            shifted = dpad[taps - 1 - k : taps - 1 - k + rows, lanes]
            term = weights[k] * shifted
            total = term if total is None else total + term
            sums.append(jnp.sum(shifted * x, axis=0, keepdims=True))
        gx_ref[:, lanes] = total.astype(bf16)
        sums = jnp.concatenate(sums + [jnp.zeros((8 - taps, LANES), f32)], axis=0)
        if last:
            at = pl.multiple_of(step * width + q * LANES, LANES)
            taps_ref[:, pl.ds(at, LANES)] = sums
        else:
            taps_ref[:, lanes] = sums

    if last:

        @pl.when(step == pl.num_programs(0) - 1)
        def _():
            pre = mapped_of(bc_ref, bch_ref, wbc_ref, bcpad, rows)
            sg = sigmoid(pre)
            dpre = dbc_ref[...] * (sg * (1.0 + pre * (1.0 - sg)))
            own_ref[...] = dpre
            at = 0
            for ref in before:
                sums_ref[:, at : at + ref.shape[1]] = ref[...]
                at += ref.shape[1]
            sums_ref[:, at : at + taps_ref.shape[1]] = taps_ref[...]
            at += taps_ref.shape[1]
            sums = []
            for k in range(taps):
                moved = bcpad[HALO - taps + 1 + k : HALO - taps + 1 + k + rows, :]
                sums.append(jnp.sum(dpre * moved, axis=0, keepdims=True))
            sums = jnp.concatenate(sums + [jnp.zeros((8 - taps, 2 * state), f32)], axis=0)
            sums_ref[:, at : at + 2 * state] = sums
            sums_ref[:, at + 2 * state :] = gs_ref[...]
            head_ref[0:rows, :] = dpre.astype(bf16)
            head_ref[rows:, :] = jnp.concatenate([sums, jnp.zeros_like(sums)], axis=0).astype(bf16)


def merge_kernel(heads, *refs):
    sums_ref, sums_dp, own_ref = refs[:3]
    others, crosses = refs[3 : 2 + heads], refs[2 + heads : 1 + 2 * heads]
    sums_out, full_ref, send_ref = refs[1 + 2 * heads :]
    rows, bc = own_ref.shape
    inner = sums_ref.shape[1] - bc - LANES
    full = own_ref[...]
    total = sums_ref[...] + sums_dp[...]
    taps_bc = total[:, inner : inner + bc]
    for ref in others:
        block = ref[...].astype(f32)
        full = full + block[:rows]
        taps_bc = taps_bc + block[rows : rows + 8]
    for ref in crosses:
        taps_bc = taps_bc + ref[...]
    full_ref[...] = full
    sums_out[:, 0:inner] = total[:, :inner]
    sums_out[:, inner : inner + bc] = taps_bc
    sums_out[:, inner + bc :] = total[:, inner + bc :]
    send_ref[0:8, :] = sums_out[...].astype(bf16)
    send_ref[8:16, :] = jnp.zeros((8, send_ref.shape[1]), bf16)
    send_ref[8:16, inner : inner + bc] = full[0:8].astype(bf16)


def last_kernel(count, norm_tokens, norm_skip, *refs):
    place_ref, sums_ref, full_ref, wbc_ref = refs[:4]
    parts = refs[4 : 3 + count]
    gbc_ref, tx_ref, tbc_ref, skip_ref, dpad = refs[3 + count :]
    taps, bc = wbc_ref.shape
    rows = full_ref.shape[0]
    inner = sums_ref.shape[1] - bc - LANES
    total = sums_ref[...]
    edge = jnp.zeros((8, bc), f32)
    for hop, ref in enumerate(parts):
        block = ref[...].astype(f32)
        total = total + block[0:8]
        if hop == count - 2:
            edge = jnp.where(place_ref[0] < count - 1, block[8:16, inner : inner + bc], 0.0)
    tx_ref[...] = total[0:taps, 0:inner] * norm_tokens
    tbc_ref[...] = total[0:taps, inner : inner + bc] * norm_tokens
    skip_ref[...] = total[0:1, inner + bc :] * norm_skip
    dpad[0:rows, :] = full_ref[...]
    dpad[rows : rows + 8, :] = edge
    out = None
    for k in range(taps):
        term = wbc_ref[k : k + 1, :] * dpad[taps - 1 - k : taps - 1 - k + rows, :]
        out = term if out is None else out + term
    gbc_ref[...] = out.astype(bf16)


def call(kernel, grid, ins, outs, scratch, name, flops=0, nbytes=0, kept=()):
    def spec(item):
        array, block, index = item
        if block == "smem":
            return pl.BlockSpec(memory_space=pltpu.SMEM)
        if block == "any":
            return pl.BlockSpec(memory_space=pl.ANY)
        if block is None:
            whole = array.shape
            return pl.BlockSpec(whole, lambda *_: (0,) * len(whole))
        return pl.BlockSpec(block, index)

    return pl.pallas_call(
        kernel,
        grid=grid,
        in_specs=[spec(i) for i in ins],
        out_specs=[spec(o) for o in outs],
        out_shape=[o[0] for o in outs],
        scratch_shapes=scratch,
        compiler_params=pltpu.CompilerParams(vmem_limit_bytes=VMEM_LIMIT),
        cost_estimate=pl.CostEstimate(flops=flops, bytes_accessed=nbytes, transcendentals=0),
        input_output_aliases=dict(kept),
        name=name,
    )(*[i[0] for i in ins])


def chain_routes(count, hop):
    return [(hop, hop + 1), (count - 1 - hop, count - 2 - hop)]


def local(x_input, bc_input, decays, conv_x, conv_bc, skip_gain, grad_out):
    x, bc, dec, g = x_input[0], bc_input[0], decays[0], grad_out[0]
    rows, inner = x.shape
    taps = conv_x.shape[0]
    heads = dec.shape[0]
    head_dim = inner // heads
    bcw = bc.shape[1]
    state = bcw // 2
    scale = state ** (-0.5)
    count = lax.axis_size("seq")
    head_count = lax.axis_size("head")
    dp_count = lax.axis_size("dp")
    assert rows == BLOCK_LEN and 2 * head_dim == LANES and count % 2 == 0 and dp_count == 2
    chunks = 2
    width = inner // chunks
    block = 640 if width % 640 == 0 else LANES
    per = width // block
    place = lax.axis_index("seq")
    place1 = place.astype(jnp.int32).reshape(1)
    chunk_heads = width // head_dim

    def shape(s, d=f32):
        return jax.ShapeDtypeStruct(s, d)

    tails = jnp.concatenate([x[rows - HALO :], bc[rows - HALO :]], axis=1)
    halo = lax.ppermute(tails, "seq", [(i, i + 1) for i in range(count - 1)])
    bc_halo = (halo, (HALO, bcw), lambda *_: (0, inner // bcw))

    states = []
    cum = mapped = None
    for c in range(chunks):
        first = c == 0

        def at(i, c=c):
            return (0, c * per + i)

        ins = [
            (dec, None, None),
            (x, (rows, block), at),
            (g, (rows, block), at),
            (halo, (HALO, block), at),
            (conv_x, (taps, block), at),
        ]
        outs = [
            (shape((state, width)), (state, block), lambda i: (0, i)),
            (shape((state, width)), (state, block), lambda i: (0, i)),
            (shape((8, width)), (8, block), lambda i: (0, i)),
            (shape((rows, width), bf16), (rows, block), lambda i: (0, i)),
            (shape((rows, width), bf16), (rows, block), lambda i: (0, i)),
        ]
        scratch = [
            pltpu.VMEM((rows + HALO, block), f32),
            pltpu.VMEM((state, rows), bf16),
            pltpu.VMEM((state, rows), bf16),
            pltpu.VMEM((heads, rows), f32),
            pltpu.VMEM((heads, rows), f32),
        ]
        if first:
            ins += [(bc, None, None), bc_halo, (conv_bc, None, None)]
            outs += [
                (shape((heads, rows)), None, None),
                (shape((rows, bcw), bf16), None, None),
            ]
            scratch += [pltpu.VMEM((rows + HALO, bcw), f32)]
        else:
            ins += [(cum, None, None), (mapped, None, None)]
        made = call(
            functools.partial(state_kernel, first, c * chunk_heads, head_dim, scale),
            (per,),
            ins,
            outs,
            scratch,
            "local_state",
        )
        if first:
            cum, mapped = made[5:]
        states.append(made[:5])

    received = [[] for _ in range(chunks)]

    def send(c, hop):
        u, v, tot = states[c][:3]
        own = jnp.where(place == hop, u, v)
        if hop:
            own = own + tot[0:1] * received[c][hop - 1].astype(f32)
        received[c].append(lax.ppermute(own.astype(bf16), "seq", chain_routes(count, hop)))

    intra = []
    dsim = gsum = None

    def inside(c):
        first, last = c == 0, c == chunks - 1

        def at(i):
            return (0, c)

        ins = [
            (x, (rows, width), at),
            (g, (rows, width), at),
            (halo, (HALO, width), at),
            (conv_x, (taps, width), at),
            (dec, None, None),
            (cum, None, None),
            (mapped, None, None),
            (skip_gain, "smem", None),
        ]
        if not first:
            ins += [(dsim, None, None), (gsum, None, None)]
        outs = [
            (shape((rows, width)), None, None),
            (shape((rows, width)), None, None),
            (shape((rows, width), bf16), None, None),
            (shape((rows, width), bf16), None, None),
            (shape((rows, rows)), None, None),
            (shape((8, LANES)), None, None),
        ]
        if last:
            outs += [(shape((rows, bcw)), None, None)]
        scratch = [
            pltpu.VMEM((rows + HALO, width), f32),
            pltpu.VMEM((rows, rows), f32),
            pltpu.VMEM((heads, rows), f32),
            pltpu.VMEM((heads, rows), f32),
            pltpu.VMEM((heads, rows), f32),
        ]
        return call(
            functools.partial(intra_kernel, first, last, c * chunk_heads, head_dim, scale),
            (1,),
            ins,
            outs,
            scratch,
            "inside_block",
        )

    edges = []

    def edge(c):
        y0, dx, q, ls = intra[c][:4]
        hops = count - 2
        made = call(
            functools.partial(edge_kernel, count, hops),
            (1,),
            [
                (place1, "smem", None),
                (dx, (16, width), lambda i: (0, 0)),
                (q, (16, width), lambda i: (0, 0)),
                (mapped, (16, bcw), lambda i: (0, 0)),
            ]
            + [(r, None, None) for r in received[c][:hops]],
            [(shape((16, width), bf16), None, None)],
            [],
            "first_rows",
        )[0]
        return lax.ppermute(made, "seq", [(i + 1, i) for i in range(count - 1)])

    for hop in range(count - 1):
        for c in range(chunks):
            send(c, hop)
    for c in range(chunks):
        made = inside(c)
        intra.append(made)
        dsim, gsum = made[4:6]
    dbc = intra[-1][6]
    for c in range(chunks):
        edges.append(edge(c))

    y = gx = None
    taps_parts = []
    for c in range(chunks):
        last = c == chunks - 1
        u, v, tot, lw, lg = states[c]
        y0, dx, q, ls = intra[c][:4]

        def mine(i):
            return (0, i)

        def at(i, c=c):
            return (0, c * per + i)

        ins = [
            (place1, "smem", None),
            (y0, (rows, block), mine),
            (dx, (rows, block), mine),
            (q, (rows, block), mine),
            (ls, (rows, block), mine),
            (x, (rows, block), at),
            (conv_x, (taps, block), at),
            (lw, (rows, block), mine),
            (lg, (rows, block), mine),
            (mapped, None, None),
            (edges[c], (16, block), mine),
            (dbc, None, None),
        ]
        ins += [(r, (state, block), mine) for r in received[c]]
        outs = [
            (shape((rows, inner), bf16), (rows, block), at),
            (shape((rows, inner), bf16), (rows, block), at),
        ]
        scratch = [pltpu.VMEM((rows + HALO, block), f32)]
        kept = ()
        if c:
            kept = ((len(ins), 0), (len(ins) + 1, 1))
            ins += [(y, "any", None), (gx, "any", None)]
        if last:
            ins += [(bc, None, None), bc_halo, (conv_bc, None, None), (gsum, None, None)]
            ins += [(t, None, None) for t in taps_parts]
            outs += [
                (shape((8, inner + bcw + LANES)), None, None),
                (shape((rows + 16, bcw), bf16), None, None),
                (shape((rows, bcw)), None, None),
            ]
            scratch += [
                pltpu.VMEM((rows, bcw), f32),
                pltpu.VMEM((8, width), f32),
                pltpu.VMEM((rows + HALO, bcw), f32),
            ]
        else:
            outs += [
                (shape((8, width)), (8, block), mine),
                (shape((rows, bcw)), None, None),
            ]
        made = call(
            functools.partial(finish_kernel, count, c, chunks),
            (per,),
            ins,
            outs,
            scratch,
            "finish",
            kept=kept,
        )
        y, gx = made[:2]
        if last:
            sums, to_heads, own = made[2:]
        else:
            taps_parts.append(made[2])
            dbc = made[3]

    cross = sums[:, inner : inner + bcw]
    swap = [(0, 1), (1, 0)]
    sums_dp = lax.ppermute(sums, "dp", swap)
    others, crosses = [], []
    for k in range(1, head_count):
        turn = [(i, (i + k) % head_count) for i in range(head_count)]
        others.append(lax.ppermute(to_heads, "head", turn))
        both = [(2 * i + j, 2 * t + 1 - j) for i, t in turn for j in range(2)]
        crosses.append(lax.ppermute(cross, ("head", "dp"), both))
    sums_all, full, to_seq = call(
        functools.partial(merge_kernel, head_count),
        (1,),
        [(a, None, None) for a in [sums, sums_dp, own] + others + crosses],
        [
            (shape(sums.shape), None, None),
            (shape((rows, bcw)), None, None),
            (shape((16, sums.shape[1]), bf16), None, None),
        ],
        [],
        "merge",
    )
    from_seq = [
        lax.ppermute(to_seq, "seq", [(i, (i + k) % count) for i in range(count)])
        for k in range(1, count)
    ]
    token_count = rows * count * dp_count
    norm_tokens = float(token_count) ** (-0.5)
    norm_skip = float(token_count * head_dim) ** (-0.5)
    gbc, tx, tbc, skip = call(
        functools.partial(last_kernel, count, norm_tokens, norm_skip),
        (1,),
        [(place1, "smem", None)] + [(a, None, None) for a in [sums_all, full, conv_bc] + from_seq],
        [
            (shape((rows, bcw), bf16), None, None),
            (shape((taps, inner)), None, None),
            (shape((taps, bcw)), None, None),
            (shape((1, LANES)), None, None),
        ],
        [pltpu.VMEM((rows + 8, bcw), f32)],
        "last",
    )
    return y[None], gx[None], gbc[None], tx, tbc, skip[0, :heads]


def solution(mesh):
    return jax.shard_map(
        local,
        mesh=mesh,
        in_specs=(
            P(("groups", "dp"), "seq", "head"),
            P(("groups", "dp"), "seq", None),
            P(("groups", "dp"), "head", "seq"),
            P(None, "head"),
            P(),
            P("head"),
            P(("groups", "dp"), "seq", "head"),
        ),
        out_specs=(
            P(("groups", "dp"), "seq", "head"),
            P(("groups", "dp"), "seq", "head"),
            P(("groups", "dp"), "seq", None),
            P("groups", "head"),
            P("groups", None),
            P(("groups", "head")),
        ),
        check_vma=False,
    )
```

```python
import functools

import jax
import jax.numpy as jnp
from jax import lax
from jax.experimental import pallas as pl
from jax.experimental.pallas import tpu as pltpu
from jax.sharding import PartitionSpec as P

BLOCK_LEN = 256
LANES = 128
HALO = 8
NEG = -1e30
f32 = jnp.float32
bf16 = jnp.bfloat16
HIGHEST = lax.Precision.HIGHEST
ROWS16 = 16
VMEM_LIMIT = 24 * 1024 * 1024


def dot(a, b, precision=None):
    return jnp.dot(a, b, preferred_element_type=f32, precision=precision)


def dot_nt(a, b):
    return lax.dot_general(a, b, (((1,), (1,)), ((), ())), preferred_element_type=f32)


def sigmoid(v):
    return 0.5 * jnp.tanh(0.5 * v) + 0.5


def conv_rows(pad_ref, taps, lanes, rows, first):
    total = None
    for k in range(len(taps)):
        term = taps[k] * pad_ref[first + k : first + k + rows, lanes]
        total = term if total is None else total + term
    return total


def tap_rows(ref, lanes, count):
    block = ref[:, lanes]
    return [block[k : k + 1] for k in range(count)]


def spread(row_a, row_b):
    half, rows = LANES // 2, row_a.shape[1]
    both = jnp.concatenate(
        [jnp.broadcast_to(row_a, (half, rows)), jnp.broadcast_to(row_b, (half, rows))], axis=0
    )
    return both.T


def column(row):
    return jnp.broadcast_to(row, (LANES, row.shape[1])).T


def running_sum(dec):
    rows = dec.shape[1]
    before = lax.broadcasted_iota(jnp.int32, (rows, rows), 0)
    after = lax.broadcasted_iota(jnp.int32, (rows, rows), 1)
    upper = (before <= after).astype(f32)
    return dot(jnp.log(dec), upper, HIGHEST)


def gain_of(dec):
    return jnp.sqrt((1.0 - dec) * (1.0 + dec))


def tail_of(cum):
    return jnp.exp(cum[:, -1:] - cum)


def mapped_of(bc_ref, bch_ref, wbc_ref, bcpad, rows):
    bcpad[0:HALO, :] = bch_ref[...].astype(f32)
    bcpad[HALO : HALO + rows, :] = bc_ref[...].astype(f32)
    taps = wbc_ref.shape[0]
    weights = [wbc_ref[k : k + 1, :] for k in range(taps)]
    return conv_rows(bcpad, weights, slice(None), rows, HALO - taps + 1)


def put_padded(pad_ref, halo, block):
    pad_ref[0:HALO, :] = halo
    pad_ref[HALO : HALO + block.shape[0], :] = block.astype(f32)


def tails_kernel(x_ref, bc_ref, out_ref):
    width = x_ref.shape[1]
    out_ref[:, :width] = x_ref[...].astype(f32)[ROWS16 - HALO :].astype(bf16)
    out_ref[:, width:] = bc_ref[...].astype(f32)[ROWS16 - HALO :].astype(bf16)


def head_rows(ref, h):
    return ref[pl.ds(h, 1), :], ref[pl.ds(h + 1, 1), :]


def first_state_kernel(head_dim, scale, *refs):
    dec_ref, x_ref, g_ref, wx_ref, bc_ref, wbc_ref, _ = refs[:7]
    u_ref, v_ref, tot_ref, gt16_ref, lg16_ref, x16_ref, cum_ref, map_ref, bc16_ref = refs[7:16]
    xpad, bt, ct, gt, sl, lw, lg, bcpad = refs[16:]
    rows, width = x_ref.shape
    taps = wx_ref.shape[0]
    state = bt.shape[0]

    @pl.when(pl.program_id(0) == 0)
    def _():
        dec = dec_ref[...]
        cum = running_sum(dec)
        cum_ref[...] = cum
        put_padded(bcpad, jnp.zeros((HALO, bcpad.shape[1]), f32), bc_ref[...])
        weights = [wbc_ref[k : k + 1, :] for k in range(taps)]
        pre = conv_rows(bcpad, weights, slice(None), rows, HALO - taps + 1)
        mapped_f = pre * sigmoid(pre)
        map_ref[...] = mapped_f.astype(bf16)
        bc16_ref[...] = bc_ref[0:ROWS16, :]
        late = lax.broadcasted_iota(jnp.int32, mapped_f.shape, 0) >= ROWS16
        mapped_f = jnp.where(late, mapped_f, 0.0)
        bt[...] = mapped_f[:, :state].T.astype(bf16)
        ct[...] = mapped_f[:, state:].T.astype(bf16)
        gt[...] = gain_of(dec) * tail_of(cum)
        sl[...] = scale * jnp.exp(cum)

    put_padded(xpad, jnp.zeros((HALO, width), f32), x_ref[...])
    x16_ref[...] = x_ref[0:ROWS16, :]
    head0 = pl.program_id(0) * (width // head_dim)
    for q in range(width // LANES):
        lanes = slice(q * LANES, (q + 1) * LANES)
        h = head0 + 2 * q
        pre = conv_rows(xpad, tap_rows(wx_ref, lanes, taps), lanes, rows, HALO - taps + 1)
        inner = (pre * sigmoid(pre)).astype(bf16).astype(f32)
        factor = spread(*head_rows(gt, h))
        gt16_ref[:, lanes] = factor[0:ROWS16]
        lw[:, lanes] = (inner * factor).astype(bf16)
        lead = spread(*head_rows(sl, h))
        lg[:, lanes] = (g_ref[:, lanes].astype(f32) * lead).astype(bf16)
        tot_ref[:, lanes] = jnp.broadcast_to(lead[rows - 1 :, :] * (1.0 / scale), (8, LANES))
    lg16_ref[...] = lg[0:ROWS16, :]
    u_ref[...] = dot(bt[...], lw[...])
    v_ref[...] = dot(ct[...], lg[...])


def fix_kernel(*refs):
    place_ref, u_ref, v_ref, gt16_ref, lg16_ref, x16_ref, wx_ref, halo_ref = refs[:8]
    map_ref, bc16_ref, wbc_ref = refs[8:11]
    pay_ref, u_out, v_out, map_out, xpad, bcpad = refs[11:]
    width = x16_ref.shape[1]
    inner_width = wx_ref.shape[1]
    taps = wx_ref.shape[0]
    state = map_ref.shape[1] // 2
    halo = halo_ref[...].astype(f32)
    put_padded(xpad, halo[:, :width], x16_ref[...])
    put_padded(bcpad, halo[:, inner_width:], bc16_ref[...])
    lanes = slice(0, width)
    pre = conv_rows(xpad, tap_rows(wx_ref, lanes, taps), lanes, ROWS16, HALO - taps + 1)
    inner = (pre * sigmoid(pre)).astype(bf16).astype(f32)
    lw = (inner * gt16_ref[...]).astype(bf16)
    weights = [wbc_ref[k : k + 1, :] for k in range(taps)]
    pre_bc = conv_rows(bcpad, weights, slice(None), ROWS16, HALO - taps + 1)
    mapped = (pre_bc * sigmoid(pre_bc)).astype(bf16)
    map_out[...] = map_ref[...]
    map_out[0:ROWS16, :] = mapped
    first = (((0,), (0,)), ((), ()))
    u = u_ref[...] + lax.dot_general(mapped[:, :state], lw, first, preferred_element_type=f32)
    v = v_ref[...] + lax.dot_general(
        mapped[:, state:], lg16_ref[...], first, preferred_element_type=f32
    )
    u_out[...] = u
    v_out[...] = v
    pay_ref[...] = jnp.where(place_ref[0] == 0, u, v).astype(bf16)


def state_kernel(start, width, head_dim, scale, *refs):
    dec_ref, x_ref, g_ref, halo_ref, wx_ref, cum_ref, map_ref, _ = refs[:8]
    u_ref, v_ref, tot_ref = refs[8:11]
    xpad, gt, sl, lw, lg = refs[11:]
    rows = x_ref.shape[0]
    taps = wx_ref.shape[0]
    state = map_ref.shape[1] // 2
    cum = cum_ref[...]
    gt[...] = gain_of(dec_ref[...]) * tail_of(cum)
    sl[...] = scale * jnp.exp(cum)
    chunk = slice(start, start + width)
    put_padded(xpad, halo_ref[:, chunk].astype(f32), x_ref[:, chunk])
    for q in range(width // LANES):
        lanes = slice(q * LANES, (q + 1) * LANES)
        full = slice(start + q * LANES, start + (q + 1) * LANES)
        h = start // head_dim + 2 * q
        pre = conv_rows(xpad, tap_rows(wx_ref, full, taps), lanes, rows, HALO - taps + 1)
        inner = (pre * sigmoid(pre)).astype(bf16).astype(f32)
        lw[:, lanes] = (inner * spread(*head_rows(gt, h))).astype(bf16)
        lead = spread(*head_rows(sl, h))
        lg[:, lanes] = (g_ref[:, full].astype(f32) * lead).astype(bf16)
        tot_ref[:, lanes] = jnp.broadcast_to(lead[rows - 1 :, :] * (1.0 / scale), (8, LANES))
    first = (((0,), (0,)), ((), ()))
    mapped = map_ref[...]
    u_ref[...] = lax.dot_general(mapped[:, :state], lw[...], first, preferred_element_type=f32)
    v_ref[...] = lax.dot_general(mapped[:, state:], lg[...], first, preferred_element_type=f32)


def message_kernel(hop, *refs):
    if hop:
        place_ref, u_ref, v_ref, tot_ref, came_ref, _, out_ref = refs
    else:
        place_ref, u_ref, v_ref, _, out_ref = refs
    own = jnp.where(place_ref[0] == hop, u_ref[...], v_ref[...])
    if hop:
        own = own + tot_ref[0:1, :] * came_ref[...].astype(f32)
    out_ref[...] = own.astype(bf16)


def intra_kernel(first, last, start, pairs, head_dim, scale, *refs):
    x_ref, g_ref, halo_ref, wx_ref, dec_ref, cum_ref, map_ref, skip_ref, _ = refs[:9]
    refs = refs[9:]
    if not first:
        dsim_in, gs_in = refs[:2]
        refs = refs[2:]
    y0_ref, dx_ref, q_ref, ls_ref, lw_ref, lg_ref, dsim_ref, gs_ref = refs[:8]
    refs = refs[8:]
    if last:
        dbc_ref = refs[0]
        refs = refs[1:]
    xpad, sim, gain, tail, sl = refs
    rows = x_ref.shape[0]
    width = pairs * LANES
    taps = wx_ref.shape[0]
    state = map_ref.shape[1] // 2
    half = rows // 2
    dec = dec_ref[...]
    gain[...] = gain_of(dec)
    tail[...] = tail_of(cum_ref[...])
    sl[...] = scale * jnp.exp(cum_ref[...])
    chunk = slice(start, start + width)
    put_padded(xpad, halo_ref[:, chunk].astype(f32), x_ref[:, chunk])
    sim[...] = dot_nt(map_ref[:, state:], map_ref[:, :state])
    if first:
        dsim_ref[...] = jnp.zeros(dsim_ref.shape, f32)
        gs_ref[...] = jnp.zeros(gs_ref.shape, f32)
    else:
        dsim_ref[...] = dsim_in[...]
        gs_ref[...] = gs_in[...]
    lane = lax.broadcasted_iota(jnp.int32, (1, LANES), 1)
    low = lane < head_dim
    r_i = lax.broadcasted_iota(jnp.int32, (half, half), 0)
    c_i = lax.broadcasted_iota(jnp.int32, (half, half), 1)
    lower = r_i >= c_i

    def pair(q, carry):
        lanes = pl.ds(pl.multiple_of(q * LANES, LANES), LANES)
        full = pl.ds(pl.multiple_of(start + q * LANES, LANES), LANES)
        h = start // head_dim + 2 * q
        pre = conv_rows(xpad, tap_rows(wx_ref, full, taps), lanes, rows, HALO - taps + 1)
        sg = sigmoid(pre)
        inner = (pre * sg).astype(bf16).astype(f32)
        sgrad = sg * (1.0 + pre * (1.0 - sg))
        gn = spread(*head_rows(gain, h))
        tl = spread(*head_rows(tail, h))
        ls = spread(*head_rows(sl, h))
        w = (inner * gn).astype(bf16)
        g = g_ref[:, full]
        gf = g.astype(f32)
        g_t = gf.T.astype(bf16)
        y = None
        dw_t = []
        for a in range(2):
            row = cum_ref[pl.ds(h + a, 1), :]
            col = column(row)
            keep = low if a == 0 else jnp.logical_not(low)
            d00 = jnp.exp(jnp.where(lower, col[:half] - row[:, :half], NEG))
            d10 = jnp.exp(col[half:] - row[:, :half])
            d11 = jnp.exp(jnp.where(lower, col[half:] - row[:, half:], NEG))
            m00 = (d00 * sim[0:half, 0:half]).astype(bf16)
            m10 = (d10 * sim[half:rows, 0:half]).astype(bf16)
            m11 = (d11 * sim[half:rows, half:rows]).astype(bf16)
            w_a = jnp.where(keep, w, jnp.zeros_like(w))
            top = dot(m00, w_a[:half])
            bot = dot(jnp.concatenate([m10, m11], axis=1), w_a)
            y_a = jnp.concatenate([top, bot], axis=0)
            y = y_a if y is None else y + y_a
            g_at = g_t[a * head_dim : (a + 1) * head_dim]
            left = dot(g_at, jnp.concatenate([m00, m10], axis=0))
            right = dot(g_at[:, half:], m11)
            dw_t.append(jnp.concatenate([left, right], axis=1))
            mix_top = dot_nt(g[:half], w_a[:half])
            mix_bot = dot_nt(g[half:], w_a)
            dsim_ref[0:half, 0:half] += d00 * mix_top
            dsim_ref[half:rows, 0:half] += d10 * mix_bot[:, :half]
            dsim_ref[half:rows, half:rows] += d11 * mix_bot[:, half:]
        dw = scale * jnp.concatenate(dw_t, axis=0).T
        skip = jnp.where(low, skip_ref[h], skip_ref[h + 1])
        y0_ref[:, lanes] = scale * y + skip * inner
        dx_ref[:, lanes] = (gn * dw + skip * gf) * sgrad
        q_ref[:, lanes] = (gn * tl * sgrad).astype(bf16)
        ls_ref[:, lanes] = ls.astype(bf16)
        lw_ref[:, lanes] = (inner * gn * tl).astype(bf16)
        lg_ref[:, lanes] = (gf * ls).astype(bf16)
        gi = jnp.sum(gf * inner, axis=0, keepdims=True)
        sum_a = jnp.sum(jnp.where(low, gi, 0.0), axis=1, keepdims=True)
        sum_b = jnp.sum(jnp.where(low, 0.0, gi), axis=1, keepdims=True)
        gs_ref[...] += jnp.where(lane == h, sum_a, 0.0) + jnp.where(lane == h + 1, sum_b, 0.0)
        return carry

    lax.fori_loop(0, pairs, pair, 0)
    if last:
        ds = scale * dsim_ref[...]
        high = ds.astype(bf16)
        rest = (ds - high.astype(f32)).astype(bf16)
        ds_t = ds.T
        high_t = ds_t.astype(bf16)
        rest_t = (ds_t - high_t.astype(f32)).astype(bf16)
        b, c = map_ref[:, :state], map_ref[:, state:]
        dbc_ref[:, :state] = dot(high_t, c) + dot(rest_t, c)
        dbc_ref[:, state:] = dot(high, b) + dot(rest, b)


def pick(place, parts, wanted):
    total = jnp.zeros(parts[0].shape, bf16)
    for hop, ref in enumerate(parts):
        total = jnp.where(place == wanted(hop), ref[...], total)
    return total


def edge_kernel(count, hops, parts, *refs):
    place_ref, map_ref = refs[:2]
    blocks, refs = refs[2 : 2 + 2 * parts], refs[2 + 2 * parts :]
    came, out_ref = refs[:hops], refs[hops]
    state = map_ref.shape[1] // 2
    grad = pick(place_ref[0], came, lambda hop: count - 2 - hop)
    extra = dot(map_ref[0:ROWS16, :state], grad)
    at = 0
    for p in range(parts):
        dx_ref, q_ref = blocks[2 * p : 2 * p + 2]
        lanes = slice(at, at + dx_ref.shape[1])
        rows = dx_ref[0:ROWS16, :] + q_ref[0:ROWS16, :].astype(f32) * extra[:, lanes]
        out_ref[:, lanes] = rows.astype(bf16)
        at += dx_ref.shape[1]


def finish_kernel(count, start, parts, last, pairs_a_step, *refs):
    hops = count - 1
    place_ref, x_ref, wx_ref, map_ref, edge_ref, dbc_in, _ = refs[:7]
    blocks, refs = refs[7 : 7 + 6 * parts], refs[7 + 6 * parts :]
    came, refs = refs[:hops], refs[hops:]
    if start:
        refs = refs[2:]
    if last:
        bc_ref, halo_ref, wbc_ref, gs_ref, before_ref = refs[:5]
        y_ref, gx_ref, own_ref, head_ref, sums_ref, sums_bc_ref = refs[5:11]
        dbc_ref, taps_ref, enter, grad, dpad, bcpad = refs[11:]
    else:
        y_ref, gx_ref, taps_ref, dbc_ref, enter, grad, dpad = refs
    rows = x_ref.shape[0]
    taps = wx_ref.shape[0]
    state = map_ref.shape[1] // 2
    step = pl.program_id(0)
    place = place_ref[0]
    b, c = map_ref[:, :state], map_ref[:, state:]

    def work(lo, part, at, out):
        y0_ref, dx_ref, q_ref, ls_ref, lw_ref, lg_ref = blocks[6 * part : 6 * part + 6]
        lanes, mine, here = (slice(v, v + LANES) for v in (lo, at, out))
        full = slice(start + lo, start + lo + LANES)
        inter = dot(c, enter[:, lanes])
        y_ref[:, here] = (y0_ref[:, mine] + ls_ref[:, mine].astype(f32) * inter).astype(bf16)
        inter = dot(b, grad[:, lanes])
        dpad[0:rows, here] = dx_ref[:, mine] + q_ref[:, mine].astype(f32) * inter
        dpad[rows : rows + HALO, here] = edge_ref[:, lanes].astype(f32)[0:HALO]
        weights = tap_rows(wx_ref, full, taps)
        x = x_ref[:, full].astype(f32)
        total = None
        sums = []
        for k in range(taps):
            shifted = dpad[taps - 1 - k : taps - 1 - k + rows, here]
            term = weights[k] * shifted
            total = term if total is None else total + term
            sums.append(jnp.sum(shifted * x, axis=0, keepdims=True))
        gx_ref[:, here] = total.astype(bf16)
        sums = jnp.concatenate(sums + [jnp.zeros((8 - taps, LANES), f32)], axis=0)
        taps_ref[:, lanes] = sums

    spans = []
    lo = 0
    for part in range(parts):
        for at in range(0, blocks[6 * part].shape[1], LANES):
            spans.append((lo, part, at))
            lo += LANES
    for number in range(len(spans) // pairs_a_step):

        @pl.when(step == number)
        def _(number=number):
            if number == 0:
                enter[...] = pick(place, came, lambda hop: hop + 1)
                grad[...] = pick(place, came, lambda hop: count - 2 - hop)
            for i in range(pairs_a_step):
                lo, part, at = spans[number * pairs_a_step + i]
                work(lo, part, at, i * LANES)

    @pl.when(step == pl.num_programs(0) - 1)
    def _():
        d_b, d_c = dbc_in[:, :state], dbc_in[:, state:]
        lo = 0
        for part in range(parts):
            lw_ref, lg_ref = blocks[6 * part + 4 : 6 * part + 6]
            lanes = slice(lo, lo + lw_ref.shape[1])
            d_b = d_b + dot_nt(lw_ref[...], grad[:, lanes])
            d_c = d_c + dot_nt(lg_ref[...], enter[:, lanes])
            lo += lw_ref.shape[1]
        dbc_ref[:, :state] = d_b
        dbc_ref[:, state:] = d_c
        if last:
            put_padded(bcpad, halo_ref[:, x_ref.shape[1] :].astype(f32), bc_ref[...])
            weights = [wbc_ref[k : k + 1, :] for k in range(taps)]
            pre = conv_rows(bcpad, weights, slice(None), rows, HALO - taps + 1)
            sg = sigmoid(pre)
            dpre = dbc_ref[...] * (sg * (1.0 + pre * (1.0 - sg)))
            own_ref[...] = dpre
            sums_ref[:, 0 : before_ref.shape[1]] = before_ref[...]
            sums_ref[:, before_ref.shape[1] :] = taps_ref[...]
            sums = []
            for k in range(taps):
                moved = bcpad[HALO - taps + 1 + k : HALO - taps + 1 + k + rows, :]
                sums.append(jnp.sum(dpre * moved, axis=0, keepdims=True))
            sums = jnp.concatenate(sums + [jnp.zeros((8 - taps, 2 * state), f32)], axis=0)
            sums_bc_ref[:, : 2 * state] = sums
            sums_bc_ref[:, 2 * state :] = gs_ref[...]
            head_ref[0:rows, :] = dpre.astype(bf16)
            head_ref[rows:, :] = jnp.concatenate([sums, jnp.zeros_like(sums)], axis=0).astype(bf16)


def merge_kernel(heads, *refs):
    sums_ref, sums_dp, small_ref, small_dp, own_ref = refs[:5]
    others, crosses = refs[5 : 4 + heads], refs[4 + heads : 3 + 2 * heads]
    full_ref, out_ref, send_ref = refs[3 + 2 * heads :]
    rows, bc = own_ref.shape
    half = sums_ref.shape[1] // 2
    full = own_ref[...]
    total = sums_ref[...] + sums_dp[...]
    small = small_ref[...] + small_dp[...]
    taps_bc = small[:, :bc]
    for ref in others:
        block = ref[...].astype(f32)
        full = full + block[:rows]
        taps_bc = taps_bc + block[rows : rows + 8]
    for ref in crosses:
        taps_bc = taps_bc + ref[:, :bc]
    full_ref[...] = full
    send_ref[0:4, 0:half] = total[0:4, :half]
    send_ref[4:8, 0:half] = total[0:4, half:]
    send_ref[0:4, half : half + bc] = taps_bc[0:4]
    send_ref[4:8, half : half + bc] = full[0:4]
    send_ref[:, half + bc :] = small[:, bc:]
    out_ref[...] = send_ref[...].astype(bf16)


def last_kernel(count, norm_tokens, norm_skip, *refs):
    place_ref, sums_ref, full_ref, wbc_ref = refs[:4]
    parts = refs[4 : 3 + count]
    gbc_ref, tx_ref, tbc_ref, skip_ref, dpad = refs[3 + count :]
    taps, bc = wbc_ref.shape
    rows = full_ref.shape[0]
    half = tx_ref.shape[1] // 2
    total = sums_ref[...].astype(f32)
    edge = jnp.zeros((4, bc), f32)
    for hop, ref in enumerate(parts):
        block = ref[...].astype(f32)
        total = total + block
        if hop == count - 2:
            edge = jnp.where(place_ref[0] < count - 1, block[4:8, half : half + bc], 0.0)
    tx_ref[:, :half] = total[0:taps, 0:half] * norm_tokens
    tx_ref[:, half:] = total[4 : 4 + taps, 0:half] * norm_tokens
    tbc_ref[...] = total[0:taps, half : half + bc] * norm_tokens
    skip_ref[...] = total[0:1, half + bc : half + bc + skip_ref.shape[1]] * norm_skip
    dpad[0:rows, :] = full_ref[...]
    dpad[rows : rows + 4, :] = edge
    out = None
    for k in range(taps):
        term = wbc_ref[k : k + 1, :] * dpad[taps - 1 - k : taps - 1 - k + rows, :]
        out = term if out is None else out + term
    gbc_ref[...] = out.astype(bf16)


def call(kernel, name, ins, outs, scratch=(), grid=(1,), kept=(), flops=0, nbytes=0):
    def spec(item):
        if not isinstance(item, tuple):
            whole = item.shape
            return pl.BlockSpec(whole, lambda *_: (0,) * len(whole))
        if item[1] == "smem":
            return pl.BlockSpec(memory_space=pltpu.SMEM)
        if item[1] == "any":
            return pl.BlockSpec(memory_space=pl.ANY)
        return pl.BlockSpec(item[1], item[2])

    def array(item):
        return item[0] if isinstance(item, tuple) else item

    return pl.pallas_call(
        kernel,
        grid=grid,
        in_specs=[spec(i) for i in ins],
        out_specs=[spec(o) for o in outs],
        out_shape=[array(o) for o in outs],
        scratch_shapes=list(scratch),
        compiler_params=pltpu.CompilerParams(vmem_limit_bytes=VMEM_LIMIT),
        cost_estimate=pl.CostEstimate(flops=flops, bytes_accessed=nbytes, transcendentals=0),
        input_output_aliases=dict(kept),
        name=name,
    )(*[array(i) for i in ins])


def chain_routes(count, hop):
    return [(hop, hop + 1), (count - 1 - hop, count - 2 - hop)]


def shape(s, d=f32):
    return jax.ShapeDtypeStruct(s, d)


def local(x_input, bc_input, decays, conv_x, conv_bc, skip_gain, grad_out):
    x, bc, dec, g = x_input[0], bc_input[0], decays[0], grad_out[0]
    rows, inner = x.shape
    taps = conv_x.shape[0]
    heads = dec.shape[0]
    head_dim = inner // heads
    bcw = bc.shape[1]
    state = bcw // 2
    scale = state ** (-0.5)
    count = lax.axis_size("seq")
    head_count = lax.axis_size("head")
    dp_count = lax.axis_size("dp")
    assert rows == BLOCK_LEN and 2 * head_dim == LANES and taps == 4
    assert count % 2 == 0 and count > 2 and dp_count == 2
    width = inner // 2
    chunks = (0, 1)
    block = 640 if width % 640 == 0 else LANES
    per = width // block
    pairs = width // LANES
    split = (pairs - pairs // 2, pairs // 2)
    place = lax.axis_index("seq").astype(jnp.int32).reshape(1)
    where_am_i = (place, "smem")

    def vmem(s, d=f32):
        return pltpu.VMEM(s, d)

    last16 = rows // ROWS16 - 1
    tails = call(
        tails_kernel,
        "tails",
        [
            (x, (ROWS16, inner), lambda i: (last16, 0)),
            (bc, (ROWS16, bcw), lambda i: (last16, 0)),
        ],
        [shape((HALO, inner + bcw), bf16)],
    )[0]
    halo = lax.ppermute(tails, "seq", [(i, i + 1) for i in range(count - 1)])

    def at(i):
        return (0, i)

    made = call(
        functools.partial(first_state_kernel, head_dim, scale),
        "first_state",
        [
            dec,
            (x, (rows, block), at),
            (g, (rows, block), at),
            (conv_x, (taps, block), at),
            bc,
            conv_bc,
            (tails, "any"),
        ],
        [
            (shape((state, width)), (state, block), at),
            (shape((state, width)), (state, block), at),
            (shape((8, width)), (8, block), at),
            (shape((ROWS16, width)), (ROWS16, block), at),
            (shape((ROWS16, width), bf16), (ROWS16, block), at),
            (shape((ROWS16, width), bf16), (ROWS16, block), at),
            shape((heads, rows)),
            shape((rows, bcw), bf16),
            shape((ROWS16, bcw), bf16),
        ],
        [
            vmem((rows + HALO, block)),
            vmem((state, rows), bf16),
            vmem((state, rows), bf16),
            vmem((heads, rows)),
            vmem((heads, rows)),
            vmem((rows, block), bf16),
            vmem((rows, block), bf16),
            vmem((rows + HALO, bcw)),
        ],
        grid=(per,),
    )
    u, v, tot, gt16, lg16, x16, cum, mapped, bc16 = made
    pay, u, v, mapped = call(
        fix_kernel,
        "fix_first_rows",
        [where_am_i, u, v, gt16, lg16, x16, conv_x, halo, mapped, bc16, conv_bc],
        [
            shape((state, width), bf16),
            shape((state, width)),
            shape((state, width)),
            shape((rows, bcw), bf16),
        ],
        [vmem((ROWS16 + HALO, width)), vmem((ROWS16 + HALO, bcw))],
    )
    states = [(u, v, tot)]
    received = [[], []]

    def hop_on(c, message):
        routes = chain_routes(count, len(received[c]))
        received[c].append(lax.ppermute(message, "seq", routes))

    def message(c, after):
        u, v, tot = states[c]
        hop = len(received[c])
        ins = [where_am_i, u, v]
        if hop:
            ins += [tot, received[c][-1]]
        return call(
            functools.partial(message_kernel, hop),
            "message",
            ins + [(after, "any")],
            [shape((state, width), bf16)],
        )[0]

    parts = [[], []]
    carried = []

    def inside(number, after):
        c, p = divmod(number, 2)
        first, last = number == 0, number == 3
        start = c * width + sum(split[:p]) * LANES
        span = split[p] * LANES
        ins = [x, g, halo, conv_x, dec, cum, mapped, (skip_gain, "smem"), (after, "any")]
        if not first:
            ins += carried
        outs = [
            shape((rows, span)),
            shape((rows, span)),
            shape((rows, span), bf16),
            shape((rows, span), bf16),
            shape((rows, span), bf16),
            shape((rows, span), bf16),
            shape((rows, rows)),
            shape((8, LANES)),
        ]
        if last:
            outs += [shape((rows, bcw))]
        made = call(
            functools.partial(intra_kernel, first, last, start, split[p], head_dim, scale),
            "inside_block",
            ins,
            outs,
            [
                vmem((rows + HALO, span)),
                vmem((rows, rows)),
                vmem((heads, rows)),
                vmem((heads, rows)),
                vmem((heads, rows)),
            ],
        )
        parts[c].append(made[:6])
        carried[:] = made[6:8]
        return made[-1]

    def edge(c):
        hops = count - 2
        ins = [where_am_i, mapped]
        for made in parts[c]:
            ins += made[1:3]
        made = call(
            functools.partial(edge_kernel, count, hops, len(parts[c])),
            "first_rows",
            ins + received[c][:hops],
            [shape((ROWS16, width), bf16)],
        )[0]
        return lax.ppermute(made, "seq", [(i + 1, i) for i in range(count - 1)])

    hop_on(0, pay)
    u, v, tot = call(
        functools.partial(state_kernel, width, width, head_dim, scale),
        "state",
        [dec, x, g, halo, conv_x, cum, mapped, (pay, "any")],
        [shape((state, width)), shape((state, width)), shape((8, width))],
        [
            vmem((rows + HALO, width)),
            vmem((heads, rows)),
            vmem((heads, rows)),
            vmem((rows, width), bf16),
            vmem((rows, width), bf16),
        ],
    )
    states.append((u, v, tot))
    done = inside(0, v)
    number = 1
    turn = 1
    sent = None
    for _ in range(2 * count - 3):
        sent = message(turn, done)
        hop_on(turn, sent)
        if number < 4:
            done = inside(number, sent)
            number += 1
        turn = 1 - turn
        if len(received[0]) == count - 1 and turn == 0:
            break
    edges = [edge(0), edge(1)]
    dbc = done

    y = gx = None
    before = None
    for c in chunks:
        last = c == 1
        a_step = 2 if pairs % 2 == 0 else 1
        steps = pairs // a_step
        step_lanes = a_step * LANES

        def out_at(i, c=c, steps=steps):
            return (0, c * steps + i)

        ins = [where_am_i, x, conv_x, mapped, edges[c], dbc, (sent, "any")]
        for made in parts[c]:
            ins += made
        ins += received[c]
        outs = [
            (shape((rows, inner), bf16), (rows, step_lanes), out_at),
            (shape((rows, inner), bf16), (rows, step_lanes), out_at),
        ]
        inner_scratch = [
            vmem((state, width), bf16),
            vmem((state, width), bf16),
            vmem((rows + HALO, step_lanes)),
        ]
        kept = ()
        if c:
            kept = ((len(ins), 0), (len(ins) + 1, 1))
            ins += [(y, "any"), (gx, "any")]
        if last:
            ins += [bc, halo, conv_bc, carried[1], before]
            outs += [
                shape((rows, bcw)),
                shape((rows + 16, bcw), bf16),
                shape((8, inner)),
                shape((8, bcw + LANES)),
            ]
            scratch = [vmem((rows, bcw)), vmem((8, width))] + inner_scratch
            scratch += [vmem((rows + HALO, bcw))]
        else:
            outs += [shape((8, width)), shape((rows, bcw))]
            scratch = inner_scratch
        made = call(
            functools.partial(finish_kernel, count, c * width, len(parts[c]), last, a_step),
            "finish",
            ins,
            outs,
            scratch,
            grid=(steps,),
            kept=kept,
        )
        y, gx = made[:2]
        if last:
            own, to_heads, sums, small = made[2:]
        else:
            before, dbc = made[2:]

    swap = [(0, 1), (1, 0)]
    sums_dp = lax.ppermute(sums, "dp", swap)
    small_dp = lax.ppermute(small, "dp", swap)
    others, crosses = [], []
    for k in range(1, head_count):
        turn = [(i, (i + k) % head_count) for i in range(head_count)]
        others.append(lax.ppermute(to_heads, "head", turn))
        both = [(2 * i + j, 2 * t + 1 - j) for i, t in turn for j in range(2)]
        crosses.append(lax.ppermute(small, ("head", "dp"), both))
    send_width = inner // 2 + bcw + LANES
    full, to_seq = call(
        functools.partial(merge_kernel, head_count),
        "merge",
        [sums, sums_dp, small, small_dp, own] + others + crosses,
        [shape((rows, bcw)), shape((8, send_width), bf16)],
        [vmem((8, send_width))],
    )
    from_seq = [
        lax.ppermute(to_seq, "seq", [(i, (i + k) % count) for i in range(count)])
        for k in range(1, count)
    ]
    token_count = rows * count * dp_count
    norm_tokens = float(token_count) ** (-0.5)
    norm_skip = float(token_count * head_dim) ** (-0.5)
    gbc, tx, tbc, skip = call(
        functools.partial(last_kernel, count, norm_tokens, norm_skip),
        "last",
        [where_am_i, to_seq, full, conv_bc] + from_seq,
        [
            shape((rows, bcw), bf16),
            shape((taps, inner)),
            shape((taps, bcw)),
            shape((1, heads)),
        ],
        [vmem((rows + 4, bcw))],
    )
    return y[None], gx[None], gbc[None], tx, tbc, skip.reshape(heads)


def solution(mesh):
    return jax.shard_map(
        local,
        mesh=mesh,
        in_specs=(
            P(("groups", "dp"), "seq", "head"),
            P(("groups", "dp"), "seq", None),
            P(("groups", "dp"), "head", "seq"),
            P(None, "head"),
            P(),
            P("head"),
            P(("groups", "dp"), "seq", "head"),
        ),
        out_specs=(
            P(("groups", "dp"), "seq", "head"),
            P(("groups", "dp"), "seq", "head"),
            P(("groups", "dp"), "seq", None),
            P("groups", "head"),
            P("groups", None),
            P(("groups", "head")),
        ),
        check_vma=False,
    )
```

```python
import functools

import jax
import jax.numpy as jnp
from jax import lax
from jax.experimental import pallas as pl
from jax.experimental.pallas import tpu as pltpu
from jax.sharding import PartitionSpec as P

BLOCK_LEN = 256
LANES = 128
HALO = 8
NEG = -1e30
f32 = jnp.float32
bf16 = jnp.bfloat16
HIGHEST = lax.Precision.HIGHEST
ROWS16 = 16
VMEM_LIMIT = 24 * 1024 * 1024


def dot(a, b, precision=None):
    return jnp.dot(a, b, preferred_element_type=f32, precision=precision)


def dot_nt(a, b):
    return lax.dot_general(a, b, (((1,), (1,)), ((), ())), preferred_element_type=f32)


def sigmoid(v):
    return 0.5 * jnp.tanh(0.5 * v) + 0.5


def conv_rows(pad_ref, weights, rows):
    first = HALO - len(weights) + 1
    total = None
    for k, weight in enumerate(weights):
        term = weight * pad_ref[first + k : first + k + rows, :]
        total = term if total is None else total + term
    return total


def tap_rows(ref, lanes):
    block = ref[:, lanes]
    return [block[k : k + 1] for k in range(block.shape[0])]


def silu_grad(pre):
    sg = sigmoid(pre)
    return sg * (1.0 + pre * (1.0 - sg))


def spread(row_a, row_b):
    half, rows = LANES // 2, row_a.shape[1]
    both = jnp.concatenate(
        [jnp.broadcast_to(row_a, (half, rows)), jnp.broadcast_to(row_b, (half, rows))], axis=0
    )
    return both.T


def column(row):
    return jnp.broadcast_to(row, (LANES, row.shape[1])).T


def running_sum(dec):
    rows = dec.shape[1]
    before = lax.broadcasted_iota(jnp.int32, (rows, rows), 0)
    after = lax.broadcasted_iota(jnp.int32, (rows, rows), 1)
    upper = (before <= after).astype(f32)
    return dot(jnp.log(dec), upper, HIGHEST)


def gain_of(dec):
    return jnp.sqrt((1.0 - dec) * (1.0 + dec))


def tail_of(cum):
    return jnp.exp(cum[:, -1:] - cum)


def put_padded(pad_ref, halo, block):
    pad_ref[0:HALO, :] = halo
    pad_ref[HALO : HALO + block.shape[0], :] = block.astype(f32)


def lane_blocks(width):
    return [slice(at, at + LANES) for at in range(0, width, LANES)]


def tails_kernel(x_hbm, bc_hbm, out_ref, x16, bc16, sems):
    rows, width = x_hbm.shape
    last = pl.ds(rows - ROWS16, ROWS16)
    run_copies(
        [
            pltpu.make_async_copy(x_hbm.at[last, :], x16, sems.at[0]),
            pltpu.make_async_copy(bc_hbm.at[last, :], bc16, sems.at[1]),
        ]
    )
    out_ref[:, :width] = x16[...].astype(f32)[ROWS16 - HALO :].astype(bf16)
    out_ref[:, width:] = bc16[...].astype(f32)[ROWS16 - HALO :].astype(bf16)


def run_copies(copies):
    for copy in copies:
        copy.start()
    for copy in copies:
        copy.wait()


def early_load_kernel(count, *refs):
    place_ref, x_hbm, g_hbm = refs[:3]
    small = (len(refs) - 7) // 2
    sources, kept, sems = refs[3 : 3 + small], refs[-1 - small : -1], refs[-1]
    xa, ga = refs[4 + small : 6 + small]
    place = place_ref[0]
    chunk = pl.ds(0, xa.shape[1])
    copies = [pltpu.make_async_copy(sources[i], kept[i], sems.at[i]) for i in range(small)]
    for copy in copies:
        copy.start()

    @pl.when(place == 0)
    def _():
        run_copies([pltpu.make_async_copy(x_hbm.at[:, chunk], xa, sems.at[small])])

    @pl.when(place == count - 1)
    def _():
        run_copies([pltpu.make_async_copy(g_hbm.at[:, chunk], ga, sems.at[small + 1])])

    for copy in copies:
        copy.wait()


def load_kernel(x_hbm, g_hbm, _, x_ref, g_ref, sems):
    run_copies(
        [
            pltpu.make_async_copy(x_hbm, x_ref, sems.at[0]),
            pltpu.make_async_copy(g_hbm, g_ref, sems.at[1]),
        ]
    )


def head_rows(ref, h):
    return ref[pl.ds(h, 1), :], ref[pl.ds(h + 1, 1), :]


def state_of(bc_rows, factors):
    over = (((0,), (0,)), ((), ()))
    return lax.dot_general(bc_rows, factors, over, preferred_element_type=f32)


def weighted_tails(start, heads_at, x_ref, wx_ref, halo, gt, pad, lw):
    rows, width = lw.shape
    for q, lanes in enumerate(lane_blocks(width)):
        full = slice(start + q * LANES, start + (q + 1) * LANES)
        one = pad.at[q]
        put_padded(one, halo(full), x_ref[:, full])
        pre = conv_rows(one, tap_rows(wx_ref, full), rows)
        inner = (pre * sigmoid(pre)).astype(bf16).astype(f32)
        factor = spread(*head_rows(gt, heads_at + 2 * q))
        lw[:, lanes] = (inner * factor).astype(bf16)


def led_gradients(start, heads_at, g_ref, sl, lg):
    for q, lanes in enumerate(lane_blocks(lg.shape[1])):
        full = slice(start + q * LANES, start + (q + 1) * LANES)
        lead = spread(*head_rows(sl, heads_at + 2 * q))
        lg[:, lanes] = (g_ref[:, full].astype(f32) * lead).astype(bf16)


def first_state_kernel(count, width, scale, *refs):
    place_ref, dec_ref, x_ref, g_ref, wx_ref, bc_ref, wbc_ref = refs[:7]
    uv_ref, lg16_ref, cum_ref, map_ref = refs[7:11]
    pad, gt, sl, lw, lg, bcpad = refs[11:]
    rows = x_ref.shape[0]
    state = map_ref.shape[1] // 2
    dec = dec_ref[...]
    cum = running_sum(dec)
    cum_ref[...] = cum
    for half in range(2):
        lanes = slice(half * state, (half + 1) * state)
        one = bcpad.at[half]
        put_padded(one, jnp.zeros((HALO, state), f32), bc_ref[:, lanes])
        pre = conv_rows(one, tap_rows(wbc_ref, lanes), rows)
        map_ref[:, lanes] = (pre * sigmoid(pre)).astype(bf16)
    place = place_ref[0]

    @pl.when(place == 0)
    def _():
        gt[...] = gain_of(dec) * tail_of(cum)
        none = jnp.zeros((HALO, LANES), f32)
        weighted_tails(0, 0, x_ref, wx_ref, lambda _: none, gt, pad, lw)
        uv_ref[...] = state_of(map_ref[:, :state], lw[...])

    @pl.when(place == count - 1)
    def _():
        sl[...] = scale * jnp.exp(cum)
        led_gradients(0, 0, g_ref, sl, lg)
        lg16_ref[...] = lg[0:ROWS16, :]
        c = map_ref[:, state:]
        late = lax.broadcasted_iota(jnp.int32, c.shape, 0) >= ROWS16
        uv_ref[...] = state_of(jnp.where(late, c, jnp.zeros_like(c)), lg[...])


def fix_kernel(count, *refs):
    place_ref, uv_ref, lg16_ref, halo_ref, map_ref, bc_ref, wbc_ref = refs[:7]
    pay_ref, map_out, bcpad = refs[7:]
    rows, bcw = map_ref.shape
    state = bcw // 2
    inner = halo_ref.shape[1] - bcw
    map_out[...] = map_ref[...]
    for half in range(2):
        lanes = slice(half * state, (half + 1) * state)
        one = bcpad.at[half]
        edge = halo_ref[:, inner + half * state : inner + (half + 1) * state].astype(f32)
        put_padded(one, edge, bc_ref[0:ROWS16, lanes])
        pre = conv_rows(one, tap_rows(wbc_ref, lanes), ROWS16)
        map_out[0:ROWS16, lanes] = (pre * sigmoid(pre)).astype(bf16)

    @pl.when(place_ref[0] == 0)
    def _():
        pay_ref[...] = uv_ref[...].astype(bf16)

    @pl.when(place_ref[0] == count - 1)
    def _():
        extra = state_of(map_out[0:ROWS16, state:], lg16_ref[...])
        pay_ref[...] = (uv_ref[...] + extra).astype(bf16)


def middle_state_kernel(count, start, heads_at, scale, *refs):
    place_ref, dec_ref, x_ref, g_ref, halo_ref, wx_ref, cum_ref, map_ref, _ = refs[:9]
    u_ref, v_ref, tot_ref = refs[9:12]
    pad, gt, sl, lw, lg = refs[12:]
    rows = x_ref.shape[0]
    state = map_ref.shape[1] // 2
    place = place_ref[0]

    @pl.when(jnp.logical_and(place > 0, place < count - 1))
    def _():
        cum = cum_ref[...]
        gt[...] = gain_of(dec_ref[...]) * tail_of(cum)
        lead = jnp.exp(cum)
        sl[...] = scale * lead

        def halo(full):
            return halo_ref[:, full].astype(f32)

        weighted_tails(start, heads_at, x_ref, wx_ref, halo, gt, pad, lw)
        led_gradients(start, heads_at, g_ref, sl, lg)
        for q, lanes in enumerate(lane_blocks(lw.shape[1])):
            low = lax.broadcasted_iota(jnp.int32, (8, LANES), 1) < LANES // 2
            a, b = (lead[heads_at + 2 * q + i :, rows - 1 :][:1] for i in range(2))
            tot_ref[:, lanes] = jnp.where(low, a, b)
        u_ref[...] = state_of(map_ref[:, :state], lw[...])
        v_ref[...] = state_of(map_ref[:, state:], lg[...])


def end_state_kernel(count, start, heads_at, scale, *refs):
    place_ref, dec_ref, x_ref, g_ref, halo_ref, wx_ref, cum_ref, map_ref, _ = refs[:9]
    pay_ref, pad, gt, sl, lw, lg = refs[9:]
    state = map_ref.shape[1] // 2
    place = place_ref[0]

    @pl.when(place == 0)
    def _():
        gt[...] = gain_of(dec_ref[...]) * tail_of(cum_ref[...])

        def halo(full):
            return halo_ref[:, full].astype(f32)

        weighted_tails(start, heads_at, x_ref, wx_ref, halo, gt, pad, lw)
        pay_ref[...] = state_of(map_ref[:, :state], lw[...]).astype(bf16)

    @pl.when(place == count - 1)
    def _():
        sl[...] = scale * jnp.exp(cum_ref[...])
        led_gradients(start, heads_at, g_ref, sl, lg)
        pay_ref[...] = state_of(map_ref[:, state:], lg[...]).astype(bf16)


def message_kernel(hop, place_ref, u_ref, v_ref, tot_ref, came_ref, _, out_ref):
    own = jnp.where(place_ref[0] == hop, u_ref[...], v_ref[...])
    out_ref[...] = (own + tot_ref[0:1, :] * came_ref[...].astype(f32)).astype(bf16)


def last_message_kernel(count, parts, *refs):
    hops = count - 2
    place_ref, u_ref, v_ref, tot_ref, map_ref = refs[:5]
    blocks, refs = refs[7 : 7 + 2 * parts], refs[7 + 2 * parts :]
    came, (out_ref, edge_ref) = refs[:hops], refs[hops:]
    state = u_ref.shape[0]
    place = place_ref[0]
    own = jnp.where(place == hops, u_ref[...], v_ref[...])
    own = own + tot_ref[0:1, :] * came[-1][...].astype(f32)
    out_ref[0:state, :] = own.astype(bf16)
    grad = pick(place, came, lambda hop: count - 2 - hop)
    extra = dot(map_ref[0:ROWS16, :state], grad)
    at = 0
    for p in range(parts):
        dx_ref, q_ref = blocks[2 * p : 2 * p + 2]
        lanes = slice(at, at + dx_ref.shape[1])
        rows = dx_ref[0:ROWS16, :] + q_ref[0:ROWS16, :].astype(f32) * extra[:, lanes]
        edge_ref[:, lanes] = rows.astype(bf16)
        at += dx_ref.shape[1]
    out_ref[state:, :] = edge_ref[...]


def intra_kernel(first, last, start, pairs, head_dim, scale, *refs):
    x_ref, g_ref, halo_ref, wx_ref, dec_ref, cum_ref, map_ref, skip_ref, _ = refs[:9]
    refs = refs[9:]
    if not first:
        dsim_in, gs_in = refs[:2]
        refs = refs[2:]
    y0_ref, dx_ref, q_ref, ls_ref, lw_ref, lg_ref, dsim_ref, gs_ref = refs[:8]
    refs = refs[8:]
    if last:
        dbc_ref = refs[0]
        refs = refs[1:]
    pad, sim, gain = refs
    rows = x_ref.shape[0]
    state = map_ref.shape[1] // 2
    half = rows // 2
    gain[...] = gain_of(dec_ref[...])
    sim[...] = dot_nt(map_ref[:, state:], map_ref[:, :state])
    if first:
        dsim_ref[...] = jnp.zeros(dsim_ref.shape, f32)
        gs_ref[...] = jnp.zeros(gs_ref.shape, f32)
    else:
        dsim_ref[...] = dsim_in[...]
        gs_ref[...] = gs_in[...]
    lane = lax.broadcasted_iota(jnp.int32, (1, LANES), 1)
    low = lane < head_dim
    r_i = lax.broadcasted_iota(jnp.int32, (half, half), 0)
    c_i = lax.broadcasted_iota(jnp.int32, (half, half), 1)
    lower = r_i >= c_i

    def pair(q):
        lanes = slice(q * LANES, (q + 1) * LANES)
        full = slice(start + q * LANES, start + (q + 1) * LANES)
        h = start // head_dim + 2 * q
        one = pad.at[q]
        put_padded(one, halo_ref[:, full].astype(f32), x_ref[:, full])
        pre = conv_rows(one, tap_rows(wx_ref, full), rows)
        sg = sigmoid(pre)
        inner = (pre * sg).astype(bf16).astype(f32)
        sgrad = sg * (1.0 + pre * (1.0 - sg))
        gn = spread(*head_rows(gain, h))
        cums = head_rows(cum_ref, h)
        cols = [column(row) for row in cums]
        both = jnp.where(low, cols[0], cols[1])
        tl = jnp.exp(both[rows - 1 :] - both)
        ls = scale * jnp.exp(both)
        w = (inner * gn).astype(bf16)
        g = g_ref[:, full]
        gf = g.astype(f32)
        g_t = gf.T.astype(bf16)
        y = None
        dw_t = []
        for a in range(2):
            row, col = cums[a], cols[a]
            keep = low if a == 0 else jnp.logical_not(low)
            d00 = jnp.exp(jnp.where(lower, col[:half] - row[:, :half], NEG))
            d10 = jnp.exp(col[half:] - row[:, :half])
            d11 = jnp.exp(jnp.where(lower, col[half:] - row[:, half:], NEG))
            m00 = (d00 * sim[0:half, 0:half]).astype(bf16)
            m10 = (d10 * sim[half:rows, 0:half]).astype(bf16)
            m11 = (d11 * sim[half:rows, half:rows]).astype(bf16)
            w_a = jnp.where(keep, w, jnp.zeros_like(w))
            top = dot(m00, w_a[:half])
            bot = dot(jnp.concatenate([m10, m11], axis=1), w_a)
            y_a = jnp.concatenate([top, bot], axis=0)
            y = y_a if y is None else y + y_a
            g_at = g_t[a * head_dim : (a + 1) * head_dim]
            left = dot(g_at, jnp.concatenate([m00, m10], axis=0))
            right = dot(g_at[:, half:], m11)
            dw_t.append(jnp.concatenate([left, right], axis=1))
            mix_top = dot_nt(g[:half], w_a[:half])
            mix_bot = dot_nt(g[half:], w_a)
            dsim_ref[0:half, 0:half] += d00 * mix_top
            dsim_ref[half:rows, 0:half] += d10 * mix_bot[:, :half]
            dsim_ref[half:rows, half:rows] += d11 * mix_bot[:, half:]
        dw = scale * jnp.concatenate(dw_t, axis=0).T
        skip = jnp.where(low, skip_ref[h], skip_ref[h + 1])
        y0_ref[:, lanes] = scale * y + skip * inner
        dx_ref[:, lanes] = (gn * dw + skip * gf) * sgrad
        q_ref[:, lanes] = (gn * tl * sgrad).astype(bf16)
        ls_ref[:, lanes] = ls.astype(bf16)
        lw_ref[:, lanes] = (inner * gn * tl).astype(bf16)
        lg_ref[:, lanes] = (gf * ls).astype(bf16)
        gi = jnp.sum(gf * inner, axis=0, keepdims=True)
        sum_a = jnp.sum(jnp.where(low, gi, 0.0), axis=1, keepdims=True)
        sum_b = jnp.sum(jnp.where(low, 0.0, gi), axis=1, keepdims=True)
        gs_ref[...] += jnp.where(lane == h, sum_a, 0.0) + jnp.where(lane == h + 1, sum_b, 0.0)

    for q in range(pairs):
        pair(q)
    if last:
        ds = scale * dsim_ref[...]
        high = ds.astype(bf16)
        rest = (ds - high.astype(f32)).astype(bf16)
        ds_t = ds.T
        high_t = ds_t.astype(bf16)
        rest_t = (ds_t - high_t.astype(f32)).astype(bf16)
        b, c = map_ref[:, :state], map_ref[:, state:]
        dbc_ref[:, :state] = dot(high_t, c) + dot(rest_t, c)
        dbc_ref[:, state:] = dot(high, b) + dot(rest, b)


def pick(place, parts, wanted, rows=None):
    total = jnp.zeros(parts[0].shape, bf16)
    for hop, ref in enumerate(parts):
        total = jnp.where(place == wanted(hop), ref[0:rows, :], total)
    return total


def finish_bc_kernel(count, last, parts, *refs):
    hops = count - 1
    place_ref, map_ref, dbc_in = refs[:3]
    blocks, refs = refs[5 : 5 + 2 * parts], refs[5 + 2 * parts :]
    came, refs = refs[:hops], refs[hops:]
    if last:
        bc_ref, halo_ref, wbc_ref, gs_ref, own_ref, small_ref, bcpad = refs
    else:
        (dbc_ref,) = refs
    rows, bcw = map_ref.shape
    state = bcw // 2
    place = place_ref[0]
    enter = pick(place, came, lambda hop: hop + 1, state)
    grad = pick(place, came, lambda hop: count - 2 - hop, state)
    d_b, d_c = dbc_in[:, :state], dbc_in[:, state:]
    lo = 0
    for part in range(parts):
        lw_ref, lg_ref = blocks[2 * part : 2 * part + 2]
        lanes = slice(lo, lo + lw_ref.shape[1])
        d_b = d_b + dot_nt(lw_ref[...], grad[:, lanes])
        d_c = d_c + dot_nt(lg_ref[...], enter[:, lanes])
        lo += lw_ref.shape[1]
    if not last:
        dbc_ref[:, :state] = d_b
        dbc_ref[:, state:] = d_c
        return
    taps = wbc_ref.shape[0]
    inner = halo_ref.shape[1] - bcw
    for half in range(2):
        lanes = slice(half * state, (half + 1) * state)
        one = bcpad.at[half]
        edge = halo_ref[:, inner + half * state : inner + (half + 1) * state].astype(f32)
        put_padded(one, edge, bc_ref[:, lanes])
        dpre = (d_b, d_c)[half] * silu_grad(conv_rows(one, tap_rows(wbc_ref, lanes), rows))
        own_ref[:, lanes] = dpre
        sums = []
        for k in range(taps):
            moved = one[HALO - taps + 1 + k : HALO - taps + 1 + k + rows, :]
            sums.append(jnp.sum(dpre * moved, axis=0, keepdims=True))
        sums = jnp.concatenate(sums + [jnp.zeros((8 - taps, state), f32)], axis=0)
        small_ref[:, lanes] = sums
    small_ref[:, bcw:] = gs_ref[...]


def finish_kernel(count, start, parts, pieces, *refs):
    hops = count - 1
    place_ref, x_ref, wx_ref, map_ref, edge_ref, _ = refs[:6]
    blocks, refs = refs[6 : 6 + 4 * parts], refs[6 + 4 * parts :]
    came, refs = refs[:hops], refs[hops:]
    if start:
        before_ref = refs[0]
        refs = refs[3:]
    y_hbm, gx_hbm, taps_ref, enter, grad, edge, pad, y_ref, gx_ref, sems = refs
    rows = x_ref.shape[0]
    taps = wx_ref.shape[0]
    state, width = enter.shape
    place = place_ref[0]
    b, c = map_ref[:, :state], map_ref[:, state:]
    enter[...] = pick(place, came, lambda hop: hop + 1, state)
    grad[...] = pick(place, came, lambda hop: count - 2 - hop, state)
    edge[...] = jnp.where(place == 0, came[-1][state:, :], edge_ref[...])
    if start:
        taps_ref[:, 0:start] = before_ref[...]
    spans = []
    for part in range(parts):
        for at in range(0, blocks[4 * part].shape[1], LANES):
            spans.append((part, slice(at, at + LANES)))
    copies = []
    first = 0
    for number, size in enumerate(pieces):
        for q in range(first, first + size):
            part, mine = spans[q]
            y0_ref, dx_ref, q_ref, ls_ref = blocks[4 * part : 4 * part + 4]
            lanes = slice(q * LANES, (q + 1) * LANES)
            full = slice(start + q * LANES, start + (q + 1) * LANES)
            inter = dot(c, enter[:, lanes])
            y_ref[:, lanes] = (y0_ref[:, mine] + ls_ref[:, mine].astype(f32) * inter).astype(bf16)
            one = pad.at[q]
            one[0:rows, :] = dx_ref[:, mine] + q_ref[:, mine].astype(f32) * dot(b, grad[:, lanes])
            one[rows : rows + HALO, :] = edge[:, lanes].astype(f32)[0:HALO]
            x = x_ref[:, full].astype(f32)
            total = None
            sums = []
            for k, weight in enumerate(tap_rows(wx_ref, full)):
                shifted = one[taps - 1 - k : taps - 1 - k + rows, :]
                term = weight * shifted
                total = term if total is None else total + term
                sums.append(jnp.sum(shifted * x, axis=0, keepdims=True))
            gx_ref[:, lanes] = total.astype(bf16)
            sums = jnp.concatenate(sums + [jnp.zeros((8 - taps, LANES), f32)], axis=0)
            taps_ref[:, full] = sums
        lanes = slice(first * LANES, (first + size) * LANES)
        full = slice(start + first * LANES, start + (first + size) * LANES)
        for i, (made, out) in enumerate(((y_ref, y_hbm), (gx_ref, gx_hbm))):
            copy = pltpu.make_async_copy(made.at[:, lanes], out.at[:, full], sems.at[number, i])
            copy.start()
            copies.append(copy)
        first += size
    for copy in copies:
        copy.wait()


def pack_kernel(own_ref, small_ref, small_dp, small_out, head_ref):
    rows, bcw = own_ref.shape
    small = small_ref[...] + small_dp[...]
    small_out[...] = small
    head_ref[0:rows, :] = own_ref[...].astype(bf16)
    sums = small[:, :bcw]
    head_ref[rows:, :] = jnp.concatenate([sums, jnp.zeros_like(sums)], axis=0).astype(bf16)


def merge_kernel(heads, *refs):
    sums_ref, sums_dp, small_ref, own_ref = refs[:4]
    others, (full_ref, out_ref, send_ref) = refs[4 : 3 + heads], refs[3 + heads :]
    rows, bc = own_ref.shape
    half = sums_ref.shape[1] // 2
    full = own_ref[...]
    total = sums_ref[...] + sums_dp[...]
    taps_bc = small_ref[:, :bc]
    for ref in others:
        block = ref[...].astype(f32)
        full = full + block[:rows]
        taps_bc = taps_bc + block[rows : rows + 8]
    full_ref[...] = full
    send_ref[0:4, 0:half] = total[0:4, :half]
    send_ref[4:8, 0:half] = total[0:4, half:]
    send_ref[0:4, half : half + bc] = taps_bc[0:4]
    send_ref[4:8, half : half + bc] = full[0:4]
    send_ref[:, half + bc :] = small_ref[:, bc:]
    out_ref[...] = send_ref[...].astype(bf16)


def conv_bc_kernel(full_ref, wbc_ref, _, out_ref, pad):
    taps = wbc_ref.shape[0]
    rows, bcw = full_ref.shape
    for half in range(2):
        lanes = slice(half * bcw // 2, (half + 1) * bcw // 2)
        one = pad.at[half]
        one[0:rows, :] = full_ref[:, lanes]
        one[rows:, :] = jnp.zeros((HALO, bcw // 2), f32)
        out = None
        for k, weight in enumerate(tap_rows(wbc_ref, lanes)):
            term = weight * one[taps - 1 - k : taps - 1 - k + rows, :]
            out = term if out is None else out + term
        out_ref[:, lanes] = out


def last_kernel(count, norm_tokens, norm_skip, *refs):
    place_ref, sums_ref, conv_ref, wbc_ref = refs[:4]
    parts = refs[4 : 3 + count]
    gbc_ref, tx_ref, tbc_ref, skip_ref = refs[3 + count :]
    taps, bc = wbc_ref.shape
    rows = conv_ref.shape[0]
    half = tx_ref.shape[1] // 2
    total = sums_ref[...].astype(f32)
    edge = jnp.zeros((4, bc), f32)
    for hop, ref in enumerate(parts):
        block = ref[...].astype(f32)
        total = total + block
        if hop == count - 2:
            edge = jnp.where(place_ref[0] < count - 1, block[4:8, half : half + bc], 0.0)
    tx_ref[:, :half] = total[0:taps, 0:half] * norm_tokens
    tx_ref[:, half:] = total[4 : 4 + taps, 0:half] * norm_tokens
    tbc_ref[...] = total[0:taps, half : half + bc] * norm_tokens
    skip_ref[...] = total[0:1, half + bc : half + bc + skip_ref.shape[1]] * norm_skip
    gbc_ref[0 : rows - ROWS16, :] = conv_ref[0 : rows - ROWS16, :].astype(bf16)
    row = lax.broadcasted_iota(jnp.int32, (ROWS16, bc), 0)
    end = conv_ref[rows - ROWS16 :, :]
    for k in range(taps - 1):
        for j in range(taps - 1 - k):
            at = ROWS16 - (taps - 1 - k) + j
            end = end + jnp.where(row == at, wbc_ref[k : k + 1, :] * edge[j : j + 1], 0.0)
    gbc_ref[rows - ROWS16 :, :] = end.astype(bf16)


COST_US = {
    "tails": 0.9,
    "early_load": 1.0,
    "load": 1.6,
    "first_state": 1.4,
    "middle_state": 1.5,
    "end_state": 1.1,
    "inside_block": 2.7,
    "finish": 2.4,
    "finish_bc": 0.6,
}
BYTES_PER_US = 3_500_000


def call(kernel, name, ins, outs, scratch=(), grid=(1,), kept=()):
    def spec(item):
        if not isinstance(item, tuple):
            whole = item.shape
            return pl.BlockSpec(whole, lambda *_: (0,) * len(whole))
        if item[1] == "smem":
            return pl.BlockSpec(memory_space=pltpu.SMEM)
        if item[1] == "any":
            return pl.BlockSpec(memory_space=pl.ANY)
        if item[1] == "hbm":
            return pl.BlockSpec(memory_space=pltpu.HBM)
        return pl.BlockSpec(item[1], item[2])

    def array(item):
        return item[0] if isinstance(item, tuple) else item

    return pl.pallas_call(
        kernel,
        grid=grid,
        in_specs=[spec(i) for i in ins],
        out_specs=[spec(o) for o in outs],
        out_shape=[array(o) for o in outs],
        scratch_shapes=list(scratch),
        compiler_params=pltpu.CompilerParams(vmem_limit_bytes=VMEM_LIMIT),
        cost_estimate=pl.CostEstimate(
            flops=0, bytes_accessed=int(COST_US.get(name, 0.1) * BYTES_PER_US), transcendentals=0
        ),
        input_output_aliases=dict(kept),
        name=name,
    )(*[array(i) for i in ins])


def chain_routes(count, hop):
    return [(hop, hop + 1), (count - 1 - hop, count - 2 - hop)]


def shape(s, d=f32):
    return jax.ShapeDtypeStruct(s, d)


def local(x_input, bc_input, decays, conv_x, conv_bc, skip_gain, grad_out):
    x, bc, dec, g = x_input[0], bc_input[0], decays[0], grad_out[0]
    rows, inner = x.shape
    taps = conv_x.shape[0]
    heads = dec.shape[0]
    head_dim = inner // heads
    bcw = bc.shape[1]
    state = bcw // 2
    scale = state ** (-0.5)
    count = lax.axis_size("seq")
    head_count = lax.axis_size("head")
    dp_count = lax.axis_size("dp")
    assert rows == BLOCK_LEN and 2 * head_dim == LANES and taps == 4
    assert count % 2 == 0 and count > 2 and dp_count == 2
    width = inner // 2
    chunks = (0, 1)
    block = 640 if width % 640 == 0 else LANES
    per = width // block
    pairs = width // LANES
    split = (pairs - pairs // 2, pairs // 2)
    place = lax.axis_index("seq").astype(jnp.int32).reshape(1)
    where_am_i = (place, "smem")

    def vmem(s, d=f32):
        return pltpu.VMEM(s, d)

    def in_hbm(a):
        return (pltpu.with_memory_space_constraint(a, pltpu.HBM), "hbm")

    tails = call(
        tails_kernel,
        "tails",
        [in_hbm(x), in_hbm(bc)],
        [shape((HALO, inner + bcw), bf16)],
        [vmem((ROWS16, inner), bf16), vmem((ROWS16, bcw), bf16), pltpu.SemaphoreType.DMA((2,))],
    )[0]
    halo = lax.ppermute(tails, "seq", [(i, i + 1) for i in range(count - 1)])
    x_in, g_in = x, g
    sources = [bc, dec, conv_x, conv_bc]
    xa, ga, bc, dec, conv_x, conv_bc = call(
        functools.partial(early_load_kernel, count),
        "early_load",
        [where_am_i, in_hbm(x), in_hbm(g)] + [in_hbm(a) for a in sources] + [(tails, "any")],
        [shape((rows, width), bf16), shape((rows, width), bf16)]
        + [shape(a.shape, a.dtype) for a in sources],
        [pltpu.SemaphoreType.DMA((len(sources) + 2,))],
    )

    def padded(blocks, length=rows):
        return vmem((blocks, length + HALO, LANES))

    state_scratch = [
        padded(pairs),
        vmem((heads, rows)),
        vmem((heads, rows)),
        vmem((rows, width), bf16),
        vmem((rows, width), bf16),
    ]
    uv, lg16, cum, mapped = call(
        functools.partial(first_state_kernel, count, width, scale),
        "first_state",
        [where_am_i, dec, xa, ga, conv_x, bc, conv_bc],
        [
            shape((state, width)),
            shape((ROWS16, width), bf16),
            shape((heads, rows)),
            shape((rows, bcw), bf16),
        ],
        state_scratch + [padded(2)],
    )
    pay, mapped = call(
        functools.partial(fix_kernel, count),
        "fix_first_rows",
        [where_am_i, uv, lg16, halo, mapped, bc, conv_bc],
        [shape((state, width), bf16), shape((rows, bcw), bf16)],
        [padded(2, ROWS16)],
    )

    def state_call(kernel, name, c, after, outs):
        start = c * width
        return call(
            functools.partial(kernel, count, start, start // head_dim, scale),
            name,
            [where_am_i, dec, x, g, halo, conv_x, cum, mapped, (after, "any")],
            outs,
            state_scratch,
        )

    def middle_state(c, after):
        outs = [shape((state, width)), shape((state, width)), shape((8, width))]
        states[c] = state_call(middle_state_kernel, "middle_state", c, after, outs)
        return states[c][0]

    def end_state(c, after):
        outs = [shape((state, width), bf16)]
        return state_call(end_state_kernel, "end_state", c, after, outs)[0]

    states = [None, None]
    received = [[], []]

    def hop_on(c, message):
        routes = chain_routes(count, len(received[c]))
        received[c].append(lax.ppermute(message, "seq", routes))

    def message(c, after):
        hop = len(received[c])
        return call(
            functools.partial(message_kernel, hop),
            "message",
            [where_am_i, *states[c], received[c][-1], (after, "any")],
            [shape((state, width), bf16)],
        )[0]

    parts = [[], []]
    carried = []
    edges = []
    inside_last = []

    def inside(number, after):
        c, p = divmod(number, 2)
        first, last = number == 0, number == 3
        start = c * width + sum(split[:p]) * LANES
        span = split[p] * LANES
        ins = [x, g, halo, conv_x, dec, cum, mapped, (skip_gain, "smem"), (after, "any")]
        if not first:
            ins += carried
        outs = [
            shape((rows, span)),
            shape((rows, span)),
            shape((rows, span), bf16),
            shape((rows, span), bf16),
            shape((rows, span), bf16),
            shape((rows, span), bf16),
            shape((rows, rows)),
            shape((8, LANES)),
        ]
        if last:
            outs += [shape((rows, bcw))]
        made = call(
            functools.partial(intra_kernel, first, last, start, split[p], head_dim, scale),
            "inside_block",
            ins,
            outs,
            [padded(split[p]), vmem((rows, rows)), vmem((heads, rows))],
        )
        parts[c].append(made[:6])
        carried[:] = made[6:8]
        if last:
            inside_last[:] = [made[8], made[7]]
        return made[0]

    def last_message(c, after):
        u, v, tot = states[c]
        seen = edges[0] if edges else after
        ins = [where_am_i, u, v, tot, mapped, (after, "any"), (seen, "any")]
        for made in parts[c]:
            ins += made[1:3]
        return call(
            functools.partial(last_message_kernel, count, len(parts[c])),
            "last_message",
            ins + received[c],
            [shape((state + ROWS16, width), bf16), shape((ROWS16, width), bf16)],
        )

    def edge_on(block):
        return lax.ppermute(block, "seq", [(i + 1, i) for i in range(1, count - 1)])

    hop_on(0, pay)
    x, g = call(
        load_kernel,
        "load",
        [in_hbm(x_in), in_hbm(g_in), (pay, "any")],
        [shape(x_in.shape, bf16), shape(g_in.shape, bf16)],
        [pltpu.SemaphoreType.DMA((2,))],
    )
    after = middle_state(0, pay)
    after = inside(0, after)
    after = end_state(1, after)
    hop_on(1, after)
    after = middle_state(1, after)
    for hop in range(1, count - 1):
        for c in chunks:
            if hop < count - 2:
                after = message(c, after)
                hop_on(c, after)
            else:
                after, block = last_message(c, after)
                hop_on(c, after)
                edges.append(edge_on(block))
            if hop == 1 and c == 0:
                after = inside(1, after)
            if hop == count - 2 and c == 0:
                after = inside(2, after)
                after = inside(3, after)
    dbc, gsum = inside_last

    def finish_bc(c, after):
        last = c == 1
        ins = [where_am_i, mapped, dbc, (after, "any"), (edges[c], "any")]
        for made in parts[c]:
            ins += made[4:6]
        ins += received[c]
        outs = [shape((rows, bcw))]
        scratch = []
        if last:
            ins += [bc, halo, conv_bc, gsum]
            outs += [shape((8, bcw + LANES))]
            scratch = [padded(2)]
        kernel = functools.partial(finish_bc_kernel, count, last, len(parts[c]))
        return call(kernel, "finish_bc", ins, outs, scratch)

    def finish(c, after, kept_y, before):
        start = c * width
        pieces = (4, 4, 2) if pairs == 10 else (pairs - 1, 1)
        ins = [where_am_i, x, conv_x, mapped, edges[c], (after, "any")]
        for made in parts[c]:
            ins += made[:4]
        ins += received[c]
        kept = ()
        if c:
            kept = ((len(ins) + 1, 0), (len(ins) + 2, 1))
            ins += [before, (kept_y[0], "hbm"), (kept_y[1], "hbm")]
        return call(
            functools.partial(finish_kernel, count, start, len(parts[c]), pieces),
            "finish",
            ins,
            [
                (shape((rows, inner), bf16), "hbm"),
                (shape((rows, inner), bf16), "hbm"),
                shape((8, start + width)),
            ],
            [
                vmem((state, width), bf16),
                vmem((state, width), bf16),
                vmem((ROWS16, width), bf16),
                padded(pairs),
                vmem((rows, width), bf16),
                vmem((rows, width), bf16),
                pltpu.SemaphoreType.DMA((len(pieces), 2)),
            ],
            kept=kept,
        )

    y, gx, before = finish(0, after, None, None)
    dbc = finish_bc(0, before)[0]
    own, small = finish_bc(1, dbc)

    swap = [(0, 1), (1, 0)]
    small, to_heads = call(
        pack_kernel,
        "pack",
        [own, small, lax.ppermute(small, "dp", swap)],
        [shape(small.shape), shape((rows + ROWS16, bcw), bf16)],
    )
    others = []
    for k in range(1, head_count):
        turn = [(i, (i + k) % head_count) for i in range(head_count)]
        others.append(lax.ppermute(to_heads, "head", turn))
    y, gx, sums = finish(1, to_heads, (y, gx), before)
    sums_dp = lax.ppermute(sums, "dp", swap)
    send_width = inner // 2 + bcw + LANES
    full, to_seq = call(
        functools.partial(merge_kernel, head_count),
        "merge",
        [sums, sums_dp, small, own] + others,
        [shape((rows, bcw)), shape((8, send_width), bf16)],
        [vmem((8, send_width))],
    )
    from_seq = [
        lax.ppermute(to_seq, "seq", [(i, (i + k) % count) for i in range(count)])
        for k in range(1, count)
    ]
    token_count = rows * count * dp_count
    norm_tokens = float(token_count) ** (-0.5)
    norm_skip = float(token_count * head_dim) ** (-0.5)
    conv = call(
        conv_bc_kernel,
        "conv_bc",
        [full, conv_bc, (to_seq, "any")],
        [shape((rows, bcw))],
        [padded(2)],
    )[0]
    gbc, tx, tbc, skip = call(
        functools.partial(last_kernel, count, norm_tokens, norm_skip),
        "last",
        [where_am_i, to_seq, conv, conv_bc] + from_seq,
        [
            shape((rows, bcw), bf16),
            shape((taps, inner)),
            shape((taps, bcw)),
            shape((1, heads)),
        ],
    )
    return y[None], gx[None], gbc[None], tx, tbc, skip.reshape(heads)


def solution(mesh):
    return jax.shard_map(
        local,
        mesh=mesh,
        in_specs=(
            P(("groups", "dp"), "seq", "head"),
            P(("groups", "dp"), "seq", None),
            P(("groups", "dp"), "head", "seq"),
            P(None, "head"),
            P(),
            P("head"),
            P(("groups", "dp"), "seq", "head"),
        ),
        out_specs=(
            P(("groups", "dp"), "seq", "head"),
            P(("groups", "dp"), "seq", "head"),
            P(("groups", "dp"), "seq", None),
            P("groups", "head"),
            P("groups", None),
            P(("groups", "head")),
        ),
        check_vma=False,
    )
```

```python
import functools

import jax
import jax.numpy as jnp
from jax import lax
from jax.experimental import pallas as pl
from jax.experimental.pallas import tpu as pltpu
from jax.sharding import PartitionSpec as P

BLOCK_LEN = 256
LANES = 128
HALO = 8
NEG = -1e30
f32 = jnp.float32
bf16 = jnp.bfloat16
HIGHEST = lax.Precision.HIGHEST
ROWS16 = 16
VMEM_LIMIT = 24 * 1024 * 1024


def dot(a, b, precision=None):
    return jnp.dot(a, b, preferred_element_type=f32, precision=precision)


def dot_nt(a, b):
    return lax.dot_general(a, b, (((1,), (1,)), ((), ())), preferred_element_type=f32)


def sigmoid(v):
    return 0.5 * jnp.tanh(0.5 * v) + 0.5


def conv_rows(pad_ref, weights, rows):
    first = HALO - len(weights) + 1
    total = None
    for k, weight in enumerate(weights):
        term = weight * pad_ref[first + k : first + k + rows, :]
        total = term if total is None else total + term
    return total


def tap_rows(ref, lanes):
    block = ref[:, lanes]
    return [block[k : k + 1] for k in range(block.shape[0])]


def silu_grad(pre):
    sg = sigmoid(pre)
    return sg * (1.0 + pre * (1.0 - sg))


def spread(row_a, row_b):
    half, rows = LANES // 2, row_a.shape[1]
    both = jnp.concatenate(
        [jnp.broadcast_to(row_a, (half, rows)), jnp.broadcast_to(row_b, (half, rows))], axis=0
    )
    return both.T


def column(row):
    return jnp.broadcast_to(row, (LANES, row.shape[1])).T


def running_sum(dec):
    rows = dec.shape[1]
    before = lax.broadcasted_iota(jnp.int32, (rows, rows), 0)
    after = lax.broadcasted_iota(jnp.int32, (rows, rows), 1)
    upper = (before <= after).astype(f32)
    return dot(jnp.log(dec), upper, HIGHEST)


def gain_of(dec):
    return jnp.sqrt((1.0 - dec) * (1.0 + dec))


def tail_of(cum):
    return jnp.exp(cum[:, -1:] - cum)


def put_padded(pad_ref, halo, block):
    pad_ref[0:HALO, :] = halo
    pad_ref[HALO : HALO + block.shape[0], :] = block.astype(f32)


def lane_blocks(width):
    return [slice(at, at + LANES) for at in range(0, width, LANES)]


def run_copies(copies):
    for copy in copies:
        copy.start()
    for copy in copies:
        copy.wait()


def early_load_kernel(count, *refs):
    place_ref, x_hbm, g_hbm = refs[:3]
    small = (len(refs) - 9) // 2
    sources, (xa, ga) = refs[3 : 3 + small], refs[3 + small : 5 + small]
    kept, (tails_ref, x16, bc16, sems) = refs[5 + small : -4], refs[-4:]
    bc_hbm = sources[2]
    rows, width = x_hbm.shape
    place = place_ref[0]
    chunk = pl.ds(0, xa.shape[1])
    last = pl.ds(rows - ROWS16, ROWS16)
    tails = [
        pltpu.make_async_copy(x_hbm.at[last, :], x16, sems.at[small + 2]),
        pltpu.make_async_copy(bc_hbm.at[last, :], bc16, sems.at[small + 3]),
    ]
    copies = [pltpu.make_async_copy(sources[i], kept[i], sems.at[i]) for i in range(small)]
    for copy in tails:
        copy.start()

    @pl.when(place == 0)
    def _():
        run_copies(copies + [pltpu.make_async_copy(x_hbm.at[:, chunk], xa, sems.at[small])])

    @pl.when(place == count - 1)
    def _():
        run_copies(copies + [pltpu.make_async_copy(g_hbm.at[:, chunk], ga, sems.at[small + 1])])

    for copy in tails:
        copy.wait()
    tails_ref[:, :width] = x16[...].astype(f32)[ROWS16 - HALO :].astype(bf16)
    tails_ref[:, width:] = bc16[...].astype(f32)[ROWS16 - HALO :].astype(bf16)


def load_kernel(*refs):
    count = (len(refs) - 2) // 2
    sources, kept, sems = refs[:count], refs[count + 1 : -1], refs[-1]
    run_copies(
        [pltpu.make_async_copy(sources[i], kept[i], sems.at[i]) for i in range(count)]
    )


def head_rows(ref, h):
    return ref[pl.ds(h, 1), :], ref[pl.ds(h + 1, 1), :]


def state_of(bc_rows, factors):
    over = (((0,), (0,)), ((), ()))
    return lax.dot_general(bc_rows, factors, over, preferred_element_type=f32)


def weighted_tails(start, heads_at, x_ref, wx_ref, halo, gt, pad, lw):
    rows, width = lw.shape
    for q, lanes in enumerate(lane_blocks(width)):
        full = slice(start + q * LANES, start + (q + 1) * LANES)
        one = pad.at[q]
        put_padded(one, halo(full), x_ref[:, full])
        pre = conv_rows(one, tap_rows(wx_ref, full), rows)
        inner = (pre * sigmoid(pre)).astype(bf16).astype(f32)
        factor = spread(*head_rows(gt, heads_at + 2 * q))
        lw[:, lanes] = (inner * factor).astype(bf16)


def led_gradients(start, heads_at, g_ref, sl, lg):
    for q, lanes in enumerate(lane_blocks(lg.shape[1])):
        full = slice(start + q * LANES, start + (q + 1) * LANES)
        lead = spread(*head_rows(sl, heads_at + 2 * q))
        lg[:, lanes] = (g_ref[:, full].astype(f32) * lead).astype(bf16)


def mapped_half(half, state, rows, bc_block, halo, wbc_ref, bcpad):
    lanes = slice(half * state, (half + 1) * state)
    put_padded(bcpad, halo, bc_block)
    pre = conv_rows(bcpad, tap_rows(wbc_ref, lanes), rows)
    return (pre * sigmoid(pre)).astype(bf16)


def put_first_rows(pay_ref, lg, bc_ref, taps):
    state = pay_ref.shape[0] - ROWS16
    width, bcw = lg.shape[1], bc_ref.shape[1]
    bc8 = bc_ref[0:ROWS16, :].astype(f32)[0:8]
    bc8 = jnp.concatenate([bc8, jnp.zeros((8, width - bcw), f32)], axis=1)
    lg8 = lg[0:ROWS16, :].astype(f32)[0:8]
    pay_ref[state:, :] = jnp.concatenate([lg8, bc8], axis=0).astype(bf16)


def first_rows_state(more, bc_ref, wbc_ref, bcpad):
    rows, bcw = bc_ref.shape
    state = bcw // 2
    taps = wbc_ref.shape[0]
    zeros = jnp.zeros((8, state), f32)
    edge = bc_ref[rows - ROWS16 :, state:].astype(f32)[ROWS16 - HALO :]
    block = jnp.concatenate([more[8:16, state:bcw], zeros], axis=0)
    c = mapped_half(1, state, ROWS16, block, edge, wbc_ref, bcpad)
    early = lax.broadcasted_iota(jnp.int32, c.shape, 0) < taps - 1
    lg = jnp.concatenate([more[0:8, :], jnp.zeros((8, more.shape[1]), f32)], axis=0)
    return state_of(jnp.where(early, c, jnp.zeros_like(c)), lg.astype(bf16))


def first_state_kernel(count, scale, *refs):
    place_ref, dec_ref, xa_ref, ga_ref, wx_ref, bc_ref, wbc_ref, tails_ref = refs[:8]
    pay_ref, pad, gt, sl, lw, lg, bcpad, tails, more = refs[8:]
    rows, width = xa_ref.shape
    taps, bcw = wbc_ref.shape
    state = bcw // 2
    place = place_ref[0]
    none = jnp.zeros((HALO, LANES), f32)

    @pl.when(place == 0)
    def _():
        dec = dec_ref[...]
        gt[...] = gain_of(dec) * tail_of(running_sum(dec))
        b = mapped_half(0, state, rows, bc_ref[:, :state], none, wbc_ref, bcpad)
        weighted_tails(0, 0, xa_ref, wx_ref, lambda _: none, gt, pad, lw)
        pay_ref[0:state, :] = state_of(b, lw[...]).astype(bf16)
        tails[...] = tails_ref[...].astype(f32)
        more[0:8, :] = tails[:, 0:width]
        more[8:16, :] = tails[:, width : 2 * width]
        more[8 : 7 + taps, 0:bcw] = tails[HALO - taps + 1 :, 2 * width :]
        pay_ref[state:, :] = more[...].astype(bf16)

    @pl.when(place == count - 1)
    def _():
        sl[...] = scale * jnp.exp(running_sum(dec_ref[...]))
        c = mapped_half(1, state, rows, bc_ref[:, state:], none, wbc_ref, bcpad)
        late = lax.broadcasted_iota(jnp.int32, c.shape, 0) >= taps - 1
        led_gradients(0, 0, ga_ref, sl, lg)
        pay_ref[0:state, :] = state_of(jnp.where(late, c, jnp.zeros_like(c)), lg[...]).astype(bf16)
        put_first_rows(pay_ref, lg, bc_ref, taps)


def middle_first_kernel(count, scale, *refs):
    place_ref, dec_ref, x_ref, g_ref, wx_ref, bc_ref, wbc_ref, _ = refs[:8]
    cum_ref, map_ref, u_ref, v_ref, tot_ref, gt16_ref, lg16_ref = refs[8:15]
    pad, gt, sl, lw, lg, bcpad = refs[15:]
    rows, bcw = bc_ref.shape
    state = bcw // 2
    none = jnp.zeros((HALO, LANES), f32)
    dec = dec_ref[...]
    cum = running_sum(dec)
    cum_ref[...] = cum
    for half in range(2):
        lanes = slice(half * state, (half + 1) * state)
        made = mapped_half(half, state, rows, bc_ref[:, lanes], none, wbc_ref, bcpad.at[half])
        map_ref[:, lanes] = made
    place = place_ref[0]

    @pl.when(jnp.logical_and(place > 0, place < count - 1))
    def _():
        gt[...] = gain_of(dec) * tail_of(cum)
        lead = jnp.exp(cum)
        sl[...] = scale * lead
        weighted_tails(0, 0, x_ref, wx_ref, lambda _: none, gt, pad, lw)
        led_gradients(0, 0, g_ref, sl, lg)
        lane_totals(lead, 0, tot_ref)
        for q, lanes in enumerate(lane_blocks(lw.shape[1])):
            half = LANES // 2
            a, b = (row[:, 0:LANES] for row in head_rows(gt, 2 * q))
            both = [jnp.broadcast_to(row, (half, LANES)) for row in (a, b)]
            gt16_ref[:, lanes] = jnp.concatenate(both, axis=0).T[0:ROWS16]
        lg16_ref[...] = lg[0:ROWS16, :]
        late = lax.broadcasted_iota(jnp.int32, (rows, state), 0) >= ROWS16
        zero = jnp.zeros((rows, state), bf16)
        u_ref[...] = state_of(jnp.where(late, map_ref[:, :state], zero), lw[...])
        v_ref[...] = state_of(jnp.where(late, map_ref[:, state:], zero), lg[...])


def fix_kernel(count, *refs):
    place_ref, halo_in, came_ref, x_ref, wx_ref, bc_ref, wbc_ref, map_in = refs[:8]
    u_in, v_in, tot_ref, gt16_ref, lg16_ref, _ = refs[8:14]
    halo_ref, map_ref, u_ref, v_ref, came_out, pay_ref, halo, more, pad, bcpad = refs[14:]
    rows, bcw = bc_ref.shape
    state = bcw // 2
    taps = wbc_ref.shape[0]
    width = u_in.shape[1]
    place = place_ref[0]
    more[...] = came_ref[state:, :].astype(f32)
    halo[...] = halo_in[...].astype(f32)

    @pl.when(place == 1)
    def _():
        halo[:, 0:width] = more[0:8, :]
        halo[:, width : 2 * width] = more[8:16, :]
        halo[HALO - taps + 1 :, 2 * width :] = more[8 : 7 + taps, 0:bcw]

    halo_ref[...] = halo[...].astype(bf16)
    map_ref[...] = map_in[...]
    for half in range(2):
        lanes = slice(half * state, (half + 1) * state)
        edge = halo[:, 2 * width + half * state : 2 * width + (half + 1) * state]
        one = bcpad.at[half]
        made = mapped_half(half, state, ROWS16, bc_ref[0:ROWS16, lanes], edge, wbc_ref, one)
        map_ref[0:ROWS16, lanes] = made
    came_out[...] = came_ref[0:state, :]
    tot = tot_ref[0:1, :]

    @pl.when(jnp.logical_and(place > 0, place < count - 1))
    def _():
        lw16 = []
        for q, lanes in enumerate(lane_blocks(width)):
            one = pad.at[q]
            put_padded(one, halo[:, lanes], x_ref[0:ROWS16, lanes])
            pre = conv_rows(one, tap_rows(wx_ref, lanes), ROWS16)
            inner = (pre * sigmoid(pre)).astype(bf16).astype(f32)
            lw16.append((inner * gt16_ref[:, lanes]).astype(bf16))
        lw16 = jnp.concatenate(lw16, axis=1)
        u_ref[...] = u_in[...] + state_of(map_ref[0:ROWS16, :state], lw16)
        v_ref[...] = v_in[...] + state_of(map_ref[0:ROWS16, state:], lg16_ref[...])

    @pl.when(place == 1)
    def _():
        pay_ref[...] = (u_ref[...] + tot * came_ref[0:state, :].astype(f32)).astype(bf16)

    @pl.when(place == count - 2)
    def _():
        extra = first_rows_state(more, bc_ref, wbc_ref, bcpad.at[0])
        came = came_ref[0:state, :].astype(f32) + extra
        came_out[...] = came.astype(bf16)
        pay_ref[...] = (v_ref[...] + tot * came).astype(bf16)


def lane_totals(lead, heads_at, tot_ref):
    rows = lead.shape[1]
    for q, lanes in enumerate(lane_blocks(tot_ref.shape[1])):
        low = lax.broadcasted_iota(jnp.int32, (8, LANES), 1) < LANES // 2
        a, b = (lead[heads_at + 2 * q + i :, rows - 1 :][:1] for i in range(2))
        tot_ref[:, lanes] = jnp.where(low, a, b)


def middle_state_kernel(count, start, heads_at, scale, *refs):
    place_ref, dec_ref, x_ref, g_ref, halo_ref, wx_ref, cum_ref, map_ref, _ = refs[:9]
    u_ref, v_ref, tot_ref = refs[9:12]
    pad, gt, sl, lw, lg = refs[12:]
    state = map_ref.shape[1] // 2
    place = place_ref[0]

    @pl.when(jnp.logical_and(place > 0, place < count - 1))
    def _():
        cum = cum_ref[...]
        gt[...] = gain_of(dec_ref[...]) * tail_of(cum)
        lead = jnp.exp(cum)
        sl[...] = scale * lead

        def halo(full):
            return halo_ref[:, full].astype(f32)

        weighted_tails(start, heads_at, x_ref, wx_ref, halo, gt, pad, lw)
        led_gradients(start, heads_at, g_ref, sl, lg)
        lane_totals(lead, heads_at, tot_ref)
        u_ref[...] = state_of(map_ref[:, :state], lw[...])
        v_ref[...] = state_of(map_ref[:, state:], lg[...])


def end_state_kernel(count, start, heads_at, scale, *refs):
    place_ref, dec_ref, x_ref, g_ref, wx_ref, bc_ref, cum_ref, map_ref, _ = refs[:9]
    pay_ref, pad, gt, sl, lw, lg = refs[9:]
    state = map_ref.shape[1] // 2
    taps = wx_ref.shape[0]
    place = place_ref[0]

    @pl.when(place == 0)
    def _():
        gt[...] = gain_of(dec_ref[...]) * tail_of(cum_ref[...])
        none = jnp.zeros((HALO, LANES), f32)
        weighted_tails(start, heads_at, x_ref, wx_ref, lambda _: none, gt, pad, lw)
        pay_ref[0:state, :] = state_of(map_ref[:, :state], lw[...]).astype(bf16)

    @pl.when(place == count - 1)
    def _():
        sl[...] = scale * jnp.exp(cum_ref[...])
        led_gradients(start, heads_at, g_ref, sl, lg)
        c = map_ref[:, state:]
        late = lax.broadcasted_iota(jnp.int32, c.shape, 0) >= taps - 1
        pay_ref[0:state, :] = state_of(jnp.where(late, c, jnp.zeros_like(c)), lg[...]).astype(bf16)
        put_first_rows(pay_ref, lg, bc_ref, taps)


def message_kernel(hop, place_ref, u_ref, v_ref, tot_ref, came_ref, _, out_ref):
    own = jnp.where(place_ref[0] == hop, u_ref[...], v_ref[...])
    out_ref[...] = (own + tot_ref[0:1, :] * came_ref[...].astype(f32)).astype(bf16)


def fix_message_kernel(count, *refs):
    place_ref, u_ref, v_ref, tot_ref, came_ref, bc_ref, wbc_ref, _ = refs[:8]
    came_out, out_ref, more, bcpad = refs[8:]
    state = u_ref.shape[0]
    place = place_ref[0]
    tot = tot_ref[0:1, :]
    came_out[...] = came_ref[0:state, :]

    @pl.when(place == 1)
    def _():
        out_ref[...] = (u_ref[...] + tot * came_ref[0:state, :].astype(f32)).astype(bf16)

    @pl.when(place == count - 2)
    def _():
        more[...] = came_ref[state:, :].astype(f32)
        extra = first_rows_state(more, bc_ref, wbc_ref, bcpad)
        came = came_ref[0:state, :].astype(f32) + extra
        came_out[...] = came.astype(bf16)
        out_ref[...] = (v_ref[...] + tot * came).astype(bf16)


def edge_kernel(count, spans, parts, *refs):
    hops = count - 2
    place_ref, map_ref = refs[:2]
    blocks, refs = refs[3 : 3 + 2 * parts], refs[3 + 2 * parts :]
    came, (out_ref, edge) = refs[: 2 * hops], refs[2 * hops :]
    state = map_ref.shape[1] // 2
    b = map_ref[0:ROWS16, :state]
    per = len(spans) // 2
    for c in range(2):
        wanted = came[c * hops : (c + 1) * hops]
        grad = pick(place_ref[0], wanted, lambda hop: count - 2 - hop, state)
        extra = dot(b, grad)
        for q in range(per):
            part, lanes = spans[c * per + q]
            dx_ref, q_ref = blocks[2 * part : 2 * part + 2]
            here = slice(q * LANES, (q + 1) * LANES)
            rows = dx_ref[0:ROWS16, lanes] + q_ref[0:ROWS16, lanes].astype(f32) * extra[:, here]
            edge[4 * c : 4 * c + 4, here] = rows[0:4]
    out_ref[...] = edge[...].astype(bf16)


def intra_kernel(first, start, pairs, head_dim, scale, *refs):
    x_ref, g_ref, halo_ref, wx_ref, dec_ref, cum_ref, map_ref, skip_ref, _ = refs[:9]
    refs = refs[9:]
    if not first:
        dsim_in, gs_in = refs[:2]
        refs = refs[2:]
    y0_ref, dx_ref, q_ref, ls_ref, lw_ref, lg_ref, dsim_ref, gs_ref = refs[:8]
    pad, sim, gain = refs[8:]
    rows = x_ref.shape[0]
    state = map_ref.shape[1] // 2
    half = rows // 2
    gain[...] = gain_of(dec_ref[...])
    sim[...] = dot_nt(map_ref[:, state:], map_ref[:, :state])
    if first:
        dsim_ref[...] = jnp.zeros(dsim_ref.shape, f32)
        gs_ref[...] = jnp.zeros(gs_ref.shape, f32)
    else:
        dsim_ref[...] = dsim_in[...]
        gs_ref[...] = gs_in[...]
    lane = lax.broadcasted_iota(jnp.int32, (1, LANES), 1)
    low = lane < head_dim
    r_i = lax.broadcasted_iota(jnp.int32, (half, half), 0)
    c_i = lax.broadcasted_iota(jnp.int32, (half, half), 1)
    lower = r_i >= c_i

    def pair(q):
        lanes = slice(q * LANES, (q + 1) * LANES)
        full = slice(start + q * LANES, start + (q + 1) * LANES)
        h = start // head_dim + 2 * q
        one = pad.at[q]
        put_padded(one, halo_ref[:, full].astype(f32), x_ref[:, full])
        pre = conv_rows(one, tap_rows(wx_ref, full), rows)
        sg = sigmoid(pre)
        inner = (pre * sg).astype(bf16).astype(f32)
        sgrad = sg * (1.0 + pre * (1.0 - sg))
        gn = spread(*head_rows(gain, h))
        cums = head_rows(cum_ref, h)
        cols = [column(row) for row in cums]
        both = jnp.where(low, cols[0], cols[1])
        tl = jnp.exp(both[rows - 1 :] - both)
        ls = scale * jnp.exp(both)
        w = (inner * gn).astype(bf16)
        g = g_ref[:, full]
        gf = g.astype(f32)
        g_t = gf.T.astype(bf16)
        y = ds = None
        dw_t = []
        for a in range(2):
            row, col = cums[a], cols[a]
            keep = low if a == 0 else jnp.logical_not(low)
            d00 = jnp.exp(jnp.where(lower, col[:half] - row[:, :half], NEG))
            d10 = jnp.exp(col[half:] - row[:, :half])
            d11 = jnp.exp(jnp.where(lower, col[half:] - row[:, half:], NEG))
            m00 = (d00 * sim[0:half, 0:half]).astype(bf16)
            m10 = (d10 * sim[half:rows, 0:half]).astype(bf16)
            m11 = (d11 * sim[half:rows, half:rows]).astype(bf16)
            w_a = jnp.where(keep, w, jnp.zeros_like(w))
            top = dot(m00, w_a[:half])
            bot = dot(jnp.concatenate([m10, m11], axis=1), w_a)
            y_a = jnp.concatenate([top, bot], axis=0)
            y = y_a if y is None else y + y_a
            g_at = g_t[a * head_dim : (a + 1) * head_dim]
            left = dot(g_at, jnp.concatenate([m00, m10], axis=0))
            right = dot(g_at[:, half:], m11)
            dw_t.append(jnp.concatenate([left, right], axis=1))
            mix_top = dot_nt(g[:half], w_a[:half])
            mix_bot = dot_nt(g[half:], w_a)
            now = (d00 * mix_top, d10 * mix_bot[:, :half], d11 * mix_bot[:, half:])
            ds = now if ds is None else [one + two for one, two in zip(ds, now)]
        dsim_ref[0:half, 0:half] += ds[0]
        dsim_ref[half:rows, 0:half] += ds[1]
        dsim_ref[half:rows, half:rows] += ds[2]
        dw = scale * jnp.concatenate(dw_t, axis=0).T
        skip = jnp.where(low, skip_ref[:, h : h + 1], skip_ref[:, h + 1 : h + 2])
        y0_ref[:, lanes] = scale * y + skip * inner
        dx_ref[:, lanes] = (gn * dw + skip * gf) * sgrad
        q_ref[:, lanes] = (gn * tl * sgrad).astype(bf16)
        ls_ref[:, lanes] = ls.astype(bf16)
        lw_ref[:, lanes] = (inner * gn * tl).astype(bf16)
        lg_ref[:, lanes] = (gf * ls).astype(bf16)
        gi = jnp.sum(gf * inner, axis=0, keepdims=True)
        sum_a = jnp.sum(jnp.where(low, gi, 0.0), axis=1, keepdims=True)
        sum_b = jnp.sum(jnp.where(low, 0.0, gi), axis=1, keepdims=True)
        gs_ref[...] += jnp.where(lane == h, sum_a, 0.0) + jnp.where(lane == h + 1, sum_b, 0.0)

    for q in range(pairs):
        pair(q)


def pick(place, parts, wanted, state):
    total = jnp.zeros((state, parts[0].shape[1]), bf16)
    for hop, ref in enumerate(parts):
        total = jnp.where(place == wanted(hop), ref[0:state, :], total)
    return total


def add_states(spans, blocks, which, states, total):
    done = 0
    while done < len(spans):
        part, lanes = spans[done]
        size = 1
        while done + size < len(spans) and spans[done + size][0] == part:
            size += 1
        mine = slice(lanes.start, lanes.start + size * LANES)
        here = slice(done * LANES, (done + size) * LANES)
        made = dot_nt(blocks[2 * part + which][:, mine], states[:, here])
        total = made if total is None else total + made
        done += size
    return total


def before_silu(half, total, bc_ref, halo_ref, wbc_ref, bcpad):
    rows, bcw = bc_ref.shape
    state = bcw // 2
    taps = wbc_ref.shape[0]
    inner = halo_ref.shape[1] - bcw
    lanes = slice(half * state, (half + 1) * state)
    edge = halo_ref[:, inner + half * state : inner + (half + 1) * state].astype(f32)
    put_padded(bcpad, edge, bc_ref[:, lanes])
    dpre = total * silu_grad(conv_rows(bcpad, tap_rows(wbc_ref, lanes), rows))
    sums = []
    for k in range(taps):
        moved = bcpad[HALO - taps + 1 + k : HALO - taps + 1 + k + rows, :]
        sums.append(jnp.sum(dpre * moved, axis=0, keepdims=True))
    return dpre, jnp.concatenate(sums + [jnp.zeros((8 - taps, state), f32)], axis=0)


def finish_bc_kernel(count, first, spans, parts, scale, *refs):
    hops = count - 1
    place_ref, map_ref, sum_in = refs[:3]
    blocks, refs = refs[4 : 4 + 2 * parts], refs[4 + 2 * parts :]
    came, refs = refs[:hops], refs[hops:]
    bcw = map_ref.shape[1]
    state = bcw // 2
    place = place_ref[0]
    enter = pick(place, came, lambda hop: hop + 1, state)
    grad = pick(place, came, lambda hop: count - 2 - hop, state)
    if first:
        ds = scale * sum_in[...]
        high = ds.astype(bf16)
        rest = (ds - high.astype(f32)).astype(bf16)
        ds_t = ds.T
        high_t = ds_t.astype(bf16)
        rest_t = (ds_t - high_t.astype(f32)).astype(bf16)
        b, c = map_ref[:, :state], map_ref[:, state:]
        d_b = dot(high_t, c) + dot(rest_t, c)
        d_c = dot(high, b) + dot(rest, b)
    else:
        d_b, d_c = sum_in[:, :state], sum_in[:, state:]
    d_b = add_states(spans, blocks, 0, grad, d_b)
    d_c = add_states(spans, blocks, 1, enter, d_c)
    if first:
        (dbc_ref,) = refs
        dbc_ref[:, :state] = d_b
        dbc_ref[:, state:] = d_c
        return
    bc_ref, halo_ref, wbc_ref, gs_ref, own_ref, small_ref, bcpad = refs
    for half in range(2):
        lanes = slice(half * state, (half + 1) * state)
        made = before_silu(half, (d_b, d_c)[half], bc_ref, halo_ref, wbc_ref, bcpad.at[half])
        own_ref[:, lanes], small_ref[:, lanes] = made
    small_ref[:, bcw:] = gs_ref[...]


def finish_kernel(count, start, spans, parts, pieces, *refs):
    hops = count - 1
    place_ref, x_ref, wx_ref, map_ref = refs[:4]
    blocks, refs = refs[5 : 5 + 4 * parts], refs[5 + 4 * parts :]
    came, refs = refs[:hops], refs[hops:]
    if start:
        refs = refs[2:]
    y_hbm, gx_hbm, taps_ref, end_ref, enter, grad, pad, y_ref, gx_ref, sems = refs
    rows = x_ref.shape[0]
    taps = wx_ref.shape[0]
    state = enter.shape[0]
    place = place_ref[0]
    b, c = map_ref[:, :state], map_ref[:, state:]
    enter[...] = pick(place, came, lambda hop: hop + 1, state)
    grad[...] = pick(place, came, lambda hop: count - 2 - hop, state)
    copies = []
    first = 0
    for number, size in enumerate(pieces):
        for q in range(first, first + size):
            part, mine = spans[q]
            y0_ref, dx_ref, q_ref, ls_ref = blocks[4 * part : 4 * part + 4]
            lanes = slice(q * LANES, (q + 1) * LANES)
            full = slice(start + q * LANES, start + (q + 1) * LANES)
            inter = dot(c, enter[:, lanes])
            y_ref[:, lanes] = (y0_ref[:, mine] + ls_ref[:, mine].astype(f32) * inter).astype(bf16)
            one = pad.at[q]
            inter = dot(b, grad[:, lanes])
            one[0:rows, :] = dx_ref[:, mine] + q_ref[:, mine].astype(f32) * inter
            one[rows : rows + HALO, :] = jnp.zeros((HALO, LANES), f32)
            x = x_ref[:, full].astype(f32)
            total = None
            sums = []
            for k, weight in enumerate(tap_rows(wx_ref, full)):
                shifted = one[taps - 1 - k : taps - 1 - k + rows, :]
                term = weight * shifted
                total = term if total is None else total + term
                sums.append(jnp.sum(shifted * x, axis=0, keepdims=True))
            gx_ref[:, lanes] = total.astype(bf16)
            end_ref[:, lanes] = total[rows - ROWS16 :]
            sums = jnp.concatenate(sums + [jnp.zeros((8 - taps, LANES), f32)], axis=0)
            taps_ref[:, lanes] = sums
        lanes = slice(first * LANES, (first + size) * LANES)
        full = slice(start + first * LANES, start + (first + size) * LANES)
        for i, (made, out) in enumerate(((y_ref, y_hbm), (gx_ref, gx_hbm))):
            copy = pltpu.make_async_copy(made.at[:, lanes], out.at[:, full], sems.at[number, i])
            copy.start()
            copies.append(copy)
        first += size
    for copy in copies:
        copy.wait()


def sums_kernel(halo_ref, edge_ref, taps_a, taps_b, sums_ref, halo):
    taps, width = 4, taps_a.shape[1]
    edge = edge_ref[...].astype(f32)
    halo[...] = halo_ref[:, 0 : 2 * width].astype(f32)
    for c, own in enumerate((taps_a, taps_b)):
        lanes = slice(c * width, (c + 1) * width)
        sums_ref[:, lanes] = own[...]
        for k in range(taps - 1):
            added = None
            for j in range(taps - 1 - k):
                at = HALO - taps + 1 + k + j
                term = edge[4 * c + j : 4 * c + j + 1] * halo[at : at + 1, lanes]
                added = term if added is None else added + term
            sums_ref[k : k + 1, lanes] += added


def write_kernel(wx_ref, edge_ref, end_a, end_b, _, gx_in, gx_hbm, gx16, sem):
    taps = wx_ref.shape[0]
    rows = gx_hbm.shape[0]
    width = end_a.shape[1]
    edge = edge_ref[...].astype(f32)
    row = lax.broadcasted_iota(jnp.int32, (ROWS16, width), 0)
    for c, end_ref in enumerate((end_a, end_b)):
        lanes = slice(c * width, (c + 1) * width)
        end = end_ref[...]
        for k in range(taps - 1):
            for j in range(taps - 1 - k):
                at = ROWS16 - (taps - 1 - k) + j
                here = wx_ref[k : k + 1, lanes] * edge[4 * c + j : 4 * c + j + 1]
                end = end + jnp.where(row == at, here, 0.0)
        gx16[:, lanes] = end.astype(bf16)
    tail = pl.ds(rows - ROWS16, ROWS16)
    run_copies([pltpu.make_async_copy(gx16, gx_hbm.at[tail, :], sem.at[0])])


def pack_kernel(own_ref, small_ref, small_dp, small_out, head_ref):
    rows, bcw = own_ref.shape
    small = small_ref[...] + small_dp[...]
    small_out[...] = small
    head_ref[0:rows, :] = own_ref[...].astype(bf16)
    sums = small[:, :bcw]
    head_ref[rows:, :] = jnp.concatenate([sums, jnp.zeros_like(sums)], axis=0).astype(bf16)


def merge_kernel(heads, *refs):
    sums_ref, sums_dp, small_ref, own_ref = refs[:4]
    others, (full_ref, out_ref, send_ref) = refs[4 : 3 + heads], refs[3 + heads :]
    rows, bc = own_ref.shape
    total = sums_ref[...] + sums_dp[...]
    half = total.shape[1] // 2
    full = own_ref[...]
    taps_bc = small_ref[:, :bc]
    for other in others:
        block = other[...].astype(f32)
        full = full + block[:rows]
        taps_bc = taps_bc + block[rows : rows + 8]
    full_ref[...] = full
    send_ref[0:4, 0:half] = total[0:4, :half]
    send_ref[4:8, 0:half] = total[0:4, half:]
    send_ref[0:4, half : half + bc] = taps_bc[0:4]
    send_ref[4:8, half : half + bc] = full[0:4]
    send_ref[:, half + bc :] = small_ref[:, bc:]
    out_ref[...] = send_ref[...].astype(bf16)


def conv_bc_kernel(full_ref, wbc_ref, _, out_ref, pad):
    taps = wbc_ref.shape[0]
    rows, bcw = full_ref.shape
    for half in range(2):
        lanes = slice(half * bcw // 2, (half + 1) * bcw // 2)
        one = pad.at[half]
        one[0:rows, :] = full_ref[:, lanes]
        one[rows:, :] = jnp.zeros((HALO, bcw // 2), f32)
        out = None
        for k, weight in enumerate(tap_rows(wbc_ref, lanes)):
            term = weight * one[taps - 1 - k : taps - 1 - k + rows, :]
            out = term if out is None else out + term
        out_ref[:, lanes] = out


def last_kernel(count, norm_tokens, norm_skip, *refs):
    place_ref, sums_ref, conv_ref, wbc_ref = refs[:4]
    parts = refs[4 : 3 + count]
    gbc_ref, tx_ref, tbc_ref, skip_ref = refs[3 + count :]
    taps, bc = wbc_ref.shape
    rows = conv_ref.shape[0]
    half = tx_ref.shape[1] // 2
    total = sums_ref[...].astype(f32)
    edge = jnp.zeros((4, bc), f32)
    for hop, ref in enumerate(parts):
        block = ref[...].astype(f32)
        total = total + block
        if hop == count - 2:
            edge = jnp.where(place_ref[0] < count - 1, block[4:8, half : half + bc], 0.0)
    tx_ref[:, :half] = total[0:taps, 0:half] * norm_tokens
    tx_ref[:, half:] = total[4 : 4 + taps, 0:half] * norm_tokens
    tbc_ref[...] = total[0:taps, half : half + bc] * norm_tokens
    skip_ref[...] = total[0:1, half + bc : half + bc + skip_ref.shape[1]] * norm_skip
    gbc_ref[0 : rows - ROWS16, :] = conv_ref[0 : rows - ROWS16, :].astype(bf16)
    row = lax.broadcasted_iota(jnp.int32, (ROWS16, bc), 0)
    end = conv_ref[rows - ROWS16 :, :]
    for k in range(taps - 1):
        for j in range(taps - 1 - k):
            at = ROWS16 - (taps - 1 - k) + j
            end = end + jnp.where(row == at, wbc_ref[k : k + 1, :] * edge[j : j + 1], 0.0)
    gbc_ref[rows - ROWS16 :, :] = end.astype(bf16)


COST_US = {"middle_state": 1.5, "inside_block": 2.7, "sums": 0.8, "write": 0.8}
BYTES_PER_US = 3_500_000


def call(kernel, name, ins, outs, scratch=(), grid=(1,), kept=()):
    def spec(item):
        if not isinstance(item, tuple):
            whole = item.shape
            return pl.BlockSpec(whole, lambda *_: (0,) * len(whole))
        if item[1] == "smem":
            return pl.BlockSpec(memory_space=pltpu.SMEM)
        if item[1] == "any":
            return pl.BlockSpec(memory_space=pl.ANY)
        if item[1] == "hbm":
            return pl.BlockSpec(memory_space=pltpu.HBM)
        return pl.BlockSpec(item[1], item[2])

    def array(item):
        return item[0] if isinstance(item, tuple) else item

    return pl.pallas_call(
        kernel,
        grid=grid,
        in_specs=[spec(i) for i in ins],
        out_specs=[spec(o) for o in outs],
        out_shape=[array(o) for o in outs],
        scratch_shapes=list(scratch),
        compiler_params=pltpu.CompilerParams(vmem_limit_bytes=VMEM_LIMIT),
        cost_estimate=pl.CostEstimate(
            flops=0, bytes_accessed=int(COST_US.get(name, 0.01) * BYTES_PER_US), transcendentals=0
        ),
        input_output_aliases=dict(kept),
        name=name,
    )(*[array(i) for i in ins])


def chain_routes(count, hop):
    return [(hop, hop + 1), (count - 1 - hop, count - 2 - hop)]


def shape(s, d=f32):
    return jax.ShapeDtypeStruct(s, d)


def local(x_input, bc_input, decays, conv_x, conv_bc, skip_gain, grad_out):
    x, bc, dec, g = x_input[0], bc_input[0], decays[0], grad_out[0]
    rows, inner = x.shape
    taps = conv_x.shape[0]
    heads = dec.shape[0]
    head_dim = inner // heads
    bcw = bc.shape[1]
    state = bcw // 2
    scale = state ** (-0.5)
    count = lax.axis_size("seq")
    head_count = lax.axis_size("head")
    dp_count = lax.axis_size("dp")
    assert rows == BLOCK_LEN and 2 * head_dim == LANES and taps == 4
    assert count % 2 == 0 and count > 2 and dp_count == 2
    width = inner // 2
    chunks = (0, 1)
    block = 640 if width % 640 == 0 else LANES
    per = width // block
    pairs = width // LANES
    split = (pairs // 2, pairs + pairs // 5, pairs - pairs // 2 - pairs // 5)
    spans = [
        (part, slice(at * LANES, (at + 1) * LANES))
        for part, size in enumerate(split)
        for at in range(size)
    ]
    place = lax.axis_index("seq").astype(jnp.int32).reshape(1)
    where_am_i = (place, "smem")

    def vmem(s, d=f32):
        return pltpu.VMEM(s, d)

    def in_hbm(a):
        return (pltpu.with_memory_space_constraint(a, pltpu.HBM), "hbm")

    def padded(blocks, length=rows):
        return vmem((blocks, length + HALO, LANES))

    state_scratch = [
        padded(pairs),
        vmem((heads, rows)),
        vmem((heads, rows)),
        vmem((rows, width), bf16),
        vmem((rows, width), bf16),
    ]
    received = [[], []]

    def hop_on(c, message):
        routes = chain_routes(count, len(received[c]))
        received[c].append(lax.ppermute(message, "seq", routes))

    skip = skip_gain.reshape(1, heads)
    sources = [dec, conv_x, bc, conv_bc]
    xa, ga, *made, tails = call(
        functools.partial(early_load_kernel, count),
        "early_load",
        [where_am_i, in_hbm(x), in_hbm(g)] + [in_hbm(a) for a in sources],
        [shape((rows, width), bf16), shape((rows, width), bf16)]
        + [shape(a.shape, a.dtype) for a in sources]
        + [shape((HALO, inner + bcw), bf16)],
        [
            vmem((ROWS16, inner), bf16),
            vmem((ROWS16, bcw), bf16),
            pltpu.SemaphoreType.DMA((len(sources) + 4,)),
        ],
    )
    pay = call(
        functools.partial(first_state_kernel, count, scale),
        "first_state",
        [where_am_i, made[0], xa, ga, *made[1:], tails],
        [shape((state + ROWS16, width), bf16)],
        state_scratch
        + [vmem((rows + HALO, LANES)), vmem((HALO, inner + bcw)), vmem((ROWS16, width))],
    )[0]
    hop_on(0, pay)
    sources = [x, bc, g, dec, conv_x, conv_bc, skip]
    x, bc, g, dec, conv_x, conv_bc, skip = call(
        load_kernel,
        "load",
        [in_hbm(a) for a in sources] + [(pay, "any")],
        [shape(a.shape, a.dtype) for a in sources],
        [pltpu.SemaphoreType.DMA((len(sources),))],
    )
    halo = lax.ppermute(tails, "seq", [(i, i + 1) for i in range(1, count - 1)])

    states = [None, None]

    def middle_state(c, after):
        start = c * width
        states[c] = call(
            functools.partial(middle_state_kernel, count, start, start // head_dim, scale),
            "middle_state",
            [where_am_i, dec, x, g, halo, conv_x, cum, mapped, (after, "any")],
            [shape((state, width)), shape((state, width)), shape((8, width))],
            state_scratch,
        )
        return states[c][0]

    def message(c, after):
        return call(
            functools.partial(message_kernel, len(received[c])),
            "message",
            [where_am_i, *states[c], received[c][-1], (after, "any")],
            [shape((state, width), bf16)],
        )[0]

    parts = []
    carried = []

    def inside(number, after):
        first = number == 0
        start = sum(split[:number]) * LANES
        span = split[number] * LANES
        ins = [x, g, halo, conv_x, dec, cum, mapped, skip, (after, "any")]
        if not first:
            ins += carried
        made = call(
            functools.partial(intra_kernel, first, start, split[number], head_dim, scale),
            "inside_block",
            ins,
            [
                shape((rows, span)),
                shape((rows, span)),
                shape((rows, span), bf16),
                shape((rows, span), bf16),
                shape((rows, span), bf16),
                shape((rows, span), bf16),
                shape((rows, rows)),
                shape((8, LANES)),
            ],
            [padded(split[number]), vmem((rows, rows)), vmem((heads, rows))],
        )
        parts.append(made[:6])
        carried[:] = made[6:8]
        return made[0]

    def chunk_parts(c):
        mine = spans[c * pairs : (c + 1) * pairs]
        used = sorted({part for part, _ in mine})
        return [(used.index(part), at) for part, at in mine], [parts[p] for p in used]

    cum, mapped, u, v, tot, gt16, lg16 = call(
        functools.partial(middle_first_kernel, count, scale),
        "middle_first",
        [where_am_i, dec, x, g, conv_x, bc, conv_bc, (tails, "any")],
        [
            shape((heads, rows)),
            shape((rows, bcw), bf16),
            shape((state, width)),
            shape((state, width)),
            shape((8, width)),
            shape((ROWS16, width)),
            shape((ROWS16, width), bf16),
        ],
        state_scratch + [padded(2)],
    )
    after = call(
        functools.partial(end_state_kernel, count, width, width // head_dim, scale),
        "end_state",
        [where_am_i, dec, x, g, conv_x, bc, cum, mapped, (u, "any")],
        [shape((state + ROWS16, width), bf16)],
        state_scratch,
    )[0]
    hop_on(1, after)
    halo, mapped, u, v, came, after = call(
        functools.partial(fix_kernel, count),
        "fix_first_rows",
        [where_am_i, halo, received[0][0], x, conv_x, bc, conv_bc, mapped]
        + [u, v, tot, gt16, lg16, (after, "any")],
        [
            shape((HALO, inner + bcw), bf16),
            shape((rows, bcw), bf16),
            shape((state, width)),
            shape((state, width)),
            shape((state, width), bf16),
            shape((state, width), bf16),
        ],
        [
            vmem((HALO, inner + bcw)),
            vmem((ROWS16, width)),
            padded(pairs, ROWS16),
            padded(2, ROWS16),
        ],
    )
    states[0] = (u, v, tot)
    received[0][0] = came
    hop_on(0, after)
    after = middle_state(1, after)
    after = inside(0, after)
    for hop in range(1, count - 1):
        for c in chunks:
            if hop > 1:
                after = message(c, after)
                hop_on(c, after)
            elif c:
                came, after = call(
                    functools.partial(fix_message_kernel, count),
                    "message",
                    [where_am_i, *states[1], received[1][0], bc, conv_bc, (after, "any")],
                    [shape((state, width), bf16), shape((state, width), bf16)],
                    [vmem((ROWS16, width)), vmem((ROWS16 + HALO, LANES))],
                )
                received[1][0] = came
                hop_on(1, after)
            if hop == count - 2:
                after = inside(1 + c, after)
    dsim, gsum = carried
    ins = [where_am_i, mapped, (after, "any")]
    for made in parts:
        ins += made[1:3]
    edge = call(
        functools.partial(edge_kernel, count, spans, len(parts)),
        "edge",
        ins + received[0][: count - 2] + received[1][: count - 2],
        [shape((8, width), bf16)],
        [vmem((8, width))],
    )[0]

    edges = lax.ppermute(edge, "seq", [(i + 1, i) for i in range(count - 1)])

    def finish_bc(c, base, after):
        where, used = chunk_parts(c)
        ins = [where_am_i, mapped, base, (after, "any")]
        for made in used:
            ins += made[4:6]
        ins += received[c]
        outs = [shape((rows, bcw))]
        scratch = []
        if c:
            ins += [bc, halo, conv_bc, gsum]
            outs += [shape((8, bcw + LANES))]
            scratch = [padded(2)]
        kernel = functools.partial(finish_bc_kernel, count, c == 0, where, len(used), scale)
        return call(kernel, "finish_bc", ins, outs, scratch)

    def finish(c, after, kept_y):
        start = c * width
        where, used = chunk_parts(c)
        pieces = (4, 4, 2) if pairs == 10 else (pairs - 1, 1)
        ins = [where_am_i, x, conv_x, mapped, (after, "any")]
        for made in used:
            ins += made[:4]
        ins += received[c]
        kept = ()
        if kept_y:
            kept = ((len(ins), 0), (len(ins) + 1, 1))
            ins += [(a, "hbm") for a in kept_y]
        made = call(
            functools.partial(finish_kernel, count, start, where, len(used), pieces),
            "finish",
            ins,
            [(shape((rows, inner), bf16), "hbm"), (shape((rows, inner), bf16), "hbm")]
            + [shape((8, width)), shape((ROWS16, width))],
            [
                vmem((state, width), bf16),
                vmem((state, width), bf16),
                padded(pairs),
                vmem((rows, width), bf16),
                vmem((rows, width), bf16),
                pltpu.SemaphoreType.DMA((len(pieces), 2)),
            ],
            kept=kept,
        )
        return made[:2], made[2], made[3]

    outs, taps_a, end_a = finish(0, edge, None)
    dbc = finish_bc(0, dsim, taps_a)[0]
    own, small = finish_bc(1, dbc, edges)

    swap = [(0, 1), (1, 0)]
    turns = [[(i, (i + k) % head_count) for i in range(head_count)] for k in range(1, head_count)]
    small, to_heads = call(
        pack_kernel,
        "pack",
        [own, small, lax.ppermute(small, "dp", swap)],
        [shape(small.shape), shape((rows + ROWS16, bcw), bf16)],
    )
    others = [lax.ppermute(to_heads, "head", turn) for turn in turns]

    (y, gx), taps_b, end_b = finish(1, to_heads, outs)
    sums = call(
        sums_kernel,
        "sums",
        [halo, edge, taps_a, taps_b],
        [shape((8, inner))],
        [vmem((HALO, inner))],
    )[0]
    sums_dp = lax.ppermute(sums, "dp", swap)
    send_width = inner // 2 + bcw + LANES
    full, to_seq = call(
        functools.partial(merge_kernel, head_count),
        "merge",
        [sums, sums_dp, small, own] + others,
        [shape((rows, bcw)), shape((8, send_width), bf16)],
        [vmem((8, send_width))],
    )
    gx = call(
        write_kernel,
        "write",
        [conv_x, edges, end_a, end_b, (to_seq, "any"), (gx, "hbm")],
        [(shape((rows, inner), bf16), "hbm")],
        [vmem((ROWS16, inner), bf16), pltpu.SemaphoreType.DMA((1,))],
        kept=((5, 0),),
    )[0]
    from_seq = [
        lax.ppermute(to_seq, "seq", [(i, (i + k) % count) for i in range(count)])
        for k in range(1, count)
    ]
    token_count = rows * count * dp_count
    norm_tokens = float(token_count) ** (-0.5)
    norm_skip = float(token_count * head_dim) ** (-0.5)
    conv = call(
        conv_bc_kernel,
        "conv_bc",
        [full, conv_bc, (to_seq, "any")],
        [shape((rows, bcw))],
        [padded(2)],
    )[0]
    gbc, tx, tbc, skip = call(
        functools.partial(last_kernel, count, norm_tokens, norm_skip),
        "last",
        [where_am_i, to_seq, conv, conv_bc] + from_seq,
        [
            shape((rows, bcw), bf16),
            shape((taps, inner)),
            shape((taps, bcw)),
            shape((1, heads)),
        ],
    )
    return y[None], gx[None], gbc[None], tx, tbc, skip.reshape(heads)


def solution(mesh):
    return jax.shard_map(
        local,
        mesh=mesh,
        in_specs=(
            P(("groups", "dp"), "seq", "head"),
            P(("groups", "dp"), "seq", None),
            P(("groups", "dp"), "head", "seq"),
            P(None, "head"),
            P(),
            P("head"),
            P(("groups", "dp"), "seq", "head"),
        ),
        out_specs=(
            P(("groups", "dp"), "seq", "head"),
            P(("groups", "dp"), "seq", "head"),
            P(("groups", "dp"), "seq", None),
            P("groups", "head"),
            P("groups", None),
            P(("groups", "head")),
        ),
        check_vma=False,
    )
```

```python
import functools

import jax
import jax.numpy as jnp
from jax import lax
from jax.experimental import pallas as pl
from jax.experimental.pallas import tpu as pltpu
from jax.sharding import PartitionSpec as P

BLOCK_LEN = 256
LANES = 128
HALO = 8
NEG = -1e30
f32 = jnp.float32
bf16 = jnp.bfloat16
HIGHEST = lax.Precision.HIGHEST
ROWS16 = 16
MORE = 8
VMEM_LIMIT = 24 * 1024 * 1024


def dot(a, b, precision=None):
    return jnp.dot(a, b, preferred_element_type=f32, precision=precision)


def dot_nt(a, b):
    return lax.dot_general(a, b, (((1,), (1,)), ((), ())), preferred_element_type=f32)


def sigmoid(v):
    return 0.5 * jnp.tanh(0.5 * v) + 0.5


def conv_rows(pad_ref, weights, rows):
    first = HALO - len(weights) + 1
    total = None
    for k, weight in enumerate(weights):
        term = weight * pad_ref[first + k : first + k + rows, :]
        total = term if total is None else total + term
    return total


def tap_rows(ref, lanes):
    block = ref[:, lanes]
    return [block[k : k + 1] for k in range(block.shape[0])]


def silu_grad(pre):
    sg = sigmoid(pre)
    return sg * (1.0 + pre * (1.0 - sg))


def spread(row_a, row_b):
    half, rows = LANES // 2, row_a.shape[1]
    both = jnp.concatenate(
        [jnp.broadcast_to(row_a, (half, rows)), jnp.broadcast_to(row_b, (half, rows))], axis=0
    )
    return both.T


def column(row):
    return jnp.broadcast_to(row, (LANES, row.shape[1])).T


def running_sum(dec):
    rows = dec.shape[1]
    before = lax.broadcasted_iota(jnp.int32, (rows, rows), 0)
    after = lax.broadcasted_iota(jnp.int32, (rows, rows), 1)
    upper = (before <= after).astype(f32)
    return dot(jnp.log(dec), upper, HIGHEST)


def gain_of(dec):
    return jnp.sqrt((1.0 - dec) * (1.0 + dec))


def tail_of(cum):
    return jnp.exp(cum[:, -1:] - cum)


def put_padded(pad_ref, halo, block):
    pad_ref[0:HALO, :] = halo
    pad_ref[HALO : HALO + block.shape[0], :] = block.astype(f32)


def lane_blocks(width):
    return [slice(at, at + LANES) for at in range(0, width, LANES)]


def run_copies(copies):
    for copy in copies:
        copy.start()
    for copy in copies:
        copy.wait()


def early_load_kernel(count, *refs):
    place_ref, x_hbm, g_hbm = refs[:3]
    small = (len(refs) - 9) // 2
    sources, (xa, ga) = refs[3 : 3 + small], refs[3 + small : 5 + small]
    kept, (tails_ref, x16, bc16, sems) = refs[5 + small : -4], refs[-4:]
    bc_hbm = sources[2]
    rows, width = x_hbm.shape
    place = place_ref[0]
    chunk = pl.ds(0, xa.shape[1])
    last = pl.ds(rows - ROWS16, ROWS16)
    tails = [
        pltpu.make_async_copy(x_hbm.at[last, :], x16, sems.at[small + 2]),
        pltpu.make_async_copy(bc_hbm.at[last, :], bc16, sems.at[small + 3]),
    ]
    copies = [pltpu.make_async_copy(sources[i], kept[i], sems.at[i]) for i in range(small)]
    for copy in tails:
        copy.start()

    @pl.when(place == 0)
    def _():
        run_copies(copies + [pltpu.make_async_copy(x_hbm.at[:, chunk], xa, sems.at[small])])

    @pl.when(place == count - 1)
    def _():
        run_copies(copies + [pltpu.make_async_copy(g_hbm.at[:, chunk], ga, sems.at[small + 1])])

    for copy in tails:
        copy.wait()
    tails_ref[:, :width] = x16[...].astype(f32)[ROWS16 - HALO :].astype(bf16)
    tails_ref[:, width:] = bc16[...].astype(f32)[ROWS16 - HALO :].astype(bf16)


def load_kernel(*refs):
    count = (len(refs) - 2) // 2
    sources, kept, sems = refs[:count], refs[count + 1 : -1], refs[-1]
    run_copies(
        [pltpu.make_async_copy(sources[i], kept[i], sems.at[i]) for i in range(count)]
    )


def head_rows(ref, h):
    return ref[pl.ds(h, 1), :], ref[pl.ds(h + 1, 1), :]


def state_of(bc_rows, factors):
    over = (((0,), (0,)), ((), ()))
    return lax.dot_general(bc_rows, factors, over, preferred_element_type=f32)


def weighted_tails(start, heads_at, x_ref, wx_ref, halo, gt, pad, lw):
    rows, width = lw.shape
    for q, lanes in enumerate(lane_blocks(width)):
        full = slice(start + q * LANES, start + (q + 1) * LANES)
        one = pad.at[q]
        put_padded(one, halo(full), x_ref[:, full])
        pre = conv_rows(one, tap_rows(wx_ref, full), rows)
        inner = (pre * sigmoid(pre)).astype(bf16).astype(f32)
        factor = spread(*head_rows(gt, heads_at + 2 * q))
        lw[:, lanes] = (inner * factor).astype(bf16)


def led_gradients(start, heads_at, g_ref, sl, lg):
    for q, lanes in enumerate(lane_blocks(lg.shape[1])):
        full = slice(start + q * LANES, start + (q + 1) * LANES)
        lead = spread(*head_rows(sl, heads_at + 2 * q))
        lg[:, lanes] = (g_ref[:, full].astype(f32) * lead).astype(bf16)


def mapped_half(half, state, rows, bc_block, halo, wbc_ref, bcpad):
    lanes = slice(half * state, (half + 1) * state)
    put_padded(bcpad, halo, bc_block)
    pre = conv_rows(bcpad, tap_rows(wbc_ref, lanes), rows)
    return (pre * sigmoid(pre)).astype(bf16)


def put_first_rows(pay_ref, lg, bc_ref, more):
    state = pay_ref.shape[0] - MORE
    bcw = bc_ref.shape[1]
    more[0:4, :] = lg[0:ROWS16, :].astype(f32)[0:4]
    more[4:8, 0:bcw] = bc_ref[0:ROWS16, :].astype(f32)[0:4]
    more[4:8, bcw:] = jnp.zeros((4, lg.shape[1] - bcw), f32)
    pay_ref[state:, :] = more[...].astype(bf16)


def first_rows_state(more, bc_ref, wbc_ref, bcpad):
    rows, bcw = bc_ref.shape
    state = bcw // 2
    taps = wbc_ref.shape[0]
    zeros = jnp.zeros((ROWS16 - 4, state), f32)
    edge = bc_ref[rows - ROWS16 :, state:].astype(f32)[ROWS16 - HALO :]
    block = jnp.concatenate([more[4:8, state:bcw], zeros], axis=0)
    c = mapped_half(1, state, ROWS16, block, edge, wbc_ref, bcpad)
    early = lax.broadcasted_iota(jnp.int32, c.shape, 0) < taps - 1
    lg = jnp.concatenate([more[0:4, :], jnp.zeros((ROWS16 - 4, more.shape[1]), f32)], axis=0)
    return state_of(jnp.where(early, c, jnp.zeros_like(c)), lg.astype(bf16))


def bc_tail_place(r, taps, bcw):
    return 2 * taps - 2 + r // 2, slice((r % 2) * bcw, (r % 2 + 1) * bcw)


def first_state_kernel(count, scale, *refs):
    place_ref, dec_ref, xa_ref, ga_ref, wx_ref, bc_ref, wbc_ref, tails_ref = refs[:8]
    pay_ref, pad, gt, sl, lw, lg, bcpad, tails, more = refs[8:]
    rows, width = xa_ref.shape
    taps, bcw = wbc_ref.shape
    state = bcw // 2
    place = place_ref[0]
    none = jnp.zeros((HALO, LANES), f32)

    @pl.when(place == 0)
    def _():
        dec = dec_ref[...]
        gt[...] = gain_of(dec) * tail_of(running_sum(dec))
        b = mapped_half(0, state, rows, bc_ref[:, :state], none, wbc_ref, bcpad)
        weighted_tails(0, 0, xa_ref, wx_ref, lambda _: none, gt, pad, lw)
        pay_ref[0:state, :] = state_of(b, lw[...]).astype(bf16)
        tails[...] = tails_ref[...].astype(f32)
        more[0 : taps - 1, :] = tails[HALO - taps + 1 :, 0:width]
        more[taps - 1 : 2 * taps - 2, :] = tails[HALO - taps + 1 :, width : 2 * width]
        for r in range(taps - 1):
            at, here = bc_tail_place(r, taps, bcw)
            more[at : at + 1, here] = tails[HALO - taps + 1 + r :, 2 * width :][0:1]
        pay_ref[state:, :] = more[...].astype(bf16)

    @pl.when(place == count - 1)
    def _():
        sl[...] = scale * jnp.exp(running_sum(dec_ref[...]))
        c = mapped_half(1, state, rows, bc_ref[:, state:], none, wbc_ref, bcpad)
        late = lax.broadcasted_iota(jnp.int32, c.shape, 0) >= taps - 1
        led_gradients(0, 0, ga_ref, sl, lg)
        pay_ref[0:state, :] = state_of(jnp.where(late, c, jnp.zeros_like(c)), lg[...]).astype(bf16)
        put_first_rows(pay_ref, lg, bc_ref, more)


def middle_first_kernel(count, scale, *refs):
    place_ref, dec_ref, x_ref, g_ref, wx_ref, bc_ref, wbc_ref, _ = refs[:8]
    cum_ref, map_ref, u_ref, v_ref, tot_ref, gt16_ref, lg16_ref = refs[8:15]
    pad, gt, sl, lw, lg, bcpad = refs[15:]
    rows, bcw = bc_ref.shape
    state = bcw // 2
    none = jnp.zeros((HALO, LANES), f32)
    dec = dec_ref[...]
    cum = running_sum(dec)
    cum_ref[...] = cum
    for half in range(2):
        lanes = slice(half * state, (half + 1) * state)
        made = mapped_half(half, state, rows, bc_ref[:, lanes], none, wbc_ref, bcpad.at[half])
        map_ref[:, lanes] = made
    place = place_ref[0]

    @pl.when(jnp.logical_and(place > 0, place < count - 1))
    def _():
        gt[...] = gain_of(dec) * tail_of(cum)
        lead = jnp.exp(cum)
        sl[...] = scale * lead
        weighted_tails(0, 0, x_ref, wx_ref, lambda _: none, gt, pad, lw)
        led_gradients(0, 0, g_ref, sl, lg)
        lane_totals(lead, 0, tot_ref)
        for q, lanes in enumerate(lane_blocks(lw.shape[1])):
            half = LANES // 2
            a, b = (row[:, 0:LANES] for row in head_rows(gt, 2 * q))
            both = [jnp.broadcast_to(row, (half, LANES)) for row in (a, b)]
            gt16_ref[:, lanes] = jnp.concatenate(both, axis=0).T[0:ROWS16]
        lg16_ref[...] = lg[0:ROWS16, :]
        late = lax.broadcasted_iota(jnp.int32, (rows, state), 0) >= ROWS16
        zero = jnp.zeros((rows, state), bf16)
        u_ref[...] = state_of(jnp.where(late, map_ref[:, :state], zero), lw[...])
        v_ref[...] = state_of(jnp.where(late, map_ref[:, state:], zero), lg[...])


def fix_kernel(count, *refs):
    place_ref, halo_in, came_ref, x_ref, wx_ref, bc_ref, wbc_ref, map_in = refs[:8]
    u_in, v_in, tot_ref, gt16_ref, lg16_ref, _ = refs[8:14]
    halo_ref, map_ref, u_ref, v_ref, came_out, pay_ref, halo, more, pad, bcpad = refs[14:]
    rows, bcw = bc_ref.shape
    state = bcw // 2
    taps = wbc_ref.shape[0]
    width = u_in.shape[1]
    place = place_ref[0]
    more[...] = came_ref[state:, :].astype(f32)
    halo[...] = halo_in[...].astype(f32)

    @pl.when(place == 1)
    def _():
        halo[HALO - taps + 1 :, 0:width] = more[0 : taps - 1, :]
        halo[HALO - taps + 1 :, width : 2 * width] = more[taps - 1 : 2 * taps - 2, :]
        for r in range(taps - 1):
            at, here = bc_tail_place(r, taps, bcw)
            row = HALO - taps + 1 + r
            halo[row : row + 1, 2 * width :] = more[at : at + 1, here]

    halo_ref[...] = halo[...].astype(bf16)
    map_ref[...] = map_in[...]
    for half in range(2):
        lanes = slice(half * state, (half + 1) * state)
        edge = halo[:, 2 * width + half * state : 2 * width + (half + 1) * state]
        one = bcpad.at[half]
        made = mapped_half(half, state, ROWS16, bc_ref[0:ROWS16, lanes], edge, wbc_ref, one)
        map_ref[0:ROWS16, lanes] = made
    came_out[...] = came_ref[0:state, :]
    tot = tot_ref[0:1, :]

    @pl.when(jnp.logical_and(place > 0, place < count - 1))
    def _():
        lw16 = []
        for q, lanes in enumerate(lane_blocks(width)):
            one = pad.at[q]
            put_padded(one, halo[:, lanes], x_ref[0:ROWS16, lanes])
            pre = conv_rows(one, tap_rows(wx_ref, lanes), ROWS16)
            inner = (pre * sigmoid(pre)).astype(bf16).astype(f32)
            lw16.append((inner * gt16_ref[:, lanes]).astype(bf16))
        lw16 = jnp.concatenate(lw16, axis=1)
        u_ref[...] = u_in[...] + state_of(map_ref[0:ROWS16, :state], lw16)
        v_ref[...] = v_in[...] + state_of(map_ref[0:ROWS16, state:], lg16_ref[...])

    @pl.when(place == 1)
    def _():
        pay_ref[...] = (u_ref[...] + tot * came_ref[0:state, :].astype(f32)).astype(bf16)

    @pl.when(place == count - 2)
    def _():
        extra = first_rows_state(more, bc_ref, wbc_ref, bcpad.at[0])
        came = came_ref[0:state, :].astype(f32) + extra
        came_out[...] = came.astype(bf16)
        pay_ref[...] = (v_ref[...] + tot * came).astype(bf16)


def lane_totals(lead, heads_at, tot_ref):
    rows = lead.shape[1]
    for q, lanes in enumerate(lane_blocks(tot_ref.shape[1])):
        low = lax.broadcasted_iota(jnp.int32, (8, LANES), 1) < LANES // 2
        a, b = (lead[heads_at + 2 * q + i :, rows - 1 :][:1] for i in range(2))
        tot_ref[:, lanes] = jnp.where(low, a, b)


def middle_state_kernel(count, start, heads_at, scale, *refs):
    place_ref, dec_ref, x_ref, g_ref, halo_ref, wx_ref, cum_ref, map_ref, _ = refs[:9]
    u_ref, v_ref, tot_ref = refs[9:12]
    pad, gt, sl, lw, lg = refs[12:]
    state = map_ref.shape[1] // 2
    place = place_ref[0]

    @pl.when(jnp.logical_and(place > 0, place < count - 1))
    def _():
        cum = cum_ref[...]
        gt[...] = gain_of(dec_ref[...]) * tail_of(cum)
        lead = jnp.exp(cum)
        sl[...] = scale * lead

        def halo(full):
            return halo_ref[:, full].astype(f32)

        weighted_tails(start, heads_at, x_ref, wx_ref, halo, gt, pad, lw)
        led_gradients(start, heads_at, g_ref, sl, lg)
        lane_totals(lead, heads_at, tot_ref)
        u_ref[...] = state_of(map_ref[:, :state], lw[...])
        v_ref[...] = state_of(map_ref[:, state:], lg[...])


def end_state_kernel(count, start, heads_at, scale, *refs):
    place_ref, dec_ref, x_ref, g_ref, wx_ref, bc_ref, cum_ref, map_ref, _ = refs[:9]
    pay_ref, pad, gt, sl, lw, lg, more = refs[9:]
    state = map_ref.shape[1] // 2
    taps = wx_ref.shape[0]
    place = place_ref[0]

    @pl.when(place == 0)
    def _():
        gt[...] = gain_of(dec_ref[...]) * tail_of(cum_ref[...])
        none = jnp.zeros((HALO, LANES), f32)
        weighted_tails(start, heads_at, x_ref, wx_ref, lambda _: none, gt, pad, lw)
        pay_ref[0:state, :] = state_of(map_ref[:, :state], lw[...]).astype(bf16)

    @pl.when(place == count - 1)
    def _():
        sl[...] = scale * jnp.exp(cum_ref[...])
        led_gradients(start, heads_at, g_ref, sl, lg)
        c = map_ref[:, state:]
        late = lax.broadcasted_iota(jnp.int32, c.shape, 0) >= taps - 1
        pay_ref[0:state, :] = state_of(jnp.where(late, c, jnp.zeros_like(c)), lg[...]).astype(bf16)
        put_first_rows(pay_ref, lg, bc_ref, more)


def message_kernel(hop, place_ref, u_ref, v_ref, tot_ref, came_ref, _, out_ref):
    own = jnp.where(place_ref[0] == hop, u_ref[...], v_ref[...])
    out_ref[...] = (own + tot_ref[0:1, :] * came_ref[...].astype(f32)).astype(bf16)


def fix_message_kernel(count, *refs):
    place_ref, u_ref, v_ref, tot_ref, came_ref, bc_ref, wbc_ref, _ = refs[:8]
    came_out, out_ref, more, bcpad = refs[8:]
    state = u_ref.shape[0]
    place = place_ref[0]
    tot = tot_ref[0:1, :]
    came_out[...] = came_ref[0:state, :]

    @pl.when(place == 1)
    def _():
        out_ref[...] = (u_ref[...] + tot * came_ref[0:state, :].astype(f32)).astype(bf16)

    @pl.when(place == count - 2)
    def _():
        more[...] = came_ref[state:, :].astype(f32)
        extra = first_rows_state(more, bc_ref, wbc_ref, bcpad)
        came = came_ref[0:state, :].astype(f32) + extra
        came_out[...] = came.astype(bf16)
        out_ref[...] = (v_ref[...] + tot * came).astype(bf16)


def edge_kernel(count, spans, parts, *refs):
    hops = count - 2
    place_ref, map_ref = refs[:2]
    blocks, refs = refs[3 : 3 + 2 * parts], refs[3 + 2 * parts :]
    came, (out_ref, edge) = refs[: 2 * hops], refs[2 * hops :]
    state = map_ref.shape[1] // 2
    b = map_ref[0:ROWS16, :state]
    per = len(spans) // 2
    for c in range(2):
        wanted = came[c * hops : (c + 1) * hops]
        grad = pick(place_ref[0], wanted, lambda hop: count - 2 - hop, state)
        extra = dot(b, grad)
        for q in range(per):
            part, lanes = spans[c * per + q]
            dx_ref, q_ref = blocks[2 * part : 2 * part + 2]
            here = slice(q * LANES, (q + 1) * LANES)
            rows = dx_ref[0:ROWS16, lanes] + q_ref[0:ROWS16, lanes].astype(f32) * extra[:, here]
            edge[4 * c : 4 * c + 4, here] = rows[0:4]
    out_ref[...] = edge[...].astype(bf16)


def intra_kernel(first, start, pairs, head_dim, scale, *refs):
    x_ref, g_ref, halo_ref, wx_ref, dec_ref, cum_ref, map_ref, skip_ref, _ = refs[:9]
    refs = refs[9:]
    if not first:
        dsim_in, gs_in = refs[:2]
        refs = refs[2:]
    y0_ref, dx_ref, q_ref, ls_ref, lw_ref, lg_ref, dsim_ref, gs_ref = refs[:8]
    pad, sim, gain = refs[8:]
    rows = x_ref.shape[0]
    state = map_ref.shape[1] // 2
    half = rows // 2
    gain[...] = gain_of(dec_ref[...])
    sim[...] = dot_nt(map_ref[:, state:], map_ref[:, :state])
    if first:
        dsim_ref[...] = jnp.zeros(dsim_ref.shape, f32)
        gs_ref[...] = jnp.zeros(gs_ref.shape, f32)
    else:
        dsim_ref[...] = dsim_in[...]
        gs_ref[...] = gs_in[...]
    lane = lax.broadcasted_iota(jnp.int32, (1, LANES), 1)
    low = lane < head_dim
    r_i = lax.broadcasted_iota(jnp.int32, (half, half), 0)
    c_i = lax.broadcasted_iota(jnp.int32, (half, half), 1)
    lower = r_i >= c_i

    def pair(q):
        lanes = slice(q * LANES, (q + 1) * LANES)
        full = slice(start + q * LANES, start + (q + 1) * LANES)
        h = start // head_dim + 2 * q
        one = pad.at[q]
        put_padded(one, halo_ref[:, full].astype(f32), x_ref[:, full])
        pre = conv_rows(one, tap_rows(wx_ref, full), rows)
        sg = sigmoid(pre)
        inner = (pre * sg).astype(bf16).astype(f32)
        sgrad = sg * (1.0 + pre * (1.0 - sg))
        gn = spread(*head_rows(gain, h))
        cums = head_rows(cum_ref, h)
        cols = [column(row) for row in cums]
        both = jnp.where(low, cols[0], cols[1])
        tl = jnp.exp(both[rows - 1 :] - both)
        ls = scale * jnp.exp(both)
        w = (inner * gn).astype(bf16)
        g = g_ref[:, full]
        gf = g.astype(f32)
        g_t = gf.T.astype(bf16)
        y = ds = None
        dw_t = []
        for a in range(2):
            row, col = cums[a], cols[a]
            keep = low if a == 0 else jnp.logical_not(low)
            d00 = jnp.exp(jnp.where(lower, col[:half] - row[:, :half], NEG))
            d10 = jnp.exp(col[half:] - row[:, :half])
            d11 = jnp.exp(jnp.where(lower, col[half:] - row[:, half:], NEG))
            m00 = (d00 * sim[0:half, 0:half]).astype(bf16)
            m10 = (d10 * sim[half:rows, 0:half]).astype(bf16)
            m11 = (d11 * sim[half:rows, half:rows]).astype(bf16)
            w_a = jnp.where(keep, w, jnp.zeros_like(w))
            top = dot(m00, w_a[:half])
            bot = dot(jnp.concatenate([m10, m11], axis=1), w_a)
            y_a = jnp.concatenate([top, bot], axis=0)
            y = y_a if y is None else y + y_a
            g_at = g_t[a * head_dim : (a + 1) * head_dim]
            left = dot(g_at, jnp.concatenate([m00, m10], axis=0))
            right = dot(g_at[:, half:], m11)
            dw_t.append(jnp.concatenate([left, right], axis=1))
            mix_top = dot_nt(g[:half], w_a[:half])
            mix_bot = dot_nt(g[half:], w_a)
            now = (d00 * mix_top, d10 * mix_bot[:, :half], d11 * mix_bot[:, half:])
            ds = now if ds is None else [one + two for one, two in zip(ds, now)]
        dsim_ref[0:half, 0:half] += ds[0]
        dsim_ref[half:rows, 0:half] += ds[1]
        dsim_ref[half:rows, half:rows] += ds[2]
        dw = scale * jnp.concatenate(dw_t, axis=0).T
        skip = jnp.where(low, skip_ref[:, h : h + 1], skip_ref[:, h + 1 : h + 2])
        y0_ref[:, lanes] = scale * y + skip * inner
        dx_ref[:, lanes] = (gn * dw + skip * gf) * sgrad
        q_ref[:, lanes] = (gn * tl * sgrad).astype(bf16)
        ls_ref[:, lanes] = ls.astype(bf16)
        lw_ref[:, lanes] = (inner * gn * tl).astype(bf16)
        lg_ref[:, lanes] = (gf * ls).astype(bf16)
        gi = jnp.sum(gf * inner, axis=0, keepdims=True)
        sum_a = jnp.sum(jnp.where(low, gi, 0.0), axis=1, keepdims=True)
        sum_b = jnp.sum(jnp.where(low, 0.0, gi), axis=1, keepdims=True)
        gs_ref[...] += jnp.where(lane == h, sum_a, 0.0) + jnp.where(lane == h + 1, sum_b, 0.0)

    for q in range(pairs):
        pair(q)


def pick(place, parts, wanted, state):
    total = jnp.zeros((state, parts[0].shape[1]), bf16)
    for hop, ref in enumerate(parts):
        total = jnp.where(place == wanted(hop), ref[0:state, :], total)
    return total


def add_states(spans, blocks, which, states, total):
    done = 0
    while done < len(spans):
        part, lanes = spans[done]
        size = 1
        while done + size < len(spans) and spans[done + size][0] == part:
            size += 1
        mine = slice(lanes.start, lanes.start + size * LANES)
        here = slice(done * LANES, (done + size) * LANES)
        made = dot_nt(blocks[2 * part + which][:, mine], states[:, here])
        total = made if total is None else total + made
        done += size
    return total


def before_silu(half, total, bc_ref, halo_ref, wbc_ref, bcpad):
    rows, bcw = bc_ref.shape
    state = bcw // 2
    taps = wbc_ref.shape[0]
    inner = halo_ref.shape[1] - bcw
    lanes = slice(half * state, (half + 1) * state)
    edge = halo_ref[:, inner + half * state : inner + (half + 1) * state].astype(f32)
    put_padded(bcpad, edge, bc_ref[:, lanes])
    dpre = total * silu_grad(conv_rows(bcpad, tap_rows(wbc_ref, lanes), rows))
    sums = []
    for k in range(taps):
        moved = bcpad[HALO - taps + 1 + k : HALO - taps + 1 + k + rows, :]
        sums.append(jnp.sum(dpre * moved, axis=0, keepdims=True))
    return dpre, jnp.concatenate(sums + [jnp.zeros((8 - taps, state), f32)], axis=0)


def finish_bc_kernel(count, first, spans, parts, scale, *refs):
    hops = count - 1
    place_ref, map_ref, sum_in = refs[:3]
    blocks, refs = refs[4 : 4 + 2 * parts], refs[4 + 2 * parts :]
    came, refs = refs[:hops], refs[hops:]
    bcw = map_ref.shape[1]
    state = bcw // 2
    place = place_ref[0]
    enter = pick(place, came, lambda hop: hop + 1, state)
    grad = pick(place, came, lambda hop: count - 2 - hop, state)
    if first:
        ds = scale * sum_in[...]
        high = ds.astype(bf16)
        rest = (ds - high.astype(f32)).astype(bf16)
        ds_t = ds.T
        high_t = ds_t.astype(bf16)
        rest_t = (ds_t - high_t.astype(f32)).astype(bf16)
        b, c = map_ref[:, :state], map_ref[:, state:]
        d_b = dot(high_t, c) + dot(rest_t, c)
        d_c = dot(high, b) + dot(rest, b)
    else:
        d_b, d_c = sum_in[:, :state], sum_in[:, state:]
    d_b = add_states(spans, blocks, 0, grad, d_b)
    d_c = add_states(spans, blocks, 1, enter, d_c)
    if first:
        (dbc_ref,) = refs
        dbc_ref[:, :state] = d_b
        dbc_ref[:, state:] = d_c
        return
    bc_ref, halo_ref, wbc_ref, gs_ref, own_ref, small_ref, bcpad = refs
    for half in range(2):
        lanes = slice(half * state, (half + 1) * state)
        made = before_silu(half, (d_b, d_c)[half], bc_ref, halo_ref, wbc_ref, bcpad.at[half])
        own_ref[:, lanes], small_ref[:, lanes] = made
    small_ref[:, bcw:] = gs_ref[...]


def finish_kernel(count, start, spans, parts, pieces, *refs):
    hops = count - 1
    place_ref, x_ref, wx_ref, map_ref = refs[:4]
    blocks, refs = refs[5 : 5 + 4 * parts], refs[5 + 4 * parts :]
    came, refs = refs[:hops], refs[hops:]
    if start:
        refs = refs[2:]
    y_hbm, gx_hbm, taps_ref, end_ref, enter, grad, pad, y_ref, gx_ref, sems = refs
    rows = x_ref.shape[0]
    taps = wx_ref.shape[0]
    state = enter.shape[0]
    place = place_ref[0]
    b, c = map_ref[:, :state], map_ref[:, state:]
    enter[...] = pick(place, came, lambda hop: hop + 1, state)
    grad[...] = pick(place, came, lambda hop: count - 2 - hop, state)
    copies = []
    first = 0
    for number, size in enumerate(pieces):
        for q in range(first, first + size):
            part, mine = spans[q]
            y0_ref, dx_ref, q_ref, ls_ref = blocks[4 * part : 4 * part + 4]
            lanes = slice(q * LANES, (q + 1) * LANES)
            full = slice(start + q * LANES, start + (q + 1) * LANES)
            inter = dot(c, enter[:, lanes])
            y_ref[:, lanes] = (y0_ref[:, mine] + ls_ref[:, mine].astype(f32) * inter).astype(bf16)
            one = pad.at[q]
            inter = dot(b, grad[:, lanes])
            one[0:rows, :] = dx_ref[:, mine] + q_ref[:, mine].astype(f32) * inter
            one[rows : rows + HALO, :] = jnp.zeros((HALO, LANES), f32)
            x = x_ref[:, full].astype(f32)
            total = None
            sums = []
            for k, weight in enumerate(tap_rows(wx_ref, full)):
                shifted = one[taps - 1 - k : taps - 1 - k + rows, :]
                term = weight * shifted
                total = term if total is None else total + term
                sums.append(jnp.sum(shifted * x, axis=0, keepdims=True))
            gx_ref[:, lanes] = total.astype(bf16)
            end_ref[:, lanes] = total[rows - ROWS16 :]
            sums = jnp.concatenate(sums + [jnp.zeros((8 - taps, LANES), f32)], axis=0)
            taps_ref[:, lanes] = sums
        lanes = slice(first * LANES, (first + size) * LANES)
        full = slice(start + first * LANES, start + (first + size) * LANES)
        for i, (made, out) in enumerate(((y_ref, y_hbm), (gx_ref, gx_hbm))):
            copy = pltpu.make_async_copy(made.at[:, lanes], out.at[:, full], sems.at[number, i])
            copy.start()
            copies.append(copy)
        first += size
    for copy in copies:
        copy.wait()


def sums_kernel(halo_ref, edge_ref, taps_a, taps_b, sums_ref, halo):
    taps, width = 4, taps_a.shape[1]
    edge = edge_ref[...].astype(f32)
    halo[...] = halo_ref[:, 0 : 2 * width].astype(f32)
    for c, own in enumerate((taps_a, taps_b)):
        lanes = slice(c * width, (c + 1) * width)
        sums_ref[:, lanes] = own[...]
        for k in range(taps - 1):
            added = None
            for j in range(taps - 1 - k):
                at = HALO - taps + 1 + k + j
                term = edge[4 * c + j : 4 * c + j + 1] * halo[at : at + 1, lanes]
                added = term if added is None else added + term
            sums_ref[k : k + 1, lanes] += added


def write_kernel(wx_ref, edge_ref, end_a, end_b, _, gx_in, gx_hbm, gx16, sem):
    taps = wx_ref.shape[0]
    rows = gx_hbm.shape[0]
    width = end_a.shape[1]
    edge = edge_ref[...].astype(f32)
    row = lax.broadcasted_iota(jnp.int32, (ROWS16, width), 0)
    for c, end_ref in enumerate((end_a, end_b)):
        lanes = slice(c * width, (c + 1) * width)
        end = end_ref[...]
        for k in range(taps - 1):
            for j in range(taps - 1 - k):
                at = ROWS16 - (taps - 1 - k) + j
                here = wx_ref[k : k + 1, lanes] * edge[4 * c + j : 4 * c + j + 1]
                end = end + jnp.where(row == at, here, 0.0)
        gx16[:, lanes] = end.astype(bf16)
    tail = pl.ds(rows - ROWS16, ROWS16)
    run_copies([pltpu.make_async_copy(gx16, gx_hbm.at[tail, :], sem.at[0])])


def pack_kernel(own_ref, small_ref, small_dp, _, small_out, head_ref):
    rows, bcw = own_ref.shape
    small = small_ref[...] + small_dp[...]
    small_out[...] = small
    head_ref[0:rows, :] = own_ref[...].astype(bf16)
    sums = small[:, :bcw]
    head_ref[rows:, :] = jnp.concatenate([sums, jnp.zeros_like(sums)], axis=0).astype(bf16)


def merge_kernel(heads, *refs):
    sums_ref, sums_dp, small_ref, own_ref = refs[:4]
    others, (full_ref, out_ref, send_ref) = refs[4 : 3 + heads], refs[3 + heads :]
    rows, bc = own_ref.shape
    total = sums_ref[...] + sums_dp[...]
    half = total.shape[1] // 2
    full = own_ref[...]
    taps_bc = small_ref[:, :bc]
    for other in others:
        block = other[...].astype(f32)
        full = full + block[:rows]
        taps_bc = taps_bc + block[rows : rows + 8]
    full_ref[...] = full
    send_ref[0:4, 0:half] = total[0:4, :half]
    send_ref[4:8, 0:half] = total[0:4, half:]
    send_ref[0:4, half : half + bc] = taps_bc[0:4]
    send_ref[4:8, half : half + bc] = full[0:4]
    send_ref[:, half + bc :] = small_ref[:, bc:]
    out_ref[...] = send_ref[...].astype(bf16)


def conv_bc_kernel(full_ref, wbc_ref, _, out_ref, pad):
    taps = wbc_ref.shape[0]
    rows, bcw = full_ref.shape
    for half in range(2):
        lanes = slice(half * bcw // 2, (half + 1) * bcw // 2)
        one = pad.at[half]
        one[0:rows, :] = full_ref[:, lanes]
        one[rows:, :] = jnp.zeros((HALO, bcw // 2), f32)
        out = None
        for k, weight in enumerate(tap_rows(wbc_ref, lanes)):
            term = weight * one[taps - 1 - k : taps - 1 - k + rows, :]
            out = term if out is None else out + term
        out_ref[:, lanes] = out


def last_kernel(count, norm_tokens, norm_skip, *refs):
    place_ref, sums_ref, conv_ref, wbc_ref = refs[:4]
    parts = refs[4 : 3 + count]
    gbc_ref, tx_ref, tbc_ref, skip_ref = refs[3 + count :]
    taps, bc = wbc_ref.shape
    rows = conv_ref.shape[0]
    half = tx_ref.shape[1] // 2
    total = sums_ref[...].astype(f32)
    edge = jnp.zeros((4, bc), f32)
    for hop, ref in enumerate(parts):
        block = ref[...].astype(f32)
        total = total + block
        if hop == count - 2:
            edge = jnp.where(place_ref[0] < count - 1, block[4:8, half : half + bc], 0.0)
    tx_ref[:, :half] = total[0:taps, 0:half] * norm_tokens
    tx_ref[:, half:] = total[4 : 4 + taps, 0:half] * norm_tokens
    tbc_ref[...] = total[0:taps, half : half + bc] * norm_tokens
    skip_ref[...] = total[0:1, half + bc : half + bc + skip_ref.shape[1]] * norm_skip
    gbc_ref[0 : rows - ROWS16, :] = conv_ref[0 : rows - ROWS16, :].astype(bf16)
    row = lax.broadcasted_iota(jnp.int32, (ROWS16, bc), 0)
    end = conv_ref[rows - ROWS16 :, :]
    for k in range(taps - 1):
        for j in range(taps - 1 - k):
            at = ROWS16 - (taps - 1 - k) + j
            end = end + jnp.where(row == at, wbc_ref[k : k + 1, :] * edge[j : j + 1], 0.0)
    gbc_ref[rows - ROWS16 :, :] = end.astype(bf16)


COST_US = {"middle_state": 1.5, "inside_block": 2.7, "sums": 0.8, "write": 0.8}
BYTES_PER_US = 3_500_000


def call(kernel, name, ins, outs, scratch=(), grid=(1,), kept=()):
    def spec(item):
        if not isinstance(item, tuple):
            whole = item.shape
            return pl.BlockSpec(whole, lambda *_: (0,) * len(whole))
        if item[1] == "smem":
            return pl.BlockSpec(memory_space=pltpu.SMEM)
        if item[1] == "any":
            return pl.BlockSpec(memory_space=pl.ANY)
        if item[1] == "hbm":
            return pl.BlockSpec(memory_space=pltpu.HBM)
        return pl.BlockSpec(item[1], item[2])

    def array(item):
        return item[0] if isinstance(item, tuple) else item

    return pl.pallas_call(
        kernel,
        grid=grid,
        in_specs=[spec(i) for i in ins],
        out_specs=[spec(o) for o in outs],
        out_shape=[array(o) for o in outs],
        scratch_shapes=list(scratch),
        compiler_params=pltpu.CompilerParams(vmem_limit_bytes=VMEM_LIMIT),
        cost_estimate=pl.CostEstimate(
            flops=0, bytes_accessed=int(COST_US.get(name, 0.01) * BYTES_PER_US), transcendentals=0
        ),
        input_output_aliases=dict(kept),
        name=name,
    )(*[array(i) for i in ins])


def chain_routes(count, hop):
    return [(hop, hop + 1), (count - 1 - hop, count - 2 - hop)]


def shape(s, d=f32):
    return jax.ShapeDtypeStruct(s, d)


def local(x_input, bc_input, decays, conv_x, conv_bc, skip_gain, grad_out):
    x, bc, dec, g = x_input[0], bc_input[0], decays[0], grad_out[0]
    rows, inner = x.shape
    taps = conv_x.shape[0]
    heads = dec.shape[0]
    head_dim = inner // heads
    bcw = bc.shape[1]
    state = bcw // 2
    scale = state ** (-0.5)
    count = lax.axis_size("seq")
    head_count = lax.axis_size("head")
    dp_count = lax.axis_size("dp")
    assert rows == BLOCK_LEN and 2 * head_dim == LANES and taps == 4
    assert count % 2 == 0 and count > 2 and dp_count == 2
    width = inner // 2
    chunks = (0, 1)
    block = 640 if width % 640 == 0 else LANES
    per = width // block
    pairs = width // LANES
    split = (pairs // 2, pairs + pairs // 5, pairs - pairs // 2 - pairs // 5)
    spans = [
        (part, slice(at * LANES, (at + 1) * LANES))
        for part, size in enumerate(split)
        for at in range(size)
    ]
    place = lax.axis_index("seq").astype(jnp.int32).reshape(1)
    where_am_i = (place, "smem")

    def vmem(s, d=f32):
        return pltpu.VMEM(s, d)

    def in_hbm(a):
        return (pltpu.with_memory_space_constraint(a, pltpu.HBM), "hbm")

    def padded(blocks, length=rows):
        return vmem((blocks, length + HALO, LANES))

    state_scratch = [
        padded(pairs),
        vmem((heads, rows)),
        vmem((heads, rows)),
        vmem((rows, width), bf16),
        vmem((rows, width), bf16),
    ]
    received = [[], []]

    def hop_on(c, message):
        routes = chain_routes(count, len(received[c]))
        received[c].append(lax.ppermute(message, "seq", routes))

    skip = skip_gain.reshape(1, heads)
    sources = [dec, conv_x, bc, conv_bc]
    xa, ga, *made, tails = call(
        functools.partial(early_load_kernel, count),
        "early_load",
        [where_am_i, in_hbm(x), in_hbm(g)] + [in_hbm(a) for a in sources],
        [shape((rows, width), bf16), shape((rows, width), bf16)]
        + [shape(a.shape, a.dtype) for a in sources]
        + [shape((HALO, inner + bcw), bf16)],
        [
            vmem((ROWS16, inner), bf16),
            vmem((ROWS16, bcw), bf16),
            pltpu.SemaphoreType.DMA((len(sources) + 4,)),
        ],
    )
    pay = call(
        functools.partial(first_state_kernel, count, scale),
        "first_state",
        [where_am_i, made[0], xa, ga, *made[1:], tails],
        [shape((state + MORE, width), bf16)],
        state_scratch
        + [vmem((rows + HALO, LANES)), vmem((HALO, inner + bcw)), vmem((MORE, width))],
    )[0]
    hop_on(0, pay)
    sources = [x, bc, g, dec, conv_x, conv_bc, skip]
    x, bc, g, dec, conv_x, conv_bc, skip = call(
        load_kernel,
        "load",
        [in_hbm(a) for a in sources] + [(pay, "any")],
        [shape(a.shape, a.dtype) for a in sources],
        [pltpu.SemaphoreType.DMA((len(sources),))],
    )
    halo = lax.ppermute(tails, "seq", [(i, i + 1) for i in range(1, count - 1)])

    states = [None, None]

    def middle_state(c, after):
        start = c * width
        states[c] = call(
            functools.partial(middle_state_kernel, count, start, start // head_dim, scale),
            "middle_state",
            [where_am_i, dec, x, g, halo, conv_x, cum, mapped, (after, "any")],
            [shape((state, width)), shape((state, width)), shape((8, width))],
            state_scratch,
        )
        return states[c][0]

    def message(c, after):
        return call(
            functools.partial(message_kernel, len(received[c])),
            "message",
            [where_am_i, *states[c], received[c][-1], (after, "any")],
            [shape((state, width), bf16)],
        )[0]

    parts = []
    carried = []

    def inside(number, after):
        first = number == 0
        start = sum(split[:number]) * LANES
        span = split[number] * LANES
        ins = [x, g, halo, conv_x, dec, cum, mapped, skip, (after, "any")]
        if not first:
            ins += carried
        made = call(
            functools.partial(intra_kernel, first, start, split[number], head_dim, scale),
            "inside_block",
            ins,
            [
                shape((rows, span)),
                shape((rows, span)),
                shape((rows, span), bf16),
                shape((rows, span), bf16),
                shape((rows, span), bf16),
                shape((rows, span), bf16),
                shape((rows, rows)),
                shape((8, LANES)),
            ],
            [padded(split[number]), vmem((rows, rows)), vmem((heads, rows))],
        )
        parts.append(made[:6])
        carried[:] = made[6:8]
        return made[0]

    def chunk_parts(c):
        mine = spans[c * pairs : (c + 1) * pairs]
        used = sorted({part for part, _ in mine})
        return [(used.index(part), at) for part, at in mine], [parts[p] for p in used]

    cum, mapped, u, v, tot, gt16, lg16 = call(
        functools.partial(middle_first_kernel, count, scale),
        "middle_first",
        [where_am_i, dec, x, g, conv_x, bc, conv_bc, (tails, "any")],
        [
            shape((heads, rows)),
            shape((rows, bcw), bf16),
            shape((state, width)),
            shape((state, width)),
            shape((8, width)),
            shape((ROWS16, width)),
            shape((ROWS16, width), bf16),
        ],
        state_scratch + [padded(2)],
    )
    after = call(
        functools.partial(end_state_kernel, count, width, width // head_dim, scale),
        "end_state",
        [where_am_i, dec, x, g, conv_x, bc, cum, mapped, (u, "any")],
        [shape((state + MORE, width), bf16)],
        state_scratch + [vmem((MORE, width))],
    )[0]
    hop_on(1, after)
    halo, mapped, u, v, came, after = call(
        functools.partial(fix_kernel, count),
        "fix_first_rows",
        [where_am_i, halo, received[0][0], x, conv_x, bc, conv_bc, mapped]
        + [u, v, tot, gt16, lg16, (after, "any")],
        [
            shape((HALO, inner + bcw), bf16),
            shape((rows, bcw), bf16),
            shape((state, width)),
            shape((state, width)),
            shape((state, width), bf16),
            shape((state, width), bf16),
        ],
        [
            vmem((HALO, inner + bcw)),
            vmem((MORE, width)),
            padded(pairs, ROWS16),
            padded(2, ROWS16),
        ],
    )
    states[0] = (u, v, tot)
    received[0][0] = came
    hop_on(0, after)
    after = middle_state(1, after)
    after = inside(0, after)
    for hop in range(1, count - 1):
        for c in chunks:
            if hop > 1:
                after = message(c, after)
                hop_on(c, after)
            elif c:
                came, after = call(
                    functools.partial(fix_message_kernel, count),
                    "message",
                    [where_am_i, *states[1], received[1][0], bc, conv_bc, (after, "any")],
                    [shape((state, width), bf16), shape((state, width), bf16)],
                    [vmem((MORE, width)), vmem((ROWS16 + HALO, LANES))],
                )
                received[1][0] = came
                hop_on(1, after)
            if hop == count - 2:
                after = inside(1 + c, after)
    dsim, gsum = carried
    ins = [where_am_i, mapped, (after, "any")]
    for made in parts:
        ins += made[1:3]
    edge = call(
        functools.partial(edge_kernel, count, spans, len(parts)),
        "edge",
        ins + received[0][: count - 2] + received[1][: count - 2],
        [shape((8, width), bf16)],
        [vmem((8, width))],
    )[0]

    edges = lax.ppermute(edge, "seq", [(i + 1, i) for i in range(count - 1)])

    def finish_bc(c, base, after):
        where, used = chunk_parts(c)
        ins = [where_am_i, mapped, base, (after, "any")]
        for made in used:
            ins += made[4:6]
        ins += received[c]
        outs = [shape((rows, bcw))]
        scratch = []
        if c:
            ins += [bc, halo, conv_bc, gsum]
            outs += [shape((8, bcw + LANES))]
            scratch = [padded(2)]
        kernel = functools.partial(finish_bc_kernel, count, c == 0, where, len(used), scale)
        return call(kernel, "finish_bc", ins, outs, scratch)

    def finish(c, after, kept_y):
        start = c * width
        where, used = chunk_parts(c)
        pieces = (4, 4, 2) if pairs == 10 else (pairs - 1, 1)
        ins = [where_am_i, x, conv_x, mapped, (after, "any")]
        for made in used:
            ins += made[:4]
        ins += received[c]
        kept = ()
        if kept_y:
            kept = ((len(ins), 0), (len(ins) + 1, 1))
            ins += [(a, "hbm") for a in kept_y]
        made = call(
            functools.partial(finish_kernel, count, start, where, len(used), pieces),
            "finish",
            ins,
            [(shape((rows, inner), bf16), "hbm"), (shape((rows, inner), bf16), "hbm")]
            + [shape((8, width)), shape((ROWS16, width))],
            [
                vmem((state, width), bf16),
                vmem((state, width), bf16),
                padded(pairs),
                vmem((rows, width), bf16),
                vmem((rows, width), bf16),
                pltpu.SemaphoreType.DMA((len(pieces), 2)),
            ],
            kept=kept,
        )
        return made[:2], made[2], made[3]

    outs, taps_a, end_a = finish(0, edge, None)
    dbc = finish_bc(0, dsim, taps_a)[0]
    own, small = finish_bc(1, dbc, dbc)

    swap = [(0, 1), (1, 0)]
    turns = [[(i, (i + k) % head_count) for i in range(head_count)] for k in range(1, head_count)]
    small, to_heads = call(
        pack_kernel,
        "pack",
        [own, small, lax.ppermute(small, "dp", swap), (edges, "any")],
        [shape(small.shape), shape((rows + ROWS16, bcw), bf16)],
    )
    others = [lax.ppermute(to_heads, "head", turn) for turn in turns]

    (y, gx), taps_b, end_b = finish(1, to_heads, outs)
    sums = call(
        sums_kernel,
        "sums",
        [halo, edge, taps_a, taps_b],
        [shape((8, inner))],
        [vmem((HALO, inner))],
    )[0]
    sums_dp = lax.ppermute(sums, "dp", swap)
    send_width = inner // 2 + bcw + LANES
    full, to_seq = call(
        functools.partial(merge_kernel, head_count),
        "merge",
        [sums, sums_dp, small, own] + others,
        [shape((rows, bcw)), shape((8, send_width), bf16)],
        [vmem((8, send_width))],
    )
    gx = call(
        write_kernel,
        "write",
        [conv_x, edges, end_a, end_b, (to_seq, "any"), (gx, "hbm")],
        [(shape((rows, inner), bf16), "hbm")],
        [vmem((ROWS16, inner), bf16), pltpu.SemaphoreType.DMA((1,))],
        kept=((5, 0),),
    )[0]
    from_seq = [
        lax.ppermute(to_seq, "seq", [(i, (i + k) % count) for i in range(count)])
        for k in range(1, count)
    ]
    token_count = rows * count * dp_count
    norm_tokens = float(token_count) ** (-0.5)
    norm_skip = float(token_count * head_dim) ** (-0.5)
    conv = call(
        conv_bc_kernel,
        "conv_bc",
        [full, conv_bc, (to_seq, "any")],
        [shape((rows, bcw))],
        [padded(2)],
    )[0]
    gbc, tx, tbc, skip = call(
        functools.partial(last_kernel, count, norm_tokens, norm_skip),
        "last",
        [where_am_i, to_seq, conv, conv_bc] + from_seq,
        [
            shape((rows, bcw), bf16),
            shape((taps, inner)),
            shape((taps, bcw)),
            shape((1, heads)),
        ],
    )
    return y[None], gx[None], gbc[None], tx, tbc, skip.reshape(heads)


def solution(mesh):
    return jax.shard_map(
        local,
        mesh=mesh,
        in_specs=(
            P(("groups", "dp"), "seq", "head"),
            P(("groups", "dp"), "seq", None),
            P(("groups", "dp"), "head", "seq"),
            P(None, "head"),
            P(),
            P("head"),
            P(("groups", "dp"), "seq", "head"),
        ),
        out_specs=(
            P(("groups", "dp"), "seq", "head"),
            P(("groups", "dp"), "seq", "head"),
            P(("groups", "dp"), "seq", None),
            P("groups", "head"),
            P("groups", None),
            P(("groups", "head")),
        ),
        check_vma=False,
    )
```

```python
import functools

import jax
import jax.numpy as jnp
from jax import lax
from jax.experimental import pallas as pl
from jax.experimental.pallas import tpu as pltpu
from jax.sharding import PartitionSpec as P

BLOCK_LEN = 256
LANES = 128
HALO = 8
NEG = -1e30
f32 = jnp.float32
bf16 = jnp.bfloat16
HIGHEST = lax.Precision.HIGHEST
ROWS16 = 16
MORE = 8
VMEM_LIMIT = 24 * 1024 * 1024


def dot(a, b, precision=None):
    return jnp.dot(a, b, preferred_element_type=f32, precision=precision)


def dot_nt(a, b):
    return lax.dot_general(a, b, (((1,), (1,)), ((), ())), preferred_element_type=f32)


def sigmoid(v):
    return 0.5 * jnp.tanh(0.5 * v) + 0.5


def conv_rows(pad_ref, weights, rows):
    first = HALO - len(weights) + 1
    total = None
    for k, weight in enumerate(weights):
        term = weight * pad_ref[first + k : first + k + rows, :]
        total = term if total is None else total + term
    return total


def tap_rows(ref, lanes):
    block = ref[:, lanes]
    return [block[k : k + 1] for k in range(block.shape[0])]


def silu_grad(pre):
    sg = sigmoid(pre)
    return sg * (1.0 + pre * (1.0 - sg))


def spread(row_a, row_b):
    half, rows = LANES // 2, row_a.shape[1]
    both = jnp.concatenate(
        [jnp.broadcast_to(row_a, (half, rows)), jnp.broadcast_to(row_b, (half, rows))], axis=0
    )
    return both.T


def column(row):
    return jnp.broadcast_to(row, (LANES, row.shape[1])).T


def running_sum(dec):
    rows = dec.shape[1]
    before = lax.broadcasted_iota(jnp.int32, (rows, rows), 0)
    after = lax.broadcasted_iota(jnp.int32, (rows, rows), 1)
    upper = (before <= after).astype(f32)
    return dot(jnp.log(dec), upper, HIGHEST)


def gain_of(dec):
    return jnp.sqrt((1.0 - dec) * (1.0 + dec))


def tail_of(cum):
    return jnp.exp(cum[:, -1:] - cum)


def put_padded(pad_ref, halo, block):
    pad_ref[0:HALO, :] = halo
    pad_ref[HALO : HALO + block.shape[0], :] = block.astype(f32)


def lane_blocks(width):
    return [slice(at, at + LANES) for at in range(0, width, LANES)]


def run_copies(copies):
    for copy in copies:
        copy.start()
    for copy in copies:
        copy.wait()


def early_load_kernel(count, *refs):
    place_ref, x_hbm, g_hbm = refs[:3]
    small = (len(refs) - 9) // 2
    sources, (xa, ga) = refs[3 : 3 + small], refs[3 + small : 5 + small]
    kept, (tails_ref, x16, bc16, sems) = refs[5 + small : -4], refs[-4:]
    bc_hbm = sources[2]
    rows, width = x_hbm.shape
    place = place_ref[0]
    chunk = pl.ds(0, xa.shape[1])
    last = pl.ds(rows - ROWS16, ROWS16)
    tails = [
        pltpu.make_async_copy(x_hbm.at[last, :], x16, sems.at[small + 2]),
        pltpu.make_async_copy(bc_hbm.at[last, :], bc16, sems.at[small + 3]),
    ]
    copies = [pltpu.make_async_copy(sources[i], kept[i], sems.at[i]) for i in range(small)]
    for copy in tails:
        copy.start()

    @pl.when(place == 0)
    def _():
        run_copies(copies + [pltpu.make_async_copy(x_hbm.at[:, chunk], xa, sems.at[small])])

    @pl.when(place == count - 1)
    def _():
        run_copies(copies + [pltpu.make_async_copy(g_hbm.at[:, chunk], ga, sems.at[small + 1])])

    for copy in tails:
        copy.wait()
    tails_ref[:, :width] = x16[...].astype(f32)[ROWS16 - HALO :].astype(bf16)
    tails_ref[:, width:] = bc16[...].astype(f32)[ROWS16 - HALO :].astype(bf16)


def load_kernel(*refs):
    count = (len(refs) - 2) // 2
    sources, kept, sems = refs[:count], refs[count + 1 : -1], refs[-1]
    run_copies(
        [pltpu.make_async_copy(sources[i], kept[i], sems.at[i]) for i in range(count)]
    )


def head_rows(ref, h):
    return ref[pl.ds(h, 1), :], ref[pl.ds(h + 1, 1), :]


def state_of(bc_rows, factors):
    over = (((0,), (0,)), ((), ()))
    return lax.dot_general(bc_rows, factors, over, preferred_element_type=f32)


def weighted_tails(start, heads_at, x_ref, wx_ref, halo, gt, pad, lw):
    rows, width = lw.shape
    for q, lanes in enumerate(lane_blocks(width)):
        full = slice(start + q * LANES, start + (q + 1) * LANES)
        one = pad.at[q]
        put_padded(one, halo(full), x_ref[:, full])
        pre = conv_rows(one, tap_rows(wx_ref, full), rows)
        inner = (pre * sigmoid(pre)).astype(bf16).astype(f32)
        factor = spread(*head_rows(gt, heads_at + 2 * q))
        lw[:, lanes] = (inner * factor).astype(bf16)


def led_gradients(start, heads_at, g_ref, sl, lg):
    for q, lanes in enumerate(lane_blocks(lg.shape[1])):
        full = slice(start + q * LANES, start + (q + 1) * LANES)
        lead = spread(*head_rows(sl, heads_at + 2 * q))
        lg[:, lanes] = (g_ref[:, full].astype(f32) * lead).astype(bf16)


def mapped_half(half, state, rows, bc_block, halo, wbc_ref, bcpad):
    lanes = slice(half * state, (half + 1) * state)
    put_padded(bcpad, halo, bc_block)
    pre = conv_rows(bcpad, tap_rows(wbc_ref, lanes), rows)
    return (pre * sigmoid(pre)).astype(bf16)


def put_first_rows(pay_ref, lg, bc_ref, more):
    state = pay_ref.shape[0] - MORE
    bcw = bc_ref.shape[1]
    more[0:4, :] = lg[0:ROWS16, :].astype(f32)[0:4]
    more[4:8, 0:bcw] = bc_ref[0:ROWS16, :].astype(f32)[0:4]
    more[4:8, bcw:] = jnp.zeros((4, lg.shape[1] - bcw), f32)
    pay_ref[state:, :] = more[...].astype(bf16)


def first_rows_state(more, bc_ref, wbc_ref, bcpad):
    rows, bcw = bc_ref.shape
    state = bcw // 2
    taps = wbc_ref.shape[0]
    zeros = jnp.zeros((ROWS16 - 4, state), f32)
    edge = bc_ref[rows - ROWS16 :, state:].astype(f32)[ROWS16 - HALO :]
    block = jnp.concatenate([more[4:8, state:bcw], zeros], axis=0)
    c = mapped_half(1, state, ROWS16, block, edge, wbc_ref, bcpad)
    early = lax.broadcasted_iota(jnp.int32, c.shape, 0) < taps - 1
    lg = jnp.concatenate([more[0:4, :], jnp.zeros((ROWS16 - 4, more.shape[1]), f32)], axis=0)
    return state_of(jnp.where(early, c, jnp.zeros_like(c)), lg.astype(bf16))


def bc_tail_place(r, taps, bcw):
    return 2 * taps - 2 + r // 2, slice((r % 2) * bcw, (r % 2 + 1) * bcw)


def first_state_kernel(count, scale, *refs):
    place_ref, dec_ref, xa_ref, ga_ref, wx_ref, bc_ref, wbc_ref, tails_ref = refs[:8]
    pay_ref, pad, gt, sl, lw, lg, bcpad, tails, more = refs[8:]
    rows, width = xa_ref.shape
    taps, bcw = wbc_ref.shape
    state = bcw // 2
    place = place_ref[0]
    none = jnp.zeros((HALO, LANES), f32)

    @pl.when(place == 0)
    def _():
        dec = dec_ref[...]
        gt[...] = gain_of(dec) * tail_of(running_sum(dec))
        b = mapped_half(0, state, rows, bc_ref[:, :state], none, wbc_ref, bcpad)
        weighted_tails(0, 0, xa_ref, wx_ref, lambda _: none, gt, pad, lw)
        pay_ref[0:state, :] = state_of(b, lw[...]).astype(bf16)
        tails[...] = tails_ref[...].astype(f32)
        more[0 : taps - 1, :] = tails[HALO - taps + 1 :, 0:width]
        more[taps - 1 : 2 * taps - 2, :] = tails[HALO - taps + 1 :, width : 2 * width]
        for r in range(taps - 1):
            at, here = bc_tail_place(r, taps, bcw)
            more[at : at + 1, here] = tails[HALO - taps + 1 + r :, 2 * width :][0:1]
        pay_ref[state:, :] = more[...].astype(bf16)

    @pl.when(place == count - 1)
    def _():
        sl[...] = scale * jnp.exp(running_sum(dec_ref[...]))
        c = mapped_half(1, state, rows, bc_ref[:, state:], none, wbc_ref, bcpad)
        late = lax.broadcasted_iota(jnp.int32, c.shape, 0) >= taps - 1
        led_gradients(0, 0, ga_ref, sl, lg)
        pay_ref[0:state, :] = state_of(jnp.where(late, c, jnp.zeros_like(c)), lg[...]).astype(bf16)
        put_first_rows(pay_ref, lg, bc_ref, more)


def middle_first_kernel(count, scale, *refs):
    place_ref, dec_ref, x_ref, g_ref, wx_ref, bc_ref, wbc_ref, _ = refs[:8]
    cum_ref, map_ref, u_ref, v_ref, tot_ref, gt16_ref, lg16_ref = refs[8:15]
    pad, gt, sl, lw, lg, bcpad = refs[15:]
    rows, bcw = bc_ref.shape
    state = bcw // 2
    none = jnp.zeros((HALO, LANES), f32)
    dec = dec_ref[...]
    cum = running_sum(dec)
    cum_ref[...] = cum
    for half in range(2):
        lanes = slice(half * state, (half + 1) * state)
        made = mapped_half(half, state, rows, bc_ref[:, lanes], none, wbc_ref, bcpad.at[half])
        map_ref[:, lanes] = made
    place = place_ref[0]

    @pl.when(jnp.logical_and(place > 0, place < count - 1))
    def _():
        gt[...] = gain_of(dec) * tail_of(cum)
        lead = jnp.exp(cum)
        sl[...] = scale * lead
        weighted_tails(0, 0, x_ref, wx_ref, lambda _: none, gt, pad, lw)
        led_gradients(0, 0, g_ref, sl, lg)
        lane_totals(lead, 0, tot_ref)
        for q, lanes in enumerate(lane_blocks(lw.shape[1])):
            half = LANES // 2
            a, b = (row[:, 0:LANES] for row in head_rows(gt, 2 * q))
            both = [jnp.broadcast_to(row, (half, LANES)) for row in (a, b)]
            gt16_ref[:, lanes] = jnp.concatenate(both, axis=0).T[0:ROWS16]
        lg16_ref[...] = lg[0:ROWS16, :]
        late = lax.broadcasted_iota(jnp.int32, (rows, state), 0) >= ROWS16
        zero = jnp.zeros((rows, state), bf16)
        u_ref[...] = state_of(jnp.where(late, map_ref[:, :state], zero), lw[...])
        v_ref[...] = state_of(jnp.where(late, map_ref[:, state:], zero), lg[...])


def fix_kernel(count, *refs):
    place_ref, halo_in, came_ref, x_ref, wx_ref, bc_ref, wbc_ref, map_in = refs[:8]
    u_in, v_in, tot_ref, gt16_ref, lg16_ref, _ = refs[8:14]
    halo_ref, map_ref, u_ref, v_ref, came_out, pay_ref, halo, more, pad, bcpad = refs[14:]
    rows, bcw = bc_ref.shape
    state = bcw // 2
    taps = wbc_ref.shape[0]
    width = u_in.shape[1]
    place = place_ref[0]
    more[...] = came_ref[state:, :].astype(f32)
    halo[...] = halo_in[...].astype(f32)

    @pl.when(place == 1)
    def _():
        halo[HALO - taps + 1 :, 0:width] = more[0 : taps - 1, :]
        halo[HALO - taps + 1 :, width : 2 * width] = more[taps - 1 : 2 * taps - 2, :]
        for r in range(taps - 1):
            at, here = bc_tail_place(r, taps, bcw)
            row = HALO - taps + 1 + r
            halo[row : row + 1, 2 * width :] = more[at : at + 1, here]

    halo_ref[...] = halo[...].astype(bf16)
    map_ref[...] = map_in[...]
    for half in range(2):
        lanes = slice(half * state, (half + 1) * state)
        edge = halo[:, 2 * width + half * state : 2 * width + (half + 1) * state]
        one = bcpad.at[half]
        made = mapped_half(half, state, ROWS16, bc_ref[0:ROWS16, lanes], edge, wbc_ref, one)
        map_ref[0:ROWS16, lanes] = made
    came_out[...] = came_ref[0:state, :]
    tot = tot_ref[0:1, :]

    @pl.when(jnp.logical_and(place > 0, place < count - 1))
    def _():
        lw16 = []
        for q, lanes in enumerate(lane_blocks(width)):
            one = pad.at[q]
            put_padded(one, halo[:, lanes], x_ref[0:ROWS16, lanes])
            pre = conv_rows(one, tap_rows(wx_ref, lanes), ROWS16)
            inner = (pre * sigmoid(pre)).astype(bf16).astype(f32)
            lw16.append((inner * gt16_ref[:, lanes]).astype(bf16))
        lw16 = jnp.concatenate(lw16, axis=1)
        u_ref[...] = u_in[...] + state_of(map_ref[0:ROWS16, :state], lw16)
        v_ref[...] = v_in[...] + state_of(map_ref[0:ROWS16, state:], lg16_ref[...])

    @pl.when(place == 1)
    def _():
        pay_ref[...] = (u_ref[...] + tot * came_ref[0:state, :].astype(f32)).astype(bf16)

    @pl.when(place == count - 2)
    def _():
        extra = first_rows_state(more, bc_ref, wbc_ref, bcpad.at[0])
        came = came_ref[0:state, :].astype(f32) + extra
        came_out[...] = came.astype(bf16)
        pay_ref[...] = (v_ref[...] + tot * came).astype(bf16)


def lane_totals(lead, heads_at, tot_ref):
    rows = lead.shape[1]
    for q, lanes in enumerate(lane_blocks(tot_ref.shape[1])):
        low = lax.broadcasted_iota(jnp.int32, (8, LANES), 1) < LANES // 2
        a, b = (lead[heads_at + 2 * q + i :, rows - 1 :][:1] for i in range(2))
        tot_ref[:, lanes] = jnp.where(low, a, b)


def middle_state_kernel(count, start, heads_at, scale, *refs):
    place_ref, dec_ref, x_ref, g_ref, halo_ref, wx_ref, cum_ref, map_ref, _ = refs[:9]
    u_ref, v_ref, tot_ref = refs[9:12]
    pad, gt, sl, lw, lg = refs[12:]
    state = map_ref.shape[1] // 2
    place = place_ref[0]

    @pl.when(jnp.logical_and(place > 0, place < count - 1))
    def _():
        cum = cum_ref[...]
        gt[...] = gain_of(dec_ref[...]) * tail_of(cum)
        lead = jnp.exp(cum)
        sl[...] = scale * lead

        def halo(full):
            return halo_ref[:, full].astype(f32)

        weighted_tails(start, heads_at, x_ref, wx_ref, halo, gt, pad, lw)
        led_gradients(start, heads_at, g_ref, sl, lg)
        lane_totals(lead, heads_at, tot_ref)
        u_ref[...] = state_of(map_ref[:, :state], lw[...])
        v_ref[...] = state_of(map_ref[:, state:], lg[...])


def end_state_kernel(count, start, heads_at, scale, *refs):
    place_ref, dec_ref, x_ref, g_ref, wx_ref, bc_ref, cum_ref, map_ref, _ = refs[:9]
    pay_ref, pad, gt, sl, lw, lg, more = refs[9:]
    state = map_ref.shape[1] // 2
    taps = wx_ref.shape[0]
    place = place_ref[0]

    @pl.when(place == 0)
    def _():
        gt[...] = gain_of(dec_ref[...]) * tail_of(cum_ref[...])
        none = jnp.zeros((HALO, LANES), f32)
        weighted_tails(start, heads_at, x_ref, wx_ref, lambda _: none, gt, pad, lw)
        pay_ref[0:state, :] = state_of(map_ref[:, :state], lw[...]).astype(bf16)

    @pl.when(place == count - 1)
    def _():
        sl[...] = scale * jnp.exp(cum_ref[...])
        led_gradients(start, heads_at, g_ref, sl, lg)
        c = map_ref[:, state:]
        late = lax.broadcasted_iota(jnp.int32, c.shape, 0) >= taps - 1
        pay_ref[0:state, :] = state_of(jnp.where(late, c, jnp.zeros_like(c)), lg[...]).astype(bf16)
        put_first_rows(pay_ref, lg, bc_ref, more)


def message_kernel(hop, place_ref, u_ref, v_ref, tot_ref, came_ref, _, out_ref):
    own = jnp.where(place_ref[0] == hop, u_ref[...], v_ref[...])
    out_ref[...] = (own + tot_ref[0:1, :] * came_ref[...].astype(f32)).astype(bf16)


def fix_message_kernel(count, *refs):
    place_ref, u_ref, v_ref, tot_ref, came_ref, bc_ref, wbc_ref, _ = refs[:8]
    came_out, out_ref, more, bcpad = refs[8:]
    state = u_ref.shape[0]
    place = place_ref[0]
    tot = tot_ref[0:1, :]
    came_out[...] = came_ref[0:state, :]

    @pl.when(place == 1)
    def _():
        out_ref[...] = (u_ref[...] + tot * came_ref[0:state, :].astype(f32)).astype(bf16)

    @pl.when(place == count - 2)
    def _():
        more[...] = came_ref[state:, :].astype(f32)
        extra = first_rows_state(more, bc_ref, wbc_ref, bcpad)
        came = came_ref[0:state, :].astype(f32) + extra
        came_out[...] = came.astype(bf16)
        out_ref[...] = (v_ref[...] + tot * came).astype(bf16)


def edge_kernel(count, spans, parts, *refs):
    hops = count - 2
    place_ref, map_ref = refs[:2]
    blocks, refs = refs[3 : 3 + 2 * parts], refs[3 + 2 * parts :]
    came, (out_ref, edge) = refs[: 2 * hops], refs[2 * hops :]
    state = map_ref.shape[1] // 2
    b = map_ref[0:ROWS16, :state]
    per = len(spans) // 2
    for c in range(2):
        wanted = came[c * hops : (c + 1) * hops]
        grad = pick(place_ref[0], wanted, lambda hop: count - 2 - hop, state)
        extra = dot(b, grad)
        for q in range(per):
            part, lanes = spans[c * per + q]
            dx_ref, q_ref = blocks[2 * part : 2 * part + 2]
            here = slice(q * LANES, (q + 1) * LANES)
            rows = dx_ref[0:ROWS16, lanes] + q_ref[0:ROWS16, lanes].astype(f32) * extra[:, here]
            edge[4 * c : 4 * c + 4, here] = rows[0:4]
    out_ref[...] = edge[...].astype(bf16)


def intra_kernel(first, start, pairs, head_dim, scale, *refs):
    x_ref, g_ref, halo_ref, wx_ref, dec_ref, cum_ref, map_ref, skip_ref, _ = refs[:9]
    refs = refs[9:]
    if not first:
        dsim_in, gs_in = refs[:2]
        refs = refs[2:]
    y0_ref, dx_ref, q_ref, ls_ref, lw_ref, lg_ref, dsim_ref, gs_ref = refs[:8]
    pad, sim, gain = refs[8:]
    rows = x_ref.shape[0]
    state = map_ref.shape[1] // 2
    half = rows // 2
    gain[...] = gain_of(dec_ref[...])
    sim[...] = dot_nt(map_ref[:, state:], map_ref[:, :state])
    if first:
        dsim_ref[...] = jnp.zeros(dsim_ref.shape, f32)
        gs_ref[...] = jnp.zeros(gs_ref.shape, f32)
    else:
        dsim_ref[...] = dsim_in[...]
        gs_ref[...] = gs_in[...]
    lane = lax.broadcasted_iota(jnp.int32, (1, LANES), 1)
    low = lane < head_dim
    r_i = lax.broadcasted_iota(jnp.int32, (half, half), 0)
    c_i = lax.broadcasted_iota(jnp.int32, (half, half), 1)
    lower = r_i >= c_i

    def pair(q):
        lanes = slice(q * LANES, (q + 1) * LANES)
        full = slice(start + q * LANES, start + (q + 1) * LANES)
        h = start // head_dim + 2 * q
        one = pad.at[q]
        put_padded(one, halo_ref[:, full].astype(f32), x_ref[:, full])
        pre = conv_rows(one, tap_rows(wx_ref, full), rows)
        sg = sigmoid(pre)
        inner = (pre * sg).astype(bf16).astype(f32)
        sgrad = sg * (1.0 + pre * (1.0 - sg))
        gn = spread(*head_rows(gain, h))
        cums = head_rows(cum_ref, h)
        cols = [column(row) for row in cums]
        both = jnp.where(low, cols[0], cols[1])
        tl = jnp.exp(both[rows - 1 :] - both)
        ls = scale * jnp.exp(both)
        w = (inner * gn).astype(bf16)
        g = g_ref[:, full]
        gf = g.astype(f32)
        g_t = gf.T.astype(bf16)
        y = ds = None
        dw_t = []
        for a in range(2):
            row, col = cums[a], cols[a]
            keep = low if a == 0 else jnp.logical_not(low)
            d00 = jnp.exp(jnp.where(lower, col[:half] - row[:, :half], NEG))
            d10 = jnp.exp(col[half:] - row[:, :half])
            d11 = jnp.exp(jnp.where(lower, col[half:] - row[:, half:], NEG))
            m00 = (d00 * sim[0:half, 0:half]).astype(bf16)
            m10 = (d10 * sim[half:rows, 0:half]).astype(bf16)
            m11 = (d11 * sim[half:rows, half:rows]).astype(bf16)
            w_a = jnp.where(keep, w, jnp.zeros_like(w))
            top = dot(m00, w_a[:half])
            bot = dot(jnp.concatenate([m10, m11], axis=1), w_a)
            y_a = jnp.concatenate([top, bot], axis=0)
            y = y_a if y is None else y + y_a
            g_at = g_t[a * head_dim : (a + 1) * head_dim]
            left = dot(g_at, jnp.concatenate([m00, m10], axis=0))
            right = dot(g_at[:, half:], m11)
            dw_t.append(jnp.concatenate([left, right], axis=1))
            mix_top = dot_nt(g[:half], w_a[:half])
            mix_bot = dot_nt(g[half:], w_a)
            now = (d00 * mix_top, d10 * mix_bot[:, :half], d11 * mix_bot[:, half:])
            ds = now if ds is None else [one + two for one, two in zip(ds, now)]
        dsim_ref[0:half, 0:half] += ds[0]
        dsim_ref[half:rows, 0:half] += ds[1]
        dsim_ref[half:rows, half:rows] += ds[2]
        dw = scale * jnp.concatenate(dw_t, axis=0).T
        skip = jnp.where(low, skip_ref[:, h : h + 1], skip_ref[:, h + 1 : h + 2])
        y0_ref[:, lanes] = scale * y + skip * inner
        dx_ref[:, lanes] = (gn * dw + skip * gf) * sgrad
        q_ref[:, lanes] = (gn * tl * sgrad).astype(bf16)
        ls_ref[:, lanes] = ls.astype(bf16)
        lw_ref[:, lanes] = (inner * gn * tl).astype(bf16)
        lg_ref[:, lanes] = (gf * ls).astype(bf16)
        gi = jnp.sum(gf * inner, axis=0, keepdims=True)
        sum_a = jnp.sum(jnp.where(low, gi, 0.0), axis=1, keepdims=True)
        sum_b = jnp.sum(jnp.where(low, 0.0, gi), axis=1, keepdims=True)
        gs_ref[...] += jnp.where(lane == h, sum_a, 0.0) + jnp.where(lane == h + 1, sum_b, 0.0)

    for q in range(pairs):
        pair(q)


def pick(place, parts, wanted, state):
    total = jnp.zeros((state, parts[0].shape[1]), bf16)
    for hop, ref in enumerate(parts):
        total = jnp.where(place == wanted(hop), ref[0:state, :], total)
    return total


def add_states(spans, blocks, which, states, total):
    done = 0
    while done < len(spans):
        part, lanes = spans[done]
        size = 1
        while done + size < len(spans) and spans[done + size][0] == part:
            size += 1
        mine = slice(lanes.start, lanes.start + size * LANES)
        here = slice(done * LANES, (done + size) * LANES)
        made = dot_nt(blocks[2 * part + which][:, mine], states[:, here])
        total = made if total is None else total + made
        done += size
    return total


def before_silu(half, total, bc_ref, halo_ref, wbc_ref, bcpad):
    rows, bcw = bc_ref.shape
    state = bcw // 2
    taps = wbc_ref.shape[0]
    inner = halo_ref.shape[1] - bcw
    lanes = slice(half * state, (half + 1) * state)
    edge = halo_ref[:, inner + half * state : inner + (half + 1) * state].astype(f32)
    put_padded(bcpad, edge, bc_ref[:, lanes])
    dpre = total * silu_grad(conv_rows(bcpad, tap_rows(wbc_ref, lanes), rows))
    sums = []
    for k in range(taps):
        moved = bcpad[HALO - taps + 1 + k : HALO - taps + 1 + k + rows, :]
        sums.append(jnp.sum(dpre * moved, axis=0, keepdims=True))
    return dpre, jnp.concatenate(sums + [jnp.zeros((8 - taps, state), f32)], axis=0)


def finish_bc_kernel(count, first, spans, parts, scale, *refs):
    hops = count - 1
    place_ref, map_ref, sum_in = refs[:3]
    blocks, refs = refs[4 : 4 + 2 * parts], refs[4 + 2 * parts :]
    came, refs = refs[:hops], refs[hops:]
    bcw = map_ref.shape[1]
    state = bcw // 2
    place = place_ref[0]
    enter = pick(place, came, lambda hop: hop + 1, state)
    grad = pick(place, came, lambda hop: count - 2 - hop, state)
    if first:
        ds = scale * sum_in[...]
        high = ds.astype(bf16)
        rest = (ds - high.astype(f32)).astype(bf16)
        ds_t = ds.T
        high_t = ds_t.astype(bf16)
        rest_t = (ds_t - high_t.astype(f32)).astype(bf16)
        b, c = map_ref[:, :state], map_ref[:, state:]
        d_b = dot(high_t, c) + dot(rest_t, c)
        d_c = dot(high, b) + dot(rest, b)
    else:
        d_b, d_c = sum_in[:, :state], sum_in[:, state:]
    d_b = add_states(spans, blocks, 0, grad, d_b)
    d_c = add_states(spans, blocks, 1, enter, d_c)
    if first:
        (dbc_ref,) = refs
        dbc_ref[:, :state] = d_b
        dbc_ref[:, state:] = d_c
        return
    bc_ref, halo_ref, wbc_ref, gs_ref, own_ref, small_ref, bcpad = refs
    for half in range(2):
        lanes = slice(half * state, (half + 1) * state)
        made = before_silu(half, (d_b, d_c)[half], bc_ref, halo_ref, wbc_ref, bcpad.at[half])
        own_ref[:, lanes], small_ref[:, lanes] = made
    small_ref[:, bcw:] = gs_ref[...]


def finish_kernel(count, start, spans, parts, pieces, *refs):
    hops = count - 1
    place_ref, x_ref, wx_ref, map_ref = refs[:4]
    blocks, refs = refs[5 : 5 + 4 * parts], refs[5 + 4 * parts :]
    came, refs = refs[:hops], refs[hops:]
    y_hbm, gx_hbm, taps_ref, end_ref, enter, grad, pad, y_ref, gx_ref, sems = refs
    rows = x_ref.shape[0]
    taps = wx_ref.shape[0]
    state = enter.shape[0]
    place = place_ref[0]
    b, c = map_ref[:, :state], map_ref[:, state:]
    enter[...] = pick(place, came, lambda hop: hop + 1, state)
    grad[...] = pick(place, came, lambda hop: count - 2 - hop, state)
    copies = []
    first = 0
    for number, size in enumerate(pieces):
        for q in range(first, first + size):
            part, mine = spans[q]
            y0_ref, dx_ref, q_ref, ls_ref = blocks[4 * part : 4 * part + 4]
            lanes = slice(q * LANES, (q + 1) * LANES)
            full = slice(start + q * LANES, start + (q + 1) * LANES)
            inter = dot(c, enter[:, lanes])
            y_ref[:, lanes] = (y0_ref[:, mine] + ls_ref[:, mine].astype(f32) * inter).astype(bf16)
            one = pad.at[q]
            inter = dot(b, grad[:, lanes])
            one[0:rows, :] = dx_ref[:, mine] + q_ref[:, mine].astype(f32) * inter
            one[rows : rows + HALO, :] = jnp.zeros((HALO, LANES), f32)
            x = x_ref[:, full].astype(f32)
            total = None
            sums = []
            for k, weight in enumerate(tap_rows(wx_ref, full)):
                shifted = one[taps - 1 - k : taps - 1 - k + rows, :]
                term = weight * shifted
                total = term if total is None else total + term
                sums.append(jnp.sum(shifted * x, axis=0, keepdims=True))
            gx_ref[:, lanes] = total.astype(bf16)
            end_ref[:, lanes] = total[rows - ROWS16 :]
            sums = jnp.concatenate(sums + [jnp.zeros((8 - taps, LANES), f32)], axis=0)
            taps_ref[:, lanes] = sums
        lanes = slice(first * LANES, (first + size) * LANES)
        full = slice(start + first * LANES, start + (first + size) * LANES)
        for i, (made, out) in enumerate(((y_ref, y_hbm), (gx_ref, gx_hbm))):
            copy = pltpu.make_async_copy(made.at[:, lanes], out.at[:, full], sems.at[number, i])
            copy.start()
            copies.append(copy)
        first += size
    for copy in copies:
        copy.wait()


def finish_grad_kernel(count, start, spans, parts, *refs):
    hops = count - 1
    place_ref, x_ref, wx_ref, map_ref = refs[:4]
    blocks, refs = refs[5 : 5 + 2 * parts], refs[5 + 2 * parts :]
    came, (gx_ref, taps_ref, end_ref, grad, pad) = refs[:hops], refs[hops:]
    rows = x_ref.shape[0]
    taps = wx_ref.shape[0]
    state = grad.shape[0]
    b = map_ref[:, :state]
    grad[...] = pick(place_ref[0], came, lambda hop: count - 2 - hop, state)
    for q, (part, mine) in enumerate(spans):
        dx_ref, q_ref = blocks[2 * part : 2 * part + 2]
        lanes = slice(q * LANES, (q + 1) * LANES)
        full = slice(start + q * LANES, start + (q + 1) * LANES)
        one = pad.at[q]
        inter = dot(b, grad[:, lanes])
        one[0:rows, :] = dx_ref[:, mine] + q_ref[:, mine].astype(f32) * inter
        one[rows : rows + HALO, :] = jnp.zeros((HALO, LANES), f32)
        x = x_ref[:, full].astype(f32)
        total = None
        sums = []
        for k, weight in enumerate(tap_rows(wx_ref, full)):
            shifted = one[taps - 1 - k : taps - 1 - k + rows, :]
            term = weight * shifted
            total = term if total is None else total + term
            sums.append(jnp.sum(shifted * x, axis=0, keepdims=True))
        gx_ref[:, lanes] = total.astype(bf16)
        end_ref[:, lanes] = total[rows - ROWS16 :]
        sums = jnp.concatenate(sums + [jnp.zeros((8 - taps, LANES), f32)], axis=0)
        taps_ref[:, lanes] = sums


def sums_kernel(halo_ref, edge_ref, taps_a, taps_b, sums_ref, halo):
    taps, width = 4, taps_a.shape[1]
    edge = edge_ref[...].astype(f32)
    halo[...] = halo_ref[:, 0 : 2 * width].astype(f32)
    for c, own in enumerate((taps_a, taps_b)):
        lanes = slice(c * width, (c + 1) * width)
        sums_ref[:, lanes] = own[...]
        for k in range(taps - 1):
            added = None
            for j in range(taps - 1 - k):
                at = HALO - taps + 1 + k + j
                term = edge[4 * c + j : 4 * c + j + 1] * halo[at : at + 1, lanes]
                added = term if added is None else added + term
            sums_ref[k : k + 1, lanes] += added


def write_kernel(count, start, spans, parts, *refs):
    hops = count - 1
    place_ref, map_ref, wx_ref, edge_ref, end_a, end_b, gx_b = refs[:7]
    blocks, refs = refs[8 : 8 + 2 * parts], refs[8 + 2 * parts :]
    came, refs = refs[:hops], refs[hops + 2 :]
    y_hbm, gx_hbm, enter, y_b, gx16, sems = refs
    taps = wx_ref.shape[0]
    rows, width = gx_b.shape
    state = enter.shape[0]
    chunk = pl.ds(start, width)
    body = pl.ds(0, rows - ROWS16)
    tail = pl.ds(rows - ROWS16, ROWS16)
    copies = [pltpu.make_async_copy(gx_b.at[body, :], gx_hbm.at[body, chunk], sems.at[0])]
    copies[0].start()
    edge = edge_ref[...].astype(f32)
    row = lax.broadcasted_iota(jnp.int32, (ROWS16, width), 0)
    for c, end_ref in enumerate((end_a, end_b)):
        lanes = slice(c * width, (c + 1) * width)
        end = end_ref[...]
        for k in range(taps - 1):
            for j in range(taps - 1 - k):
                at = ROWS16 - (taps - 1 - k) + j
                here = wx_ref[k : k + 1, lanes] * edge[4 * c + j : 4 * c + j + 1]
                end = end + jnp.where(row == at, here, 0.0)
        gx16[:, lanes] = end.astype(bf16)
    copies.append(pltpu.make_async_copy(gx16, gx_hbm.at[tail, :], sems.at[1]))
    copies[1].start()
    c = map_ref[:, state:]
    enter[...] = pick(place_ref[0], came, lambda hop: hop + 1, state)
    for q, (part, mine) in enumerate(spans):
        y0_ref, ls_ref = blocks[2 * part : 2 * part + 2]
        lanes = slice(q * LANES, (q + 1) * LANES)
        inter = dot(c, enter[:, lanes])
        y_b[:, lanes] = (y0_ref[:, mine] + ls_ref[:, mine].astype(f32) * inter).astype(bf16)
    copies.append(pltpu.make_async_copy(y_b, y_hbm.at[:, chunk], sems.at[2]))
    copies[2].start()
    for copy in copies:
        copy.wait()


def pack_kernel(own_ref, small_ref, small_dp, _, small_out, head_ref):
    rows, bcw = own_ref.shape
    small = small_ref[...] + small_dp[...]
    small_out[...] = small
    head_ref[0:rows, :] = own_ref[...].astype(bf16)
    sums = small[:, :bcw]
    head_ref[rows:, :] = jnp.concatenate([sums, jnp.zeros_like(sums)], axis=0).astype(bf16)


def merge_kernel(heads, *refs):
    sums_ref, sums_dp, small_ref, own_ref = refs[:4]
    others, (full_ref, out_ref, send_ref) = refs[4 : 3 + heads], refs[3 + heads :]
    rows, bc = own_ref.shape
    total = sums_ref[...] + sums_dp[...]
    half = total.shape[1] // 2
    full = own_ref[...]
    taps_bc = small_ref[:, :bc]
    for other in others:
        block = other[...].astype(f32)
        full = full + block[:rows]
        taps_bc = taps_bc + block[rows : rows + 8]
    full_ref[...] = full
    send_ref[0:4, 0:half] = total[0:4, :half]
    send_ref[4:8, 0:half] = total[0:4, half:]
    send_ref[0:4, half : half + bc] = taps_bc[0:4]
    send_ref[4:8, half : half + bc] = full[0:4]
    send_ref[:, half + bc :] = small_ref[:, bc:]
    out_ref[...] = send_ref[...].astype(bf16)


def conv_bc_kernel(full_ref, wbc_ref, _, out_ref, pad):
    taps = wbc_ref.shape[0]
    rows, bcw = full_ref.shape
    for half in range(2):
        lanes = slice(half * bcw // 2, (half + 1) * bcw // 2)
        one = pad.at[half]
        one[0:rows, :] = full_ref[:, lanes]
        one[rows:, :] = jnp.zeros((HALO, bcw // 2), f32)
        out = None
        for k, weight in enumerate(tap_rows(wbc_ref, lanes)):
            term = weight * one[taps - 1 - k : taps - 1 - k + rows, :]
            out = term if out is None else out + term
        out_ref[:, lanes] = out


def last_kernel(count, norm_tokens, norm_skip, *refs):
    place_ref, sums_ref, conv_ref, wbc_ref = refs[:4]
    parts = refs[4 : 3 + count]
    gbc_ref, tx_ref, tbc_ref, skip_ref = refs[3 + count :]
    taps, bc = wbc_ref.shape
    rows = conv_ref.shape[0]
    half = tx_ref.shape[1] // 2
    total = sums_ref[...].astype(f32)
    edge = jnp.zeros((4, bc), f32)
    for hop, ref in enumerate(parts):
        block = ref[...].astype(f32)
        total = total + block
        if hop == count - 2:
            edge = jnp.where(place_ref[0] < count - 1, block[4:8, half : half + bc], 0.0)
    tx_ref[:, :half] = total[0:taps, 0:half] * norm_tokens
    tx_ref[:, half:] = total[4 : 4 + taps, 0:half] * norm_tokens
    tbc_ref[...] = total[0:taps, half : half + bc] * norm_tokens
    skip_ref[...] = total[0:1, half + bc : half + bc + skip_ref.shape[1]] * norm_skip
    gbc_ref[0 : rows - ROWS16, :] = conv_ref[0 : rows - ROWS16, :].astype(bf16)
    row = lax.broadcasted_iota(jnp.int32, (ROWS16, bc), 0)
    end = conv_ref[rows - ROWS16 :, :]
    for k in range(taps - 1):
        for j in range(taps - 1 - k):
            at = ROWS16 - (taps - 1 - k) + j
            end = end + jnp.where(row == at, wbc_ref[k : k + 1, :] * edge[j : j + 1], 0.0)
    gbc_ref[rows - ROWS16 :, :] = end.astype(bf16)


COST_US = {"middle_state": 1.5, "inside_block": 2.7, "sums": 0.8, "write": 0.8}
BYTES_PER_US = 3_500_000


def call(kernel, name, ins, outs, scratch=(), grid=(1,), kept=()):
    def spec(item):
        if not isinstance(item, tuple):
            whole = item.shape
            return pl.BlockSpec(whole, lambda *_: (0,) * len(whole))
        if item[1] == "smem":
            return pl.BlockSpec(memory_space=pltpu.SMEM)
        if item[1] == "any":
            return pl.BlockSpec(memory_space=pl.ANY)
        if item[1] == "hbm":
            return pl.BlockSpec(memory_space=pltpu.HBM)
        return pl.BlockSpec(item[1], item[2])

    def array(item):
        return item[0] if isinstance(item, tuple) else item

    return pl.pallas_call(
        kernel,
        grid=grid,
        in_specs=[spec(i) for i in ins],
        out_specs=[spec(o) for o in outs],
        out_shape=[array(o) for o in outs],
        scratch_shapes=list(scratch),
        compiler_params=pltpu.CompilerParams(vmem_limit_bytes=VMEM_LIMIT),
        cost_estimate=pl.CostEstimate(
            flops=0, bytes_accessed=int(COST_US.get(name, 0.01) * BYTES_PER_US), transcendentals=0
        ),
        input_output_aliases=dict(kept),
        name=name,
    )(*[array(i) for i in ins])


def chain_routes(count, hop):
    return [(hop, hop + 1), (count - 1 - hop, count - 2 - hop)]


def shape(s, d=f32):
    return jax.ShapeDtypeStruct(s, d)


def local(x_input, bc_input, decays, conv_x, conv_bc, skip_gain, grad_out):
    x, bc, dec, g = x_input[0], bc_input[0], decays[0], grad_out[0]
    rows, inner = x.shape
    taps = conv_x.shape[0]
    heads = dec.shape[0]
    head_dim = inner // heads
    bcw = bc.shape[1]
    state = bcw // 2
    scale = state ** (-0.5)
    count = lax.axis_size("seq")
    head_count = lax.axis_size("head")
    dp_count = lax.axis_size("dp")
    assert rows == BLOCK_LEN and 2 * head_dim == LANES and taps == 4
    assert count % 2 == 0 and count > 2 and dp_count == 2
    width = inner // 2
    chunks = (0, 1)
    block = 640 if width % 640 == 0 else LANES
    per = width // block
    pairs = width // LANES
    split = (pairs // 2 + pairs // 10, pairs + pairs // 10)
    split += (2 * pairs - sum(split),)
    spans = [
        (part, slice(at * LANES, (at + 1) * LANES))
        for part, size in enumerate(split)
        for at in range(size)
    ]
    place = lax.axis_index("seq").astype(jnp.int32).reshape(1)
    where_am_i = (place, "smem")

    def vmem(s, d=f32):
        return pltpu.VMEM(s, d)

    def in_hbm(a):
        return (pltpu.with_memory_space_constraint(a, pltpu.HBM), "hbm")

    def padded(blocks, length=rows):
        return vmem((blocks, length + HALO, LANES))

    state_scratch = [
        padded(pairs),
        vmem((heads, rows)),
        vmem((heads, rows)),
        vmem((rows, width), bf16),
        vmem((rows, width), bf16),
    ]
    received = [[], []]

    def hop_on(c, message):
        routes = chain_routes(count, len(received[c]))
        received[c].append(lax.ppermute(message, "seq", routes))

    skip = skip_gain.reshape(1, heads)
    sources = [dec, conv_x, bc, conv_bc]
    xa, ga, *made, tails = call(
        functools.partial(early_load_kernel, count),
        "early_load",
        [where_am_i, in_hbm(x), in_hbm(g)] + [in_hbm(a) for a in sources],
        [shape((rows, width), bf16), shape((rows, width), bf16)]
        + [shape(a.shape, a.dtype) for a in sources]
        + [shape((HALO, inner + bcw), bf16)],
        [
            vmem((ROWS16, inner), bf16),
            vmem((ROWS16, bcw), bf16),
            pltpu.SemaphoreType.DMA((len(sources) + 4,)),
        ],
    )
    pay = call(
        functools.partial(first_state_kernel, count, scale),
        "first_state",
        [where_am_i, made[0], xa, ga, *made[1:], tails],
        [shape((state + MORE, width), bf16)],
        state_scratch
        + [vmem((rows + HALO, LANES)), vmem((HALO, inner + bcw)), vmem((MORE, width))],
    )[0]
    hop_on(0, pay)
    sources = [x, bc, g, dec, conv_x, conv_bc, skip]
    x, bc, g, dec, conv_x, conv_bc, skip = call(
        load_kernel,
        "load",
        [in_hbm(a) for a in sources] + [(pay, "any")],
        [shape(a.shape, a.dtype) for a in sources],
        [pltpu.SemaphoreType.DMA((len(sources),))],
    )
    halo = lax.ppermute(tails, "seq", [(i, i + 1) for i in range(1, count - 1)])

    states = [None, None]

    def middle_state(c, after):
        start = c * width
        states[c] = call(
            functools.partial(middle_state_kernel, count, start, start // head_dim, scale),
            "middle_state",
            [where_am_i, dec, x, g, halo, conv_x, cum, mapped, (after, "any")],
            [shape((state, width)), shape((state, width)), shape((8, width))],
            state_scratch,
        )
        return states[c][0]

    def message(c, after):
        return call(
            functools.partial(message_kernel, len(received[c])),
            "message",
            [where_am_i, *states[c], received[c][-1], (after, "any")],
            [shape((state, width), bf16)],
        )[0]

    parts = []
    carried = []

    def inside(number, after):
        first = number == 0
        start = sum(split[:number]) * LANES
        span = split[number] * LANES
        ins = [x, g, halo, conv_x, dec, cum, mapped, skip, (after, "any")]
        if not first:
            ins += carried
        made = call(
            functools.partial(intra_kernel, first, start, split[number], head_dim, scale),
            "inside_block",
            ins,
            [
                shape((rows, span)),
                shape((rows, span)),
                shape((rows, span), bf16),
                shape((rows, span), bf16),
                shape((rows, span), bf16),
                shape((rows, span), bf16),
                shape((rows, rows)),
                shape((8, LANES)),
            ],
            [padded(split[number]), vmem((rows, rows)), vmem((heads, rows))],
        )
        parts.append(made[:6])
        carried[:] = made[6:8]
        return made[0]

    def chunk_parts(c):
        mine = spans[c * pairs : (c + 1) * pairs]
        used = sorted({part for part, _ in mine})
        return [(used.index(part), at) for part, at in mine], [parts[p] for p in used]

    cum, mapped, u, v, tot, gt16, lg16 = call(
        functools.partial(middle_first_kernel, count, scale),
        "middle_first",
        [where_am_i, dec, x, g, conv_x, bc, conv_bc, (tails, "any")],
        [
            shape((heads, rows)),
            shape((rows, bcw), bf16),
            shape((state, width)),
            shape((state, width)),
            shape((8, width)),
            shape((ROWS16, width)),
            shape((ROWS16, width), bf16),
        ],
        state_scratch + [padded(2)],
    )
    after = call(
        functools.partial(end_state_kernel, count, width, width // head_dim, scale),
        "end_state",
        [where_am_i, dec, x, g, conv_x, bc, cum, mapped, (u, "any")],
        [shape((state + MORE, width), bf16)],
        state_scratch + [vmem((MORE, width))],
    )[0]
    hop_on(1, after)
    halo, mapped, u, v, came, after = call(
        functools.partial(fix_kernel, count),
        "fix_first_rows",
        [where_am_i, halo, received[0][0], x, conv_x, bc, conv_bc, mapped]
        + [u, v, tot, gt16, lg16, (after, "any")],
        [
            shape((HALO, inner + bcw), bf16),
            shape((rows, bcw), bf16),
            shape((state, width)),
            shape((state, width)),
            shape((state, width), bf16),
            shape((state, width), bf16),
        ],
        [
            vmem((HALO, inner + bcw)),
            vmem((MORE, width)),
            padded(pairs, ROWS16),
            padded(2, ROWS16),
        ],
    )
    states[0] = (u, v, tot)
    received[0][0] = came
    hop_on(0, after)
    after = middle_state(1, after)
    after = inside(0, after)
    for hop in range(1, count - 1):
        for c in chunks:
            if hop > 1:
                after = message(c, after)
                hop_on(c, after)
            elif c:
                came, after = call(
                    functools.partial(fix_message_kernel, count),
                    "message",
                    [where_am_i, *states[1], received[1][0], bc, conv_bc, (after, "any")],
                    [shape((state, width), bf16), shape((state, width), bf16)],
                    [vmem((MORE, width)), vmem((ROWS16 + HALO, LANES))],
                )
                received[1][0] = came
                hop_on(1, after)
            if hop == count - 2:
                after = inside(1 + c, after)
    dsim, gsum = carried
    ins = [where_am_i, mapped, (after, "any")]
    for made in parts:
        ins += made[1:3]
    edge = call(
        functools.partial(edge_kernel, count, spans, len(parts)),
        "edge",
        ins + received[0][: count - 2] + received[1][: count - 2],
        [shape((8, width), bf16)],
        [vmem((8, width))],
    )[0]

    edges = lax.ppermute(edge, "seq", [(i + 1, i) for i in range(count - 1)])

    def finish_bc(c, base, after):
        where, used = chunk_parts(c)
        ins = [where_am_i, mapped, base, (after, "any")]
        for made in used:
            ins += made[4:6]
        ins += received[c]
        outs = [shape((rows, bcw))]
        scratch = []
        if c:
            ins += [bc, halo, conv_bc, gsum]
            outs += [shape((8, bcw + LANES))]
            scratch = [padded(2)]
        kernel = functools.partial(finish_bc_kernel, count, c == 0, where, len(used), scale)
        return call(kernel, "finish_bc", ins, outs, scratch)

    def finish(c, after):
        start = c * width
        where, used = chunk_parts(c)
        pieces = (4, 4, 2) if pairs == 10 else (pairs - 1, 1)
        ins = [where_am_i, x, conv_x, mapped, (after, "any")]
        for made in used:
            ins += made[:4]
        ins += received[c]
        made = call(
            functools.partial(finish_kernel, count, start, where, len(used), pieces),
            "finish",
            ins,
            [(shape((rows, inner), bf16), "hbm"), (shape((rows, inner), bf16), "hbm")]
            + [shape((8, width)), shape((ROWS16, width))],
            [
                vmem((state, width), bf16),
                vmem((state, width), bf16),
                padded(pairs),
                vmem((rows, width), bf16),
                vmem((rows, width), bf16),
                pltpu.SemaphoreType.DMA((len(pieces), 2)),
            ],
        )
        return made[:2], made[2], made[3]

    outs, taps_a, end_a = finish(0, edge)
    dbc = finish_bc(0, dsim, taps_a)[0]
    own, small = finish_bc(1, dbc, dbc)

    swap = [(0, 1), (1, 0)]
    turns = [[(i, (i + k) % head_count) for i in range(head_count)] for k in range(1, head_count)]
    small, to_heads = call(
        pack_kernel,
        "pack",
        [own, small, lax.ppermute(small, "dp", swap), (edges, "any")],
        [shape(small.shape), shape((rows + ROWS16, bcw), bf16)],
    )
    others = [lax.ppermute(to_heads, "head", turn) for turn in turns]

    where, used = chunk_parts(1)
    ins = [where_am_i, x, conv_x, mapped, (to_heads, "any")]
    for made in used:
        ins += made[1:3]
    gx_b, taps_b, end_b = call(
        functools.partial(finish_grad_kernel, count, width, where, len(used)),
        "finish_grad",
        ins + received[1],
        [shape((rows, width), bf16), shape((8, width)), shape((ROWS16, width))],
        [vmem((state, width), bf16), padded(pairs)],
    )
    sums = call(
        sums_kernel,
        "sums",
        [halo, edge, taps_a, taps_b],
        [shape((8, inner))],
        [vmem((HALO, inner))],
    )[0]
    sums_dp = lax.ppermute(sums, "dp", swap)
    send_width = inner // 2 + bcw + LANES
    full, to_seq = call(
        functools.partial(merge_kernel, head_count),
        "merge",
        [sums, sums_dp, small, own] + others,
        [shape((rows, bcw)), shape((8, send_width), bf16)],
        [vmem((8, send_width))],
    )
    ins = [where_am_i, mapped, conv_x, edges, end_a, end_b, gx_b, (to_seq, "any")]
    for made in used:
        ins += [made[0], made[3]]
    ins += received[1]
    y, gx = call(
        functools.partial(write_kernel, count, width, where, len(used)),
        "write",
        ins + [(outs[0], "hbm"), (outs[1], "hbm")],
        [(shape((rows, inner), bf16), "hbm"), (shape((rows, inner), bf16), "hbm")],
        [
            vmem((state, width), bf16),
            vmem((rows, width), bf16),
            vmem((ROWS16, inner), bf16),
            pltpu.SemaphoreType.DMA((3,)),
        ],
        kept=((len(ins), 0), (len(ins) + 1, 1)),
    )
    from_seq = [
        lax.ppermute(to_seq, "seq", [(i, (i + k) % count) for i in range(count)])
        for k in range(1, count)
    ]
    token_count = rows * count * dp_count
    norm_tokens = float(token_count) ** (-0.5)
    norm_skip = float(token_count * head_dim) ** (-0.5)
    conv = call(
        conv_bc_kernel,
        "conv_bc",
        [full, conv_bc, (to_seq, "any")],
        [shape((rows, bcw))],
        [padded(2)],
    )[0]
    gbc, tx, tbc, skip = call(
        functools.partial(last_kernel, count, norm_tokens, norm_skip),
        "last",
        [where_am_i, to_seq, conv, conv_bc] + from_seq,
        [
            shape((rows, bcw), bf16),
            shape((taps, inner)),
            shape((taps, bcw)),
            shape((1, heads)),
        ],
    )
    return y[None], gx[None], gbc[None], tx, tbc, skip.reshape(heads)


def solution(mesh):
    return jax.shard_map(
        local,
        mesh=mesh,
        in_specs=(
            P(("groups", "dp"), "seq", "head"),
            P(("groups", "dp"), "seq", None),
            P(("groups", "dp"), "head", "seq"),
            P(None, "head"),
            P(),
            P("head"),
            P(("groups", "dp"), "seq", "head"),
        ),
        out_specs=(
            P(("groups", "dp"), "seq", "head"),
            P(("groups", "dp"), "seq", "head"),
            P(("groups", "dp"), "seq", None),
            P("groups", "head"),
            P("groups", None),
            P(("groups", "head")),
        ),
        check_vma=False,
    )
```

```python
import functools

import jax
import jax.numpy as jnp
from jax import lax
from jax.experimental import pallas as pl
from jax.experimental.pallas import tpu as pltpu
from jax.sharding import PartitionSpec as P

BLOCK_LEN = 256
LANES = 128
HALO = 8
NEG = -1e30
f32 = jnp.float32
bf16 = jnp.bfloat16
HIGHEST = lax.Precision.HIGHEST
ROWS16 = 16
MORE = 8
VMEM_LIMIT = 24 * 1024 * 1024


def dot(a, b, precision=None):
    return jnp.dot(a, b, preferred_element_type=f32, precision=precision)


def dot_nt(a, b):
    return lax.dot_general(a, b, (((1,), (1,)), ((), ())), preferred_element_type=f32)


def sigmoid(v):
    return 0.5 * jnp.tanh(0.5 * v) + 0.5


def conv_rows(pad_ref, weights, rows):
    first = HALO - len(weights) + 1
    total = None
    for k, weight in enumerate(weights):
        term = weight * pad_ref[first + k : first + k + rows, :]
        total = term if total is None else total + term
    return total


def tap_rows(ref, lanes):
    block = ref[:, lanes]
    return [block[k : k + 1] for k in range(block.shape[0])]


def silu_grad(pre):
    sg = sigmoid(pre)
    return sg * (1.0 + pre * (1.0 - sg))


def spread(row_a, row_b):
    half, rows = LANES // 2, row_a.shape[1]
    both = jnp.concatenate(
        [jnp.broadcast_to(row_a, (half, rows)), jnp.broadcast_to(row_b, (half, rows))], axis=0
    )
    return both.T


def column(row):
    return jnp.broadcast_to(row, (LANES, row.shape[1])).T


def running_sum(dec):
    rows = dec.shape[1]
    before = lax.broadcasted_iota(jnp.int32, (rows, rows), 0)
    after = lax.broadcasted_iota(jnp.int32, (rows, rows), 1)
    upper = (before <= after).astype(f32)
    return dot(jnp.log(dec), upper, HIGHEST)


def gain_of(dec):
    return jnp.sqrt((1.0 - dec) * (1.0 + dec))


def tail_of(cum):
    return jnp.exp(cum[:, -1:] - cum)


def put_padded(pad_ref, halo, block):
    pad_ref[0:HALO, :] = halo
    pad_ref[HALO : HALO + block.shape[0], :] = block.astype(f32)


def lane_blocks(width):
    return [slice(at, at + LANES) for at in range(0, width, LANES)]


def run_copies(copies):
    for copy in copies:
        copy.start()
    for copy in copies:
        copy.wait()


def early_load_kernel(count, *refs):
    place_ref, x_hbm, g_hbm = refs[:3]
    small = (len(refs) - 9) // 2
    sources, (xa, ga) = refs[3 : 3 + small], refs[3 + small : 5 + small]
    kept, (tails_ref, x16, bc16, sems) = refs[5 + small : -4], refs[-4:]
    bc_hbm = sources[2]
    rows, width = x_hbm.shape
    place = place_ref[0]
    chunk = pl.ds(0, xa.shape[1])
    last = pl.ds(rows - ROWS16, ROWS16)
    tails = [
        pltpu.make_async_copy(x_hbm.at[last, :], x16, sems.at[small + 2]),
        pltpu.make_async_copy(bc_hbm.at[last, :], bc16, sems.at[small + 3]),
    ]
    copies = [pltpu.make_async_copy(sources[i], kept[i], sems.at[i]) for i in range(small)]
    first = [pltpu.make_async_copy(x_hbm.at[:, chunk], xa, sems.at[small])] + copies
    last_ones = [pltpu.make_async_copy(g_hbm.at[:, chunk], ga, sems.at[small + 1])]
    last_ones += copies[:1] + copies[2:]

    def start(found):
        for copy in found:
            copy.start()

    def wait(found):
        for copy in found:
            copy.wait()

    pl.when(place == 0)(lambda: start(first))
    pl.when(place == count - 1)(lambda: start(last_ones))
    run_copies(tails)
    pl.when(place == 0)(lambda: wait(first))
    pl.when(place == count - 1)(lambda: wait(last_ones))
    tails_ref[:, :width] = x16[...].astype(f32)[ROWS16 - HALO :].astype(bf16)
    tails_ref[:, width:] = bc16[...].astype(f32)[ROWS16 - HALO :].astype(bf16)


def load_kernel(*refs):
    count = (len(refs) - 2) // 2
    sources, kept, sems = refs[:count], refs[count + 1 : -1], refs[-1]
    run_copies(
        [pltpu.make_async_copy(sources[i], kept[i], sems.at[i]) for i in range(count)]
    )


def head_rows(ref, h):
    return ref[pl.ds(h, 1), :], ref[pl.ds(h + 1, 1), :]


def state_of(bc_rows, factors):
    over = (((0,), (0,)), ((), ()))
    return lax.dot_general(bc_rows, factors, over, preferred_element_type=f32)


def weighted_tails(start, heads_at, x_ref, wx_ref, halo, gt, pad, lw):
    rows, width = lw.shape
    for q, lanes in enumerate(lane_blocks(width)):
        full = slice(start + q * LANES, start + (q + 1) * LANES)
        one = pad.at[q]
        put_padded(one, halo(full), x_ref[:, full])
        pre = conv_rows(one, tap_rows(wx_ref, full), rows)
        inner = (pre * sigmoid(pre)).astype(bf16).astype(f32)
        factor = spread(*head_rows(gt, heads_at + 2 * q))
        lw[:, lanes] = (inner * factor).astype(bf16)


def led_gradients(start, heads_at, g_ref, sl, lg):
    for q, lanes in enumerate(lane_blocks(lg.shape[1])):
        full = slice(start + q * LANES, start + (q + 1) * LANES)
        lead = spread(*head_rows(sl, heads_at + 2 * q))
        lg[:, lanes] = (g_ref[:, full].astype(f32) * lead).astype(bf16)


def mapped_half(half, state, rows, bc_block, halo, wbc_ref, bcpad):
    lanes = slice(half * state, (half + 1) * state)
    put_padded(bcpad, halo, bc_block)
    pre = conv_rows(bcpad, tap_rows(wbc_ref, lanes), rows)
    return (pre * sigmoid(pre)).astype(bf16)


def put_first_rows(pay_ref, lg, bc_ref, more):
    state = pay_ref.shape[0] - MORE
    bcw = bc_ref.shape[1]
    more[0:4, :] = lg[0:ROWS16, :].astype(f32)[0:4]
    more[4:8, 0:bcw] = bc_ref[0:ROWS16, :].astype(f32)[0:4]
    more[4:8, bcw:] = jnp.zeros((4, lg.shape[1] - bcw), f32)
    pay_ref[state:, :] = more[...].astype(bf16)


def first_rows_state(more, bc_ref, wbc_ref, bcpad):
    rows, bcw = bc_ref.shape
    state = bcw // 2
    taps = wbc_ref.shape[0]
    zeros = jnp.zeros((ROWS16 - 4, state), f32)
    edge = bc_ref[rows - ROWS16 :, state:].astype(f32)[ROWS16 - HALO :]
    block = jnp.concatenate([more[4:8, state:bcw], zeros], axis=0)
    c = mapped_half(1, state, ROWS16, block, edge, wbc_ref, bcpad)
    early = lax.broadcasted_iota(jnp.int32, c.shape, 0) < taps - 1
    lg = jnp.concatenate([more[0:4, :], jnp.zeros((ROWS16 - 4, more.shape[1]), f32)], axis=0)
    return state_of(jnp.where(early, c, jnp.zeros_like(c)), lg.astype(bf16))


def bc_tail_place(r, taps, bcw):
    return 2 * taps - 2 + r // 2, slice((r % 2) * bcw, (r % 2 + 1) * bcw)


def first_state_kernel(count, scale, *refs):
    place_ref, dec_ref, xa_ref, ga_ref, wx_ref, bc_ref, wbc_ref, tails_ref = refs[:8]
    pay_ref, pad, gt, sl, lw, lg, bcpad, tails, more = refs[8:]
    rows, width = xa_ref.shape
    taps, bcw = wbc_ref.shape
    state = bcw // 2
    place = place_ref[0]
    none = jnp.zeros((HALO, LANES), f32)

    @pl.when(place == 0)
    def _():
        dec = dec_ref[...]
        gt[...] = gain_of(dec) * tail_of(running_sum(dec))
        b = mapped_half(0, state, rows, bc_ref[:, :state], none, wbc_ref, bcpad)
        weighted_tails(0, 0, xa_ref, wx_ref, lambda _: none, gt, pad, lw)
        pay_ref[0:state, :] = state_of(b, lw[...]).astype(bf16)
        tails[...] = tails_ref[...].astype(f32)
        more[0 : taps - 1, :] = tails[HALO - taps + 1 :, 0:width]
        more[taps - 1 : 2 * taps - 2, :] = tails[HALO - taps + 1 :, width : 2 * width]
        for r in range(taps - 1):
            at, here = bc_tail_place(r, taps, bcw)
            more[at : at + 1, here] = tails[HALO - taps + 1 + r :, 2 * width :][0:1]
        pay_ref[state:, :] = more[...].astype(bf16)

    @pl.when(place == count - 1)
    def _():
        sl[...] = scale * jnp.exp(running_sum(dec_ref[...]))
        c = mapped_half(1, state, rows, bc_ref[:, state:], none, wbc_ref, bcpad)
        late = lax.broadcasted_iota(jnp.int32, c.shape, 0) >= taps - 1
        led_gradients(0, 0, ga_ref, sl, lg)
        pay_ref[0:state, :] = state_of(jnp.where(late, c, jnp.zeros_like(c)), lg[...]).astype(bf16)
        put_first_rows(pay_ref, lg, bc_ref, more)


def middle_first_kernel(count, scale, *refs):
    place_ref, dec_ref, x_ref, g_ref, wx_ref, bc_ref, wbc_ref, _ = refs[:8]
    cum_ref, map_ref, u_ref, v_ref, tot_ref, gt16_ref, lg16_ref = refs[8:15]
    pad, gt, sl, lw, lg, bcpad = refs[15:]
    rows, bcw = bc_ref.shape
    state = bcw // 2
    none = jnp.zeros((HALO, LANES), f32)
    dec = dec_ref[...]
    cum = running_sum(dec)
    cum_ref[...] = cum
    for half in range(2):
        lanes = slice(half * state, (half + 1) * state)
        made = mapped_half(half, state, rows, bc_ref[:, lanes], none, wbc_ref, bcpad.at[half])
        map_ref[:, lanes] = made
    place = place_ref[0]

    @pl.when(jnp.logical_and(place > 0, place < count - 1))
    def _():
        gt[...] = gain_of(dec) * tail_of(cum)
        lead = jnp.exp(cum)
        sl[...] = scale * lead
        weighted_tails(0, 0, x_ref, wx_ref, lambda _: none, gt, pad, lw)
        led_gradients(0, 0, g_ref, sl, lg)
        lane_totals(lead, 0, tot_ref)
        for q, lanes in enumerate(lane_blocks(lw.shape[1])):
            half = LANES // 2
            a, b = (row[:, 0:LANES] for row in head_rows(gt, 2 * q))
            both = [jnp.broadcast_to(row, (half, LANES)) for row in (a, b)]
            gt16_ref[:, lanes] = jnp.concatenate(both, axis=0).T[0:ROWS16]
        lg16_ref[...] = lg[0:ROWS16, :]
        late = lax.broadcasted_iota(jnp.int32, (rows, state), 0) >= ROWS16
        zero = jnp.zeros((rows, state), bf16)
        u_ref[...] = state_of(jnp.where(late, map_ref[:, :state], zero), lw[...])
        v_ref[...] = state_of(jnp.where(late, map_ref[:, state:], zero), lg[...])


def fix_kernel(count, *refs):
    place_ref, halo_in, came_ref, x_ref, wx_ref, bc_ref, wbc_ref, map_in = refs[:8]
    u_in, v_in, tot_ref, gt16_ref, lg16_ref, _ = refs[8:14]
    halo_ref, map_ref, u_ref, v_ref, came_out, pay_ref, halo, more, pad, bcpad = refs[14:]
    rows, bcw = bc_ref.shape
    state = bcw // 2
    taps = wbc_ref.shape[0]
    width = u_in.shape[1]
    place = place_ref[0]
    more[...] = came_ref[state:, :].astype(f32)
    halo[...] = halo_in[...].astype(f32)

    @pl.when(place == 1)
    def _():
        halo[HALO - taps + 1 :, 0:width] = more[0 : taps - 1, :]
        halo[HALO - taps + 1 :, width : 2 * width] = more[taps - 1 : 2 * taps - 2, :]
        for r in range(taps - 1):
            at, here = bc_tail_place(r, taps, bcw)
            row = HALO - taps + 1 + r
            halo[row : row + 1, 2 * width :] = more[at : at + 1, here]

    halo_ref[...] = halo[...].astype(bf16)
    map_ref[...] = map_in[...]
    for half in range(2):
        lanes = slice(half * state, (half + 1) * state)
        edge = halo[:, 2 * width + half * state : 2 * width + (half + 1) * state]
        one = bcpad.at[half]
        made = mapped_half(half, state, ROWS16, bc_ref[0:ROWS16, lanes], edge, wbc_ref, one)
        map_ref[0:ROWS16, lanes] = made
    came_out[...] = came_ref[0:state, :]
    tot = tot_ref[0:1, :]

    @pl.when(jnp.logical_and(place > 0, place < count - 1))
    def _():
        lw16 = []
        for q, lanes in enumerate(lane_blocks(width)):
            one = pad.at[q]
            put_padded(one, halo[:, lanes], x_ref[0:ROWS16, lanes])
            pre = conv_rows(one, tap_rows(wx_ref, lanes), ROWS16)
            inner = (pre * sigmoid(pre)).astype(bf16).astype(f32)
            lw16.append((inner * gt16_ref[:, lanes]).astype(bf16))
        lw16 = jnp.concatenate(lw16, axis=1)
        u_ref[...] = u_in[...] + state_of(map_ref[0:ROWS16, :state], lw16)
        v_ref[...] = v_in[...] + state_of(map_ref[0:ROWS16, state:], lg16_ref[...])

    @pl.when(place == 1)
    def _():
        pay_ref[...] = (u_ref[...] + tot * came_ref[0:state, :].astype(f32)).astype(bf16)

    @pl.when(place == count - 2)
    def _():
        extra = first_rows_state(more, bc_ref, wbc_ref, bcpad.at[0])
        came = came_ref[0:state, :].astype(f32) + extra
        came_out[...] = came.astype(bf16)
        pay_ref[...] = (v_ref[...] + tot * came).astype(bf16)


def lane_totals(lead, heads_at, tot_ref):
    rows = lead.shape[1]
    for q, lanes in enumerate(lane_blocks(tot_ref.shape[1])):
        low = lax.broadcasted_iota(jnp.int32, (8, LANES), 1) < LANES // 2
        a, b = (lead[heads_at + 2 * q + i :, rows - 1 :][:1] for i in range(2))
        tot_ref[:, lanes] = jnp.where(low, a, b)


def middle_state_kernel(count, start, heads_at, scale, *refs):
    place_ref, dec_ref, x_ref, g_ref, halo_ref, wx_ref, cum_ref, map_ref, _ = refs[:9]
    u_ref, v_ref, tot_ref = refs[9:12]
    pad, gt, sl, lw, lg = refs[12:]
    state = map_ref.shape[1] // 2
    place = place_ref[0]

    @pl.when(jnp.logical_and(place > 0, place < count - 1))
    def _():
        cum = cum_ref[...]
        gt[...] = gain_of(dec_ref[...]) * tail_of(cum)
        lead = jnp.exp(cum)
        sl[...] = scale * lead

        def halo(full):
            return halo_ref[:, full].astype(f32)

        weighted_tails(start, heads_at, x_ref, wx_ref, halo, gt, pad, lw)
        led_gradients(start, heads_at, g_ref, sl, lg)
        lane_totals(lead, heads_at, tot_ref)
        u_ref[...] = state_of(map_ref[:, :state], lw[...])
        v_ref[...] = state_of(map_ref[:, state:], lg[...])


def end_state_kernel(count, start, heads_at, scale, *refs):
    place_ref, dec_ref, x_ref, g_ref, wx_ref, bc_ref, cum_ref, map_ref, _ = refs[:9]
    pay_ref, pad, gt, sl, lw, lg, more = refs[9:]
    state = map_ref.shape[1] // 2
    taps = wx_ref.shape[0]
    place = place_ref[0]

    @pl.when(place == 0)
    def _():
        gt[...] = gain_of(dec_ref[...]) * tail_of(cum_ref[...])
        none = jnp.zeros((HALO, LANES), f32)
        weighted_tails(start, heads_at, x_ref, wx_ref, lambda _: none, gt, pad, lw)
        pay_ref[0:state, :] = state_of(map_ref[:, :state], lw[...]).astype(bf16)

    @pl.when(place == count - 1)
    def _():
        sl[...] = scale * jnp.exp(cum_ref[...])
        led_gradients(start, heads_at, g_ref, sl, lg)
        c = map_ref[:, state:]
        late = lax.broadcasted_iota(jnp.int32, c.shape, 0) >= taps - 1
        pay_ref[0:state, :] = state_of(jnp.where(late, c, jnp.zeros_like(c)), lg[...]).astype(bf16)
        put_first_rows(pay_ref, lg, bc_ref, more)


def message_kernel(hop, place_ref, u_ref, v_ref, tot_ref, came_ref, _, out_ref):
    own = jnp.where(place_ref[0] == hop, u_ref[...], v_ref[...])
    out_ref[...] = (own + tot_ref[0:1, :] * came_ref[...].astype(f32)).astype(bf16)


def fix_message_kernel(count, *refs):
    place_ref, u_ref, v_ref, tot_ref, came_ref, bc_ref, wbc_ref, _ = refs[:8]
    came_out, out_ref, more, bcpad = refs[8:]
    state = u_ref.shape[0]
    place = place_ref[0]
    tot = tot_ref[0:1, :]
    came_out[...] = came_ref[0:state, :]

    @pl.when(place == 1)
    def _():
        out_ref[...] = (u_ref[...] + tot * came_ref[0:state, :].astype(f32)).astype(bf16)

    @pl.when(place == count - 2)
    def _():
        more[...] = came_ref[state:, :].astype(f32)
        extra = first_rows_state(more, bc_ref, wbc_ref, bcpad)
        came = came_ref[0:state, :].astype(f32) + extra
        came_out[...] = came.astype(bf16)
        out_ref[...] = (v_ref[...] + tot * came).astype(bf16)


def edge_kernel(count, spans, parts, *refs):
    hops = count - 2
    place_ref, map_ref = refs[:2]
    blocks, refs = refs[3 : 3 + 2 * parts], refs[3 + 2 * parts :]
    came, (out_ref, edge) = refs[: 2 * hops], refs[2 * hops :]
    state = map_ref.shape[1] // 2
    b = map_ref[0:ROWS16, :state]
    per = len(spans) // 2
    for c in range(2):
        wanted = came[c * hops : (c + 1) * hops]
        grad = pick(place_ref[0], wanted, lambda hop: count - 2 - hop, state)
        extra = dot(b, grad)
        for q in range(per):
            part, lanes = spans[c * per + q]
            dx_ref, q_ref = blocks[2 * part : 2 * part + 2]
            here = slice(q * LANES, (q + 1) * LANES)
            rows = dx_ref[0:ROWS16, lanes] + q_ref[0:ROWS16, lanes].astype(f32) * extra[:, here]
            edge[4 * c : 4 * c + 4, here] = rows[0:4]
    out_ref[...] = edge[...].astype(bf16)


def intra_kernel(first, start, pairs, head_dim, scale, *refs):
    x_ref, g_ref, halo_ref, wx_ref, dec_ref, cum_ref, map_ref, skip_ref, _ = refs[:9]
    refs = refs[9:]
    if not first:
        dsim_in, gs_in = refs[:2]
        refs = refs[2:]
    y0_ref, dx_ref, q_ref, ls_ref, lw_ref, lg_ref, dsim_ref, gs_ref = refs[:8]
    pad, sim, gain = refs[8:]
    rows = x_ref.shape[0]
    state = map_ref.shape[1] // 2
    half = rows // 2
    gain[...] = gain_of(dec_ref[...])
    sim[...] = dot_nt(map_ref[:, state:], map_ref[:, :state])
    if first:
        dsim_ref[...] = jnp.zeros(dsim_ref.shape, f32)
        gs_ref[...] = jnp.zeros(gs_ref.shape, f32)
    else:
        dsim_ref[...] = dsim_in[...]
        gs_ref[...] = gs_in[...]
    lane = lax.broadcasted_iota(jnp.int32, (1, LANES), 1)
    low = lane < head_dim
    r_i = lax.broadcasted_iota(jnp.int32, (half, half), 0)
    c_i = lax.broadcasted_iota(jnp.int32, (half, half), 1)
    lower = r_i >= c_i

    def pair(q):
        lanes = slice(q * LANES, (q + 1) * LANES)
        full = slice(start + q * LANES, start + (q + 1) * LANES)
        h = start // head_dim + 2 * q
        one = pad.at[q]
        put_padded(one, halo_ref[:, full].astype(f32), x_ref[:, full])
        pre = conv_rows(one, tap_rows(wx_ref, full), rows)
        sg = sigmoid(pre)
        inner = (pre * sg).astype(bf16).astype(f32)
        sgrad = sg * (1.0 + pre * (1.0 - sg))
        gn = spread(*head_rows(gain, h))
        cums = head_rows(cum_ref, h)
        cols = [column(row) for row in cums]
        both = jnp.where(low, cols[0], cols[1])
        tl = jnp.exp(both[rows - 1 :] - both)
        ls = scale * jnp.exp(both)
        w = (inner * gn).astype(bf16)
        g = g_ref[:, full]
        gf = g.astype(f32)
        g_t = gf.T.astype(bf16)
        y = ds = None
        dw_t = []
        for a in range(2):
            row, col = cums[a], cols[a]
            keep = low if a == 0 else jnp.logical_not(low)
            d00 = jnp.exp(jnp.where(lower, col[:half] - row[:, :half], NEG))
            d10 = jnp.exp(col[half:] - row[:, :half])
            d11 = jnp.exp(jnp.where(lower, col[half:] - row[:, half:], NEG))
            m00 = (d00 * sim[0:half, 0:half]).astype(bf16)
            m10 = (d10 * sim[half:rows, 0:half]).astype(bf16)
            m11 = (d11 * sim[half:rows, half:rows]).astype(bf16)
            w_a = jnp.where(keep, w, jnp.zeros_like(w))
            top = dot(m00, w_a[:half])
            bot = dot(jnp.concatenate([m10, m11], axis=1), w_a)
            y_a = jnp.concatenate([top, bot], axis=0)
            y = y_a if y is None else y + y_a
            g_at = g_t[a * head_dim : (a + 1) * head_dim]
            left = dot(g_at, jnp.concatenate([m00, m10], axis=0))
            right = dot(g_at[:, half:], m11)
            dw_t.append(jnp.concatenate([left, right], axis=1))
            mix_top = dot_nt(g[:half], w_a[:half])
            mix_bot = dot_nt(g[half:], w_a)
            now = (d00 * mix_top, d10 * mix_bot[:, :half], d11 * mix_bot[:, half:])
            ds = now if ds is None else [one + two for one, two in zip(ds, now)]
        dsim_ref[0:half, 0:half] += ds[0]
        dsim_ref[half:rows, 0:half] += ds[1]
        dsim_ref[half:rows, half:rows] += ds[2]
        dw = scale * jnp.concatenate(dw_t, axis=0).T
        skip = jnp.where(low, skip_ref[:, h : h + 1], skip_ref[:, h + 1 : h + 2])
        y0_ref[:, lanes] = scale * y + skip * inner
        dx_ref[:, lanes] = (gn * dw + skip * gf) * sgrad
        q_ref[:, lanes] = (gn * tl * sgrad).astype(bf16)
        ls_ref[:, lanes] = ls.astype(bf16)
        lw_ref[:, lanes] = (inner * gn * tl).astype(bf16)
        lg_ref[:, lanes] = (gf * ls).astype(bf16)
        gi = jnp.sum(gf * inner, axis=0, keepdims=True)
        sum_a = jnp.sum(jnp.where(low, gi, 0.0), axis=1, keepdims=True)
        sum_b = jnp.sum(jnp.where(low, 0.0, gi), axis=1, keepdims=True)
        gs_ref[...] += jnp.where(lane == h, sum_a, 0.0) + jnp.where(lane == h + 1, sum_b, 0.0)

    for q in range(pairs):
        pair(q)


def pick(place, parts, wanted, state):
    total = jnp.zeros((state, parts[0].shape[1]), bf16)
    for hop, ref in enumerate(parts):
        total = jnp.where(place == wanted(hop), ref[0:state, :], total)
    return total


def add_states(spans, blocks, which, states, total):
    done = 0
    while done < len(spans):
        part, lanes = spans[done]
        size = 1
        while done + size < len(spans) and spans[done + size][0] == part:
            size += 1
        mine = slice(lanes.start, lanes.start + size * LANES)
        here = slice(done * LANES, (done + size) * LANES)
        made = dot_nt(blocks[2 * part + which][:, mine], states[:, here])
        total = made if total is None else total + made
        done += size
    return total


def before_silu(half, total, bc_ref, halo_ref, wbc_ref, bcpad):
    rows, bcw = bc_ref.shape
    state = bcw // 2
    taps = wbc_ref.shape[0]
    inner = halo_ref.shape[1] - bcw
    lanes = slice(half * state, (half + 1) * state)
    edge = halo_ref[:, inner + half * state : inner + (half + 1) * state].astype(f32)
    put_padded(bcpad, edge, bc_ref[:, lanes])
    dpre = total * silu_grad(conv_rows(bcpad, tap_rows(wbc_ref, lanes), rows))
    sums = []
    for k in range(taps):
        moved = bcpad[HALO - taps + 1 + k : HALO - taps + 1 + k + rows, :]
        sums.append(jnp.sum(dpre * moved, axis=0, keepdims=True))
    return dpre, jnp.concatenate(sums + [jnp.zeros((8 - taps, state), f32)], axis=0)


def finish_bc_kernel(count, first, spans, parts, scale, *refs):
    hops = count - 1
    place_ref, map_ref, sum_in = refs[:3]
    blocks, refs = refs[4 : 4 + 2 * parts], refs[4 + 2 * parts :]
    came, refs = refs[:hops], refs[hops:]
    bcw = map_ref.shape[1]
    state = bcw // 2
    place = place_ref[0]
    enter = pick(place, came, lambda hop: hop + 1, state)
    grad = pick(place, came, lambda hop: count - 2 - hop, state)
    if first:
        ds = scale * sum_in[...]
        high = ds.astype(bf16)
        rest = (ds - high.astype(f32)).astype(bf16)
        ds_t = ds.T
        high_t = ds_t.astype(bf16)
        rest_t = (ds_t - high_t.astype(f32)).astype(bf16)
        b, c = map_ref[:, :state], map_ref[:, state:]
        d_b = dot(high_t, c) + dot(rest_t, c)
        d_c = dot(high, b) + dot(rest, b)
    else:
        d_b, d_c = sum_in[:, :state], sum_in[:, state:]
    d_b = add_states(spans, blocks, 0, grad, d_b)
    d_c = add_states(spans, blocks, 1, enter, d_c)
    if first:
        (dbc_ref,) = refs
        dbc_ref[:, :state] = d_b
        dbc_ref[:, state:] = d_c
        return
    bc_ref, halo_ref, wbc_ref, gs_ref, own_ref, small_ref, bcpad = refs
    for half in range(2):
        lanes = slice(half * state, (half + 1) * state)
        made = before_silu(half, (d_b, d_c)[half], bc_ref, halo_ref, wbc_ref, bcpad.at[half])
        own_ref[:, lanes], small_ref[:, lanes] = made
    small_ref[:, bcw:] = gs_ref[...]


def finish_kernel(count, start, spans, parts, pieces, *refs):
    hops = count - 1
    place_ref, x_ref, wx_ref, map_ref = refs[:4]
    blocks, refs = refs[5 : 5 + 4 * parts], refs[5 + 4 * parts :]
    came, refs = refs[:hops], refs[hops:]
    y_hbm, gx_hbm, taps_ref, end_ref, enter, grad, pad, y_ref, gx_ref, sems = refs
    rows = x_ref.shape[0]
    taps = wx_ref.shape[0]
    state = enter.shape[0]
    place = place_ref[0]
    b, c = map_ref[:, :state], map_ref[:, state:]
    enter[...] = pick(place, came, lambda hop: hop + 1, state)
    grad[...] = pick(place, came, lambda hop: count - 2 - hop, state)
    copies = []
    first = 0
    for number, size in enumerate(pieces):
        for q in range(first, first + size):
            part, mine = spans[q]
            y0_ref, dx_ref, q_ref, ls_ref = blocks[4 * part : 4 * part + 4]
            lanes = slice(q * LANES, (q + 1) * LANES)
            full = slice(start + q * LANES, start + (q + 1) * LANES)
            inter = dot(c, enter[:, lanes])
            y_ref[:, lanes] = (y0_ref[:, mine] + ls_ref[:, mine].astype(f32) * inter).astype(bf16)
            one = pad.at[q]
            inter = dot(b, grad[:, lanes])
            one[0:rows, :] = dx_ref[:, mine] + q_ref[:, mine].astype(f32) * inter
            one[rows : rows + HALO, :] = jnp.zeros((HALO, LANES), f32)
            x = x_ref[:, full].astype(f32)
            total = None
            sums = []
            for k, weight in enumerate(tap_rows(wx_ref, full)):
                shifted = one[taps - 1 - k : taps - 1 - k + rows, :]
                term = weight * shifted
                total = term if total is None else total + term
                sums.append(jnp.sum(shifted * x, axis=0, keepdims=True))
            gx_ref[:, lanes] = total.astype(bf16)
            end_ref[:, lanes] = total[rows - ROWS16 :]
            sums = jnp.concatenate(sums + [jnp.zeros((8 - taps, LANES), f32)], axis=0)
            taps_ref[:, lanes] = sums
        lanes = slice(first * LANES, (first + size) * LANES)
        full = slice(start + first * LANES, start + (first + size) * LANES)
        for i, (made, out) in enumerate(((y_ref, y_hbm), (gx_ref, gx_hbm))):
            copy = pltpu.make_async_copy(made.at[:, lanes], out.at[:, full], sems.at[number, i])
            copy.start()
            copies.append(copy)
        first += size
    for copy in copies:
        copy.wait()


def finish_grad_kernel(count, start, spans, parts, *refs):
    hops = count - 1
    place_ref, x_ref, wx_ref, map_ref = refs[:4]
    blocks, refs = refs[5 : 5 + 2 * parts], refs[5 + 2 * parts :]
    came, (gx_ref, taps_ref, end_ref, grad, pad) = refs[:hops], refs[hops:]
    rows = x_ref.shape[0]
    taps = wx_ref.shape[0]
    state = grad.shape[0]
    b = map_ref[:, :state]
    grad[...] = pick(place_ref[0], came, lambda hop: count - 2 - hop, state)
    for q, (part, mine) in enumerate(spans):
        dx_ref, q_ref = blocks[2 * part : 2 * part + 2]
        lanes = slice(q * LANES, (q + 1) * LANES)
        full = slice(start + q * LANES, start + (q + 1) * LANES)
        one = pad.at[q]
        inter = dot(b, grad[:, lanes])
        one[0:rows, :] = dx_ref[:, mine] + q_ref[:, mine].astype(f32) * inter
        one[rows : rows + HALO, :] = jnp.zeros((HALO, LANES), f32)
        x = x_ref[:, full].astype(f32)
        total = None
        sums = []
        for k, weight in enumerate(tap_rows(wx_ref, full)):
            shifted = one[taps - 1 - k : taps - 1 - k + rows, :]
            term = weight * shifted
            total = term if total is None else total + term
            sums.append(jnp.sum(shifted * x, axis=0, keepdims=True))
        gx_ref[:, lanes] = total.astype(bf16)
        end_ref[:, lanes] = total[rows - ROWS16 :]
        sums = jnp.concatenate(sums + [jnp.zeros((8 - taps, LANES), f32)], axis=0)
        taps_ref[:, lanes] = sums


def sums_kernel(halo_ref, edge_ref, taps_a, taps_b, sums_ref, halo):
    taps, width = 4, taps_a.shape[1]
    edge = edge_ref[...].astype(f32)
    halo[...] = halo_ref[:, 0 : 2 * width].astype(f32)
    for c, own in enumerate((taps_a, taps_b)):
        lanes = slice(c * width, (c + 1) * width)
        sums_ref[:, lanes] = own[...]
        for k in range(taps - 1):
            added = None
            for j in range(taps - 1 - k):
                at = HALO - taps + 1 + k + j
                term = edge[4 * c + j : 4 * c + j + 1] * halo[at : at + 1, lanes]
                added = term if added is None else added + term
            sums_ref[k : k + 1, lanes] += added


def write_kernel(count, start, spans, parts, *refs):
    hops = count - 1
    place_ref, map_ref, wx_ref, edge_ref, end_a, end_b, gx_b = refs[:7]
    blocks, refs = refs[8 : 8 + 2 * parts], refs[8 + 2 * parts :]
    came, refs = refs[:hops], refs[hops + 2 :]
    y_hbm, gx_hbm, enter, y_b, gx16, sems = refs
    taps = wx_ref.shape[0]
    rows, width = gx_b.shape
    state = enter.shape[0]
    chunk = pl.ds(start, width)
    body = pl.ds(0, rows - ROWS16)
    tail = pl.ds(rows - ROWS16, ROWS16)
    copies = [pltpu.make_async_copy(gx_b.at[body, :], gx_hbm.at[body, chunk], sems.at[0])]
    copies[0].start()
    edge = edge_ref[...].astype(f32)
    row = lax.broadcasted_iota(jnp.int32, (ROWS16, width), 0)
    for c, end_ref in enumerate((end_a, end_b)):
        lanes = slice(c * width, (c + 1) * width)
        end = end_ref[...]
        for k in range(taps - 1):
            for j in range(taps - 1 - k):
                at = ROWS16 - (taps - 1 - k) + j
                here = wx_ref[k : k + 1, lanes] * edge[4 * c + j : 4 * c + j + 1]
                end = end + jnp.where(row == at, here, 0.0)
        gx16[:, lanes] = end.astype(bf16)
    copies.append(pltpu.make_async_copy(gx16, gx_hbm.at[tail, :], sems.at[1]))
    copies[1].start()
    c = map_ref[:, state:]
    enter[...] = pick(place_ref[0], came, lambda hop: hop + 1, state)
    for q, (part, mine) in enumerate(spans):
        y0_ref, ls_ref = blocks[2 * part : 2 * part + 2]
        lanes = slice(q * LANES, (q + 1) * LANES)
        inter = dot(c, enter[:, lanes])
        y_b[:, lanes] = (y0_ref[:, mine] + ls_ref[:, mine].astype(f32) * inter).astype(bf16)
    copies.append(pltpu.make_async_copy(y_b, y_hbm.at[:, chunk], sems.at[2]))
    copies[2].start()
    for copy in copies:
        copy.wait()


def pack_kernel(own_ref, small_ref, small_dp, _, small_out, head_ref):
    rows, bcw = own_ref.shape
    small = small_ref[...] + small_dp[...]
    small_out[...] = small
    head_ref[0:rows, :] = own_ref[...].astype(bf16)
    sums = small[:, :bcw]
    head_ref[rows:, :] = jnp.concatenate([sums, jnp.zeros_like(sums)], axis=0).astype(bf16)


def merge_kernel(heads, *refs):
    sums_ref, sums_dp, small_ref, own_ref = refs[:4]
    others, (full_ref, out_ref, send_ref) = refs[4 : 3 + heads], refs[3 + heads :]
    rows, bc = own_ref.shape
    total = sums_ref[...] + sums_dp[...]
    half = total.shape[1] // 2
    full = own_ref[...]
    taps_bc = small_ref[:, :bc]
    for other in others:
        block = other[...].astype(f32)
        full = full + block[:rows]
        taps_bc = taps_bc + block[rows : rows + 8]
    full_ref[...] = full
    send_ref[0:4, 0:half] = total[0:4, :half]
    send_ref[4:8, 0:half] = total[0:4, half:]
    send_ref[0:4, half : half + bc] = taps_bc[0:4]
    send_ref[4:8, half : half + bc] = full[0:4]
    send_ref[:, half + bc :] = small_ref[:, bc:]
    out_ref[...] = send_ref[...].astype(bf16)


def conv_bc_kernel(full_ref, wbc_ref, _, out_ref, pad):
    taps = wbc_ref.shape[0]
    rows, bcw = full_ref.shape
    for half in range(2):
        lanes = slice(half * bcw // 2, (half + 1) * bcw // 2)
        one = pad.at[half]
        one[0:rows, :] = full_ref[:, lanes]
        one[rows:, :] = jnp.zeros((HALO, bcw // 2), f32)
        out = None
        for k, weight in enumerate(tap_rows(wbc_ref, lanes)):
            term = weight * one[taps - 1 - k : taps - 1 - k + rows, :]
            out = term if out is None else out + term
        out_ref[:, lanes] = out


def last_kernel(count, norm_tokens, norm_skip, *refs):
    place_ref, sums_ref, conv_ref, wbc_ref = refs[:4]
    parts = refs[4 : 3 + count]
    gbc_ref, tx_ref, tbc_ref, skip_ref = refs[3 + count :]
    taps, bc = wbc_ref.shape
    rows = conv_ref.shape[0]
    half = tx_ref.shape[1] // 2
    total = sums_ref[...].astype(f32)
    edge = jnp.zeros((4, bc), f32)
    for hop, ref in enumerate(parts):
        block = ref[...].astype(f32)
        total = total + block
        if hop == count - 2:
            edge = jnp.where(place_ref[0] < count - 1, block[4:8, half : half + bc], 0.0)
    tx_ref[:, :half] = total[0:taps, 0:half] * norm_tokens
    tx_ref[:, half:] = total[4 : 4 + taps, 0:half] * norm_tokens
    tbc_ref[...] = total[0:taps, half : half + bc] * norm_tokens
    skip_ref[...] = total[0:1, half + bc : half + bc + skip_ref.shape[1]] * norm_skip
    gbc_ref[0 : rows - ROWS16, :] = conv_ref[0 : rows - ROWS16, :].astype(bf16)
    row = lax.broadcasted_iota(jnp.int32, (ROWS16, bc), 0)
    end = conv_ref[rows - ROWS16 :, :]
    for k in range(taps - 1):
        for j in range(taps - 1 - k):
            at = ROWS16 - (taps - 1 - k) + j
            end = end + jnp.where(row == at, wbc_ref[k : k + 1, :] * edge[j : j + 1], 0.0)
    gbc_ref[rows - ROWS16 :, :] = end.astype(bf16)


COST_US = {"middle_state": 1.5, "inside_block": 2.7, "sums": 0.8, "write": 0.8}
BYTES_PER_US = 3_500_000


def call(kernel, name, ins, outs, scratch=(), grid=(1,), kept=()):
    def spec(item):
        if not isinstance(item, tuple):
            whole = item.shape
            return pl.BlockSpec(whole, lambda *_: (0,) * len(whole))
        if item[1] == "smem":
            return pl.BlockSpec(memory_space=pltpu.SMEM)
        if item[1] == "any":
            return pl.BlockSpec(memory_space=pl.ANY)
        if item[1] == "hbm":
            return pl.BlockSpec(memory_space=pltpu.HBM)
        return pl.BlockSpec(item[1], item[2])

    def array(item):
        return item[0] if isinstance(item, tuple) else item

    return pl.pallas_call(
        kernel,
        grid=grid,
        in_specs=[spec(i) for i in ins],
        out_specs=[spec(o) for o in outs],
        out_shape=[array(o) for o in outs],
        scratch_shapes=list(scratch),
        compiler_params=pltpu.CompilerParams(vmem_limit_bytes=VMEM_LIMIT),
        cost_estimate=pl.CostEstimate(
            flops=0, bytes_accessed=int(COST_US.get(name, 0.01) * BYTES_PER_US), transcendentals=0
        ),
        input_output_aliases=dict(kept),
        name=name,
    )(*[array(i) for i in ins])


def chain_routes(count, hop):
    return [(hop, hop + 1), (count - 1 - hop, count - 2 - hop)]


def shape(s, d=f32):
    return jax.ShapeDtypeStruct(s, d)


def local(x_input, bc_input, decays, conv_x, conv_bc, skip_gain, grad_out):
    x, bc, dec, g = x_input[0], bc_input[0], decays[0], grad_out[0]
    rows, inner = x.shape
    taps = conv_x.shape[0]
    heads = dec.shape[0]
    head_dim = inner // heads
    bcw = bc.shape[1]
    state = bcw // 2
    scale = state ** (-0.5)
    count = lax.axis_size("seq")
    head_count = lax.axis_size("head")
    dp_count = lax.axis_size("dp")
    assert rows == BLOCK_LEN and 2 * head_dim == LANES and taps == 4
    assert count % 2 == 0 and count > 2 and dp_count == 2
    width = inner // 2
    chunks = (0, 1)
    block = 640 if width % 640 == 0 else LANES
    per = width // block
    pairs = width // LANES
    split = (pairs // 2 + pairs // 10, pairs + pairs // 10)
    split += (2 * pairs - sum(split),)
    spans = [
        (part, slice(at * LANES, (at + 1) * LANES))
        for part, size in enumerate(split)
        for at in range(size)
    ]
    place = lax.axis_index("seq").astype(jnp.int32).reshape(1)
    where_am_i = (place, "smem")

    def vmem(s, d=f32):
        return pltpu.VMEM(s, d)

    def in_hbm(a):
        return (pltpu.with_memory_space_constraint(a, pltpu.HBM), "hbm")

    def padded(blocks, length=rows):
        return vmem((blocks, length + HALO, LANES))

    state_scratch = [
        padded(pairs),
        vmem((heads, rows)),
        vmem((heads, rows)),
        vmem((rows, width), bf16),
        vmem((rows, width), bf16),
    ]
    received = [[], []]

    def hop_on(c, message):
        routes = chain_routes(count, len(received[c]))
        received[c].append(lax.ppermute(message, "seq", routes))

    skip = skip_gain.reshape(1, heads)
    sources = [dec, conv_x, bc, conv_bc]
    xa, ga, *made, tails = call(
        functools.partial(early_load_kernel, count),
        "early_load",
        [where_am_i, in_hbm(x), in_hbm(g)] + [in_hbm(a) for a in sources],
        [shape((rows, width), bf16), shape((rows, width), bf16)]
        + [shape(a.shape, a.dtype) for a in sources]
        + [shape((HALO, inner + bcw), bf16)],
        [
            vmem((ROWS16, inner), bf16),
            vmem((ROWS16, bcw), bf16),
            pltpu.SemaphoreType.DMA((len(sources) + 4,)),
        ],
    )
    pay = call(
        functools.partial(first_state_kernel, count, scale),
        "first_state",
        [where_am_i, made[0], xa, ga, *made[1:], tails],
        [shape((state + MORE, width), bf16)],
        state_scratch
        + [vmem((rows + HALO, LANES)), vmem((HALO, inner + bcw)), vmem((MORE, width))],
    )[0]
    hop_on(0, pay)
    sources = [x, bc, g, dec, conv_x, conv_bc, skip]
    x, bc, g, dec, conv_x, conv_bc, skip = call(
        load_kernel,
        "load",
        [in_hbm(a) for a in sources] + [(pay, "any")],
        [shape(a.shape, a.dtype) for a in sources],
        [pltpu.SemaphoreType.DMA((len(sources),))],
    )
    halo = lax.ppermute(tails, "seq", [(i, i + 1) for i in range(1, count - 1)])

    states = [None, None]

    def middle_state(c, after):
        start = c * width
        states[c] = call(
            functools.partial(middle_state_kernel, count, start, start // head_dim, scale),
            "middle_state",
            [where_am_i, dec, x, g, halo, conv_x, cum, mapped, (after, "any")],
            [shape((state, width)), shape((state, width)), shape((8, width))],
            state_scratch,
        )
        return states[c][0]

    def message(c, after):
        return call(
            functools.partial(message_kernel, len(received[c])),
            "message",
            [where_am_i, *states[c], received[c][-1], (after, "any")],
            [shape((state, width), bf16)],
        )[0]

    parts = []
    carried = []

    def inside(number, after):
        first = number == 0
        start = sum(split[:number]) * LANES
        span = split[number] * LANES
        ins = [x, g, halo, conv_x, dec, cum, mapped, skip, (after, "any")]
        if not first:
            ins += carried
        made = call(
            functools.partial(intra_kernel, first, start, split[number], head_dim, scale),
            "inside_block",
            ins,
            [
                shape((rows, span)),
                shape((rows, span)),
                shape((rows, span), bf16),
                shape((rows, span), bf16),
                shape((rows, span), bf16),
                shape((rows, span), bf16),
                shape((rows, rows)),
                shape((8, LANES)),
            ],
            [padded(split[number]), vmem((rows, rows)), vmem((heads, rows))],
        )
        parts.append(made[:6])
        carried[:] = made[6:8]
        return made[0]

    def chunk_parts(c):
        mine = spans[c * pairs : (c + 1) * pairs]
        used = sorted({part for part, _ in mine})
        return [(used.index(part), at) for part, at in mine], [parts[p] for p in used]

    cum, mapped, u, v, tot, gt16, lg16 = call(
        functools.partial(middle_first_kernel, count, scale),
        "middle_first",
        [where_am_i, dec, x, g, conv_x, bc, conv_bc, (tails, "any")],
        [
            shape((heads, rows)),
            shape((rows, bcw), bf16),
            shape((state, width)),
            shape((state, width)),
            shape((8, width)),
            shape((ROWS16, width)),
            shape((ROWS16, width), bf16),
        ],
        state_scratch + [padded(2)],
    )
    after = call(
        functools.partial(end_state_kernel, count, width, width // head_dim, scale),
        "end_state",
        [where_am_i, dec, x, g, conv_x, bc, cum, mapped, (u, "any")],
        [shape((state + MORE, width), bf16)],
        state_scratch + [vmem((MORE, width))],
    )[0]
    hop_on(1, after)
    halo, mapped, u, v, came, after = call(
        functools.partial(fix_kernel, count),
        "fix_first_rows",
        [where_am_i, halo, received[0][0], x, conv_x, bc, conv_bc, mapped]
        + [u, v, tot, gt16, lg16, (after, "any")],
        [
            shape((HALO, inner + bcw), bf16),
            shape((rows, bcw), bf16),
            shape((state, width)),
            shape((state, width)),
            shape((state, width), bf16),
            shape((state, width), bf16),
        ],
        [
            vmem((HALO, inner + bcw)),
            vmem((MORE, width)),
            padded(pairs, ROWS16),
            padded(2, ROWS16),
        ],
    )
    states[0] = (u, v, tot)
    received[0][0] = came
    hop_on(0, after)
    after = middle_state(1, after)
    after = inside(0, after)
    for hop in range(1, count - 1):
        for c in chunks:
            if hop > 1:
                after = message(c, after)
                hop_on(c, after)
            elif c:
                came, after = call(
                    functools.partial(fix_message_kernel, count),
                    "message",
                    [where_am_i, *states[1], received[1][0], bc, conv_bc, (after, "any")],
                    [shape((state, width), bf16), shape((state, width), bf16)],
                    [vmem((MORE, width)), vmem((ROWS16 + HALO, LANES))],
                )
                received[1][0] = came
                hop_on(1, after)
            if hop == count - 2:
                after = inside(1 + c, after)
    dsim, gsum = carried
    ins = [where_am_i, mapped, (after, "any")]
    for made in parts:
        ins += made[1:3]
    edge = call(
        functools.partial(edge_kernel, count, spans, len(parts)),
        "edge",
        ins + received[0][: count - 2] + received[1][: count - 2],
        [shape((8, width), bf16)],
        [vmem((8, width))],
    )[0]

    edges = lax.ppermute(edge, "seq", [(i + 1, i) for i in range(count - 1)])

    def finish_bc(c, base, after):
        where, used = chunk_parts(c)
        ins = [where_am_i, mapped, base, (after, "any")]
        for made in used:
            ins += made[4:6]
        ins += received[c]
        outs = [shape((rows, bcw))]
        scratch = []
        if c:
            ins += [bc, halo, conv_bc, gsum]
            outs += [shape((8, bcw + LANES))]
            scratch = [padded(2)]
        kernel = functools.partial(finish_bc_kernel, count, c == 0, where, len(used), scale)
        return call(kernel, "finish_bc", ins, outs, scratch)

    def finish(c, after):
        start = c * width
        where, used = chunk_parts(c)
        pieces = (4, 4, 2) if pairs == 10 else (pairs - 1, 1)
        ins = [where_am_i, x, conv_x, mapped, (after, "any")]
        for made in used:
            ins += made[:4]
        ins += received[c]
        made = call(
            functools.partial(finish_kernel, count, start, where, len(used), pieces),
            "finish",
            ins,
            [(shape((rows, inner), bf16), "hbm"), (shape((rows, inner), bf16), "hbm")]
            + [shape((8, width)), shape((ROWS16, width))],
            [
                vmem((state, width), bf16),
                vmem((state, width), bf16),
                padded(pairs),
                vmem((rows, width), bf16),
                vmem((rows, width), bf16),
                pltpu.SemaphoreType.DMA((len(pieces), 2)),
            ],
        )
        return made[:2], made[2], made[3]

    outs, taps_a, end_a = finish(0, edge)
    dbc = finish_bc(0, dsim, taps_a)[0]
    own, small = finish_bc(1, dbc, dbc)

    swap = [(0, 1), (1, 0)]
    turns = [[(i, (i + k) % head_count) for i in range(head_count)] for k in range(1, head_count)]
    small, to_heads = call(
        pack_kernel,
        "pack",
        [own, small, lax.ppermute(small, "dp", swap), (edges, "any")],
        [shape(small.shape), shape((rows + ROWS16, bcw), bf16)],
    )
    others = [lax.ppermute(to_heads, "head", turn) for turn in turns]

    where, used = chunk_parts(1)
    ins = [where_am_i, x, conv_x, mapped, (to_heads, "any")]
    for made in used:
        ins += made[1:3]
    gx_b, taps_b, end_b = call(
        functools.partial(finish_grad_kernel, count, width, where, len(used)),
        "finish_grad",
        ins + received[1],
        [shape((rows, width), bf16), shape((8, width)), shape((ROWS16, width))],
        [vmem((state, width), bf16), padded(pairs)],
    )
    sums = call(
        sums_kernel,
        "sums",
        [halo, edge, taps_a, taps_b],
        [shape((8, inner))],
        [vmem((HALO, inner))],
    )[0]
    sums_dp = lax.ppermute(sums, "dp", swap)
    send_width = inner // 2 + bcw + LANES
    full, to_seq = call(
        functools.partial(merge_kernel, head_count),
        "merge",
        [sums, sums_dp, small, own] + others,
        [shape((rows, bcw)), shape((8, send_width), bf16)],
        [vmem((8, send_width))],
    )
    ins = [where_am_i, mapped, conv_x, edges, end_a, end_b, gx_b, (to_seq, "any")]
    for made in used:
        ins += [made[0], made[3]]
    ins += received[1]
    y, gx = call(
        functools.partial(write_kernel, count, width, where, len(used)),
        "write",
        ins + [(outs[0], "hbm"), (outs[1], "hbm")],
        [(shape((rows, inner), bf16), "hbm"), (shape((rows, inner), bf16), "hbm")],
        [
            vmem((state, width), bf16),
            vmem((rows, width), bf16),
            vmem((ROWS16, inner), bf16),
            pltpu.SemaphoreType.DMA((3,)),
        ],
        kept=((len(ins), 0), (len(ins) + 1, 1)),
    )
    from_seq = [
        lax.ppermute(to_seq, "seq", [(i, (i + k) % count) for i in range(count)])
        for k in range(1, count)
    ]
    token_count = rows * count * dp_count
    norm_tokens = float(token_count) ** (-0.5)
    norm_skip = float(token_count * head_dim) ** (-0.5)
    conv = call(
        conv_bc_kernel,
        "conv_bc",
        [full, conv_bc, (to_seq, "any")],
        [shape((rows, bcw))],
        [padded(2)],
    )[0]
    gbc, tx, tbc, skip = call(
        functools.partial(last_kernel, count, norm_tokens, norm_skip),
        "last",
        [where_am_i, to_seq, conv, conv_bc] + from_seq,
        [
            shape((rows, bcw), bf16),
            shape((taps, inner)),
            shape((taps, bcw)),
            shape((1, heads)),
        ],
    )
    return y[None], gx[None], gbc[None], tx, tbc, skip.reshape(heads)


def solution(mesh):
    return jax.shard_map(
        local,
        mesh=mesh,
        in_specs=(
            P(("groups", "dp"), "seq", "head"),
            P(("groups", "dp"), "seq", None),
            P(("groups", "dp"), "head", "seq"),
            P(None, "head"),
            P(),
            P("head"),
            P(("groups", "dp"), "seq", "head"),
        ),
        out_specs=(
            P(("groups", "dp"), "seq", "head"),
            P(("groups", "dp"), "seq", "head"),
            P(("groups", "dp"), "seq", None),
            P("groups", "head"),
            P("groups", None),
            P(("groups", "head")),
        ),
        check_vma=False,
    )
```
